32 devices in a mesh: dp: 8 (over z, x), tensor: 4 (over y, core).
Axes of the slice: x: 2, y: 2, z: 4, core: 2. Of those that a mesh axis runs over, the one named last changes fastest.
Arguments:
- features: bfloat16 [8, 1500, 768], P('dp', 'tensor'), may hold values from -6 to 6
- cotangent: bfloat16 [8, 1500, 768], P('dp', 'tensor'), may hold values from -6 to 6
- w_query: bfloat16 [768, 768], P(None, 'tensor'), may hold values from -0.21875 to 0.21875
- bias_query: bfloat16 [768], P('tensor'), may hold values from -3 to 3
- w_key: bfloat16 [768, 768], P(None, 'tensor'), may hold values from -0.21875 to 0.21875
- w_value: bfloat16 [768, 768], P(None, 'tensor'), may hold values from -0.21875 to 0.21875
- bias_value: bfloat16 [768], P('tensor'), may hold values from -3 to 3
- w_out: bfloat16 [768, 768], P('tensor'), may hold values from -0.875 to 0.875
- bias_out: float32 [768], replicated, may hold values from -3 to 3
- norm1_gain: float32 [768], replicated, may hold values from 0.5 to 1.5
- norm1_bias: float32 [768], replicated, may hold values from -2 to 2
- norm2_gain: float32 [768], replicated, may hold values from 0.5 to 1.5
- norm2_bias: float32 [768], replicated, may hold values from -2 to 2
- w_fc1: bfloat16 [768, 3072], P(None, 'tensor'), may hold values from -0.21875 to 0.21875
- bias_fc1: bfloat16 [3072], P('tensor'), may hold values from -3 to 3
- w_fc2: bfloat16 [3072, 768], P('tensor'), may hold values from -0.21875 to 0.21875
- bias_fc2: float32 [768], replicated, may hold values from -3 to 3
Outputs:
- layer_out: bfloat16 [8, 1500, 768], P('dp', 'tensor')
- features_grad: bfloat16 [8, 1500, 768], P('dp', 'tensor')
- w_query_grad: float32 [768, 768], P(None, 'tensor')
- bias_query_grad: float32 [768], P('tensor')
- w_key_grad: float32 [768, 768], P(None, 'tensor')
- w_value_grad: float32 [768, 768], P(None, 'tensor')
- bias_value_grad: float32 [768], P('tensor')
- w_out_grad: float32 [768, 768], P('tensor')
- bias_out_grad: float32 [768], replicated
- norm1_gain_grad: float32 [768], replicated
- norm1_bias_grad: float32 [768], replicated
- norm2_gain_grad: float32 [768], replicated
- norm2_bias_grad: float32 [768], replicated
- w_fc1_grad: float32 [768, 3072], P(None, 'tensor')
- bias_fc1_grad: float32 [3072], P('tensor')
- w_fc2_grad: float32 [3072, 768], P('tensor')
- bias_fc2_grad: float32 [768], replicated
The draws below stay inside these ranges and needn't reach their ends.
All inputs are finite; a program needn't handle non-finite values.
Results may differ from the reference program's by a relative error of at most 0.015.
Values may be sent and summed in bfloat16 or wider, within the bound.
No kernel may reach another device: no remote copies, remote signals or barrier semaphores. Data moves between devices by JAX's collectives and lax.ppermute only.
A program may use at most 192 MiB of HBM per device.

```python
import jax
import jax.numpy as jnp
from jax import lax

D = 768
HEADS = 12
HEAD_DIM = 64
FF = 3072
FRAMES = 1500
CLIPS = 8


def block_scale(stream_key, extent, pieces, low, high):
    level, own = 1.0, jax.random.fold_in(stream_key, 6)
    for dim, blocks in pieces:
        draws = jnp.exp(jax.random.uniform(jax.random.fold_in(own, dim), (blocks,), jnp.float32, low / len(pieces), high / len(pieces)))
        level = level * jnp.repeat(draws, extent[dim] // blocks).reshape([-1 if axis == dim else 1 for axis in range(len(extent))])
    return level


def gaussian(key, extent, deviation, most, cuts=(), kind=jnp.bfloat16):
    entries = jax.random.normal(key, extent, jnp.float32) * deviation
    if len(cuts) > 0:
        entries = block_scale(key, extent, cuts, -0.22, 0.18) * entries
    return jnp.clip(entries, min=-most, max=most).astype(kind)


def setup_inputs(seed: int = 0) -> dict:
    streams_of = jax.random.split(jax.random.key(seed), 18)
    return {
        "features": gaussian(streams_of[0], (CLIPS, FRAMES, D), 1.0, 6.0, ((0, 8), (1, 4))),
        "cotangent": gaussian(streams_of[1], (CLIPS, FRAMES, D), 1.0, 6.0, ((0, 8), (1, 4))),
        "w_query": gaussian(streams_of[2], (D, D), D ** -0.5, 0.21875, ((1, 4),)),
        "bias_query": gaussian(streams_of[3], (D,), 0.5, 3.0, ((0, 4),)),
        "w_key": gaussian(streams_of[4], (D, D), D ** -0.5, 0.21875, ((1, 4),)),
        "w_value": gaussian(streams_of[5], (D, D), D ** -0.5, 0.21875, ((1, 4),)),
        "bias_value": gaussian(streams_of[6], (D,), 0.5, 3.0, ((0, 4),)),
        "w_out": gaussian(streams_of[7], (D, D), (D // 16) ** -0.5, 0.875, ((0, 4),)),
        "bias_out": gaussian(streams_of[8], (D,), 0.5, 3.0, (), jnp.float32),
        "norm1_gain": jnp.clip(1.0 + 0.1 * jax.random.normal(streams_of[9], (D,), jnp.float32), 0.5, 1.5),
        "norm1_bias": gaussian(streams_of[10], (D,), 0.3, 2.0, (), jnp.float32),
        "norm2_gain": jnp.clip(1.0 + 0.1 * jax.random.normal(streams_of[11], (D,), jnp.float32), 0.5, 1.5),
        "norm2_bias": gaussian(streams_of[12], (D,), 0.3, 2.0, (), jnp.float32),
        "w_fc1": gaussian(streams_of[13], (D, FF), D ** -0.5, 0.21875, ((1, 4),)),
        "bias_fc1": gaussian(streams_of[14], (FF,), 0.5, 3.0, ((0, 4),)),
        "w_fc2": gaussian(streams_of[15], (FF, D), (FF // 4) ** -0.5, 0.21875, ((0, 4),)),
        "bias_fc2": gaussian(streams_of[16], (D,), 0.5, 3.0, (), jnp.float32),
    }


@jax.custom_vjp
def low(v):
    return lax.optimization_barrier(v.astype(jnp.bfloat16)).astype(jnp.float32)

@jax.custom_vjp
def low_back(v):
    return v

def low_keep(v):
    return (low(v), None)

def low_pass(kept, grad):
    return (grad,)

def back_keep(v):
    return (v, None)

def back_low(kept, grad):
    return (low(grad),)
low.defvjp(low_keep, low_pass)
low_back.defvjp(back_keep, back_low)

def matmul(left, right):
    return jnp.dot(left, right, precision=lax.Precision.HIGHEST)

def normalize(values, gain, shift):
    mean = lax.optimization_barrier(jnp.mean(values, axis=-1, keepdims=True))
    centred = values - mean
    spread = lax.optimization_barrier(jnp.mean(centred * centred, axis=-1, keepdims=True))
    return centred * lax.rsqrt(spread + 1e-05) * gain + shift

def clip_layer(weights, inputs):
    w_query, bias_query, w_key, w_value, bias_value, w_out, bias_out, norm1_gain, norm1_bias, norm2_gain, norm2_bias, w_fc1, bias_fc1, w_fc2, bias_fc2 = weights
    normed1 = low(normalize(inputs, norm1_gain, norm1_bias))
    query = low(low_back(matmul(normed1, w_query) + bias_query)).reshape(FRAMES, HEADS, HEAD_DIM)
    key = low(low_back(matmul(normed1, w_key))).reshape(FRAMES, HEADS, HEAD_DIM)
    value = low(low_back(matmul(normed1, w_value) + bias_value)).reshape(FRAMES, HEADS, HEAD_DIM)
    scale = HEAD_DIM ** (-0.5)
    scores = low_back(scale * jnp.einsum('qhd,khd->hqk', query, key, precision=lax.Precision.HIGHEST))
    probs = low(jax.nn.softmax(scores, axis=-1))
    mixed = jnp.einsum('hqk,khd->qhd', probs, value, precision=lax.Precision.HIGHEST)
    mixed = low(low_back(mixed)).reshape(FRAMES, D)
    hidden1 = inputs + low_back(matmul(mixed, w_out)) + bias_out
    normed2 = low(normalize(hidden1, norm2_gain, norm2_bias))
    pre = low_back(matmul(normed2, w_fc1)) + bias_fc1
    active = low(jax.nn.gelu(pre, approximate=False))
    return hidden1 + low_back(matmul(active, w_fc2)) + bias_fc2

def forward(weights, features):
    step = jax.checkpoint(clip_layer)
    return lax.map(lambda clip: step(weights, clip), features)

def reference(features, cotangent, w_query, bias_query, w_key, w_value, bias_value, w_out, bias_out, norm1_gain, norm1_bias, norm2_gain, norm2_bias, w_fc1, bias_fc1, w_fc2, bias_fc2):
    weights = tuple((t.astype(jnp.float32) for t in (w_query, bias_query, w_key, w_value, bias_value, w_out, bias_out, norm1_gain, norm1_bias, norm2_gain, norm2_bias, w_fc1, bias_fc1, w_fc2, bias_fc2)))
    layer_out, pullback = jax.vjp(forward, weights, features.astype(jnp.float32))
    grads, features_grad = pullback(cotangent.astype(jnp.float32))
    return (layer_out.astype(jnp.bfloat16), features_grad.astype(jnp.bfloat16), grads[0], grads[1], grads[2], grads[3], grads[4], grads[5], grads[6], grads[7], grads[8], grads[9], grads[10], grads[11], grads[12], grads[13], grads[14])
```

```python
import functools

import jax
import jax.numpy as jnp
from jax import lax
from jax.experimental import pallas as pl
from jax.experimental.pallas import tpu as pltpu
from jax.sharding import PartitionSpec as P

HEAD_DIM = 64
LANES = 128
F32 = jnp.float32
LOW = jnp.bfloat16
MASK = -1e30
CORE, CHIP = 1, 2
ROOM = 56 * 1024 * 1024
NT = (((1,), (1,)), ((), ()))


def params(steps=0):
    semantics = ("arbitrary",) * steps if steps else None
    return pltpu.CompilerParams(vmem_limit_bytes=ROOM, dimension_semantics=semantics)


def cost(flops, moved, exps=0):
    return pl.CostEstimate(flops=flops, bytes_accessed=moved, transcendentals=exps)


def whole(shape):
    return pl.BlockSpec(shape, lambda *_: (0,) * len(shape))


def swap(value, partner):
    size = lax.axis_size("tensor")
    return lax.ppermute(value, "tensor", [(i, i ^ partner) for i in range(size)])


def gather(own):
    across = swap(own, CHIP)
    beside = swap(own, CORE)
    return [own, beside, across, swap(across, CORE)]


def scatter(parts):
    far = parts[2] + swap(parts[3], CORE)
    far = swap(far, CHIP)
    return parts[0], swap(parts[1], CORE), far


def thirds(value):
    high = value.astype(LOW)
    rest = value - high.astype(F32)
    mid = rest.astype(LOW)
    return high, mid, (rest - mid.astype(F32)).astype(LOW)


def place(base, lane, first, pieces):
    for offset, piece in enumerate(pieces):
        base = jnp.where(lane == first + offset, piece, base)
    return base


def norm(values):
    mean = jnp.mean(values, axis=-1, keepdims=True)
    centred = values - mean
    spread = jnp.mean(centred * centred, axis=-1, keepdims=True)
    scaler = lax.rsqrt(spread + 1e-05)
    return centred * scaler, scaler


def norm_back(grad, unit, scaler, gain):
    scaled = grad * gain
    return scaler * (
        scaled
        - jnp.mean(scaled, axis=-1, keepdims=True)
        - unit * jnp.mean(scaled * unit, axis=-1, keepdims=True)
    )


def project_kernel(share, x_ref, gain_ref, shift_ref, w_ref, bias_ref, n_ref, q_ref, k_ref, v_ref):
    unit, _ = norm(x_ref[...].astype(F32))
    normed = (unit * gain_ref[...] + shift_ref[...]).astype(LOW)
    n_ref[...] = normed
    out = jnp.dot(normed, w_ref[...], preferred_element_type=F32) + bias_ref[...]
    heads = q_ref.shape[0]
    row = lax.broadcasted_iota(jnp.int32, (out.shape[0], LANES), 0)
    lane = lax.broadcasted_iota(jnp.int32, (out.shape[0], LANES), 1)
    absent = (row >= share) & (lane == HEAD_DIM)
    scale = HEAD_DIM ** (-0.5)
    for head in range(heads):
        part = lambda which: out[:, (which * heads + head) * LANES :][:, :LANES]
        q_ref[head] = (part(0).astype(LOW).astype(F32) * scale).astype(LOW)
        k_ref[head] = jnp.where(absent, MASK, part(1)).astype(LOW)
        v_ref[head] = part(2).astype(LOW)


def attend_kernel(qa_ref, qb_ref, k_ref, v_ref, o_ref, qa_out, qb_out):
    heads, block, _ = qa_ref.shape
    lane = lax.broadcasted_iota(jnp.int32, (block, LANES), 1)
    for half, (q_ref, q_out) in enumerate(((qa_ref, qa_out), (qb_ref, qb_out))):
        for head in range(heads):
            query = q_ref[head]
            scores = lax.dot_general(query, k_ref[head], NT, preferred_element_type=F32)
            top = jnp.max(scores, axis=-1, keepdims=True)
            weights = jnp.exp(scores - top).astype(LOW)
            out = jnp.dot(weights, v_ref[head], preferred_element_type=F32)
            total = out[:, HEAD_DIM : HEAD_DIM + 1]
            at = (half * heads + head) * HEAD_DIM
            o_ref[:, at : at + HEAD_DIM] = (out / total)[:, :HEAD_DIM].astype(LOW)
            logsum = top + jnp.log(total)
            q_out[head] = place(query, lane, HEAD_DIM + 1, thirds(-logsum))


def feed_kernel(
    x_ref, m_ref, wo_ref, bo_ref, gain_ref, shift_ref, w1_ref, b1_ref, w2_ref, g_ref,
    h_ref, n_ref, a_ref, p_ref, d_ref, db_ref,
):
    step = pl.program_id(0)
    branch = jnp.dot(m_ref[...], wo_ref[...], preferred_element_type=F32)
    hidden = x_ref[...].astype(F32) + branch + bo_ref[...]

    @pl.when(step == 0)
    def _():
        h_ref[...] = hidden
        db_ref[...] = jnp.zeros_like(db_ref)

    unit, _ = norm(hidden)
    normed = (unit * gain_ref[...] + shift_ref[...]).astype(LOW)
    n_ref[...] = normed
    pre = jnp.dot(normed, w1_ref[...], preferred_element_type=F32) + b1_ref[...]
    active_grad = lax.dot_general(g_ref[...], w2_ref[...], NT, preferred_element_type=F32)
    size = jnp.abs(pre)
    bell = jnp.exp(-0.5 * pre * pre)
    t = 1.0 / (1.0 + (0.3275911 * 0.5**0.5) * size)
    poly = t * (
        0.127414796 + t * (-0.142248368 + t * (0.7107068705 + t * (-0.7265760135 + t * 0.5307027145)))
    )
    tail = poly * bell
    gate = jnp.where(pre >= 0, 1.0 - tail, tail)
    a_ref[...] = (pre * gate).astype(LOW)
    pre_grad = active_grad * (gate + pre * bell * 0.3989422804014327)
    db_ref[...] += jnp.sum(pre_grad, axis=0, keepdims=True)
    pre_low = pre_grad.astype(LOW)
    p_ref[...] = pre_low
    d_ref[...] = lax.dot_general(pre_low, w1_ref[...], NT, preferred_element_type=F32).astype(LOW)


def middle_kernel(h_ref, d0_ref, d1_ref, d2_ref, g_ref, gain_ref, out_ref, low_ref, sums_ref):
    grad = d0_ref[...].astype(F32) + d1_ref[...].astype(F32) + d2_ref[...].astype(F32)
    unit, scaler = norm(h_ref[...])
    cot = g_ref[...].astype(F32)
    hidden_grad = cot + norm_back(grad, unit, scaler, gain_ref[...])
    out_ref[...] = hidden_grad
    low_ref[...] = hidden_grad.astype(LOW)
    add = lambda value: jnp.sum(value, axis=0, keepdims=True)
    sums_ref[...] = jnp.concatenate(
        [add(grad * unit), add(grad), add(hidden_grad), add(cot)], axis=0
    )


def attend_back_kernel(
    h_ref, m_ref, q_ref, k_ref, v_ref, wo_ref, dq_ref, dk_ref, dv_ref, kt_ref, dk_sum, dv_sum
):
    step = pl.program_id(0)
    heads, block, _ = q_ref.shape

    @pl.when(step == 0)
    def _():
        dk_sum[...] = jnp.zeros_like(dk_sum)
        dv_sum[...] = jnp.zeros_like(dv_sum)
        for head in range(heads):
            kt_ref[head] = k_ref[head].astype(F32).T[:HEAD_DIM].astype(LOW)

    scale = HEAD_DIM ** (-0.5)
    lane = lax.broadcasted_iota(jnp.int32, (block, LANES), 1)
    mixed_grad = lax.dot_general(
        h_ref[...], wo_ref[...], NT, preferred_element_type=F32
    ).astype(LOW)
    for head in range(heads):
        at = head * HEAD_DIM
        out_grad = mixed_grad[:, head * LANES : (head + 1) * LANES]
        mixed = m_ref[:, at : at + HEAD_DIM].astype(F32)
        delta = jnp.sum(out_grad[:, :HEAD_DIM].astype(F32) * mixed, axis=-1, keepdims=True)
        out_grad = place(out_grad, lane, HEAD_DIM, thirds(-delta))
        query = q_ref[head]
        scores = lax.dot_general(k_ref[head], query, NT, preferred_element_type=F32)
        probs = jnp.exp(scores)
        prob_grad = lax.dot_general(v_ref[head], out_grad, NT, preferred_element_type=F32)
        score_grad = (probs * prob_grad).astype(LOW)
        dv_sum[head] += jnp.dot(probs.astype(LOW), out_grad, preferred_element_type=F32)
        dk_sum[head] += jnp.dot(score_grad, query, preferred_element_type=F32)
        turned = jnp.dot(kt_ref[head], score_grad, preferred_element_type=F32)
        dq_ref[:, at : at + HEAD_DIM] = (turned.T * scale).astype(LOW)

    @pl.when(step == pl.num_programs(0) - 1)
    def _():
        for head in range(heads):
            at = head * HEAD_DIM
            dk_ref[:, at : at + HEAD_DIM] = dk_sum[head][:, :HEAD_DIM].astype(LOW)
            dv_ref[:, at : at + HEAD_DIM] = dv_sum[head][:, :HEAD_DIM].astype(LOW)


def last_kernel(x_ref, d0_ref, d1_ref, d2_ref, h_ref, gain_ref, out_ref, sums_ref):
    share = x_ref.shape[0]
    total = d0_ref[...].astype(F32) + d1_ref[...].astype(F32) + d2_ref[...].astype(F32)
    grad = total[:share]
    unit, scaler = norm(x_ref[...].astype(F32))
    out_ref[...] = (h_ref[...][:share] + norm_back(grad, unit, scaler, gain_ref[...])).astype(LOW)
    add = lambda value: jnp.sum(value, axis=0, keepdims=True)
    sums_ref[...] = jnp.concatenate([add(grad * unit), add(grad)], axis=0)


def on_device(
    features, cotangent, w_query, bias_query, w_key, w_value, bias_value, w_out, bias_out,
    norm1_gain, norm1_bias, norm2_gain, norm2_bias, w_fc1, bias_fc1, w_fc2, bias_fc2,
):
    _, share, width = features.shape
    local = w_query.shape[1]
    heads = local // HEAD_DIM
    hidden = w_fc1.shape[1]
    group = lax.axis_size("tensor")
    rows = -(-share // LANES) * LANES
    frames = group * rows
    block = 256
    row = lambda value: value.astype(F32).reshape(1, -1)
    shape = jax.ShapeDtypeStruct
    x_own, g_own = features[0], cotangent[0]
    fill = ((0, rows - share), (0, 0))
    x_pad, g_pad = jnp.pad(x_own, fill), jnp.pad(g_own, fill)
    x_all = jnp.concatenate(gather(x_pad), axis=0)
    g_all = jnp.concatenate(gather(g_pad), axis=0)
    wo_all = jnp.concatenate(gather(w_out), axis=0)

    tiles = lambda value: jnp.pad(
        value.reshape(-1, heads, HEAD_DIM), ((0, 0), (0, 0), (0, LANES - HEAD_DIM))
    )
    w_tiles = jnp.concatenate([tiles(w_query), tiles(w_key), tiles(w_value)], axis=1)
    w_tiles = w_tiles.reshape(width, 3 * heads * LANES)
    spot = jnp.arange(LANES) - HEAD_DIM
    one_q = jnp.where(spot == 0, HEAD_DIM**0.5, 0.0)
    one_k = jnp.where((spot >= 1) & (spot <= 3), 1.0, 0.0)
    one_v = jnp.where((spot >= 0) & (spot <= 2), 1.0, 0.0)
    bias_tiles = jnp.concatenate(
        [
            tiles(bias_query.astype(F32)) + one_q,
            jnp.broadcast_to(one_k, (1, heads, LANES)),
            tiles(bias_value.astype(F32)) + one_v,
        ],
        axis=1,
    ).reshape(1, 3 * heads * LANES)

    per_rows = lambda n: pl.BlockSpec((rows, n), lambda i: (i, 0))
    head_rows = pl.BlockSpec((heads, rows, LANES), lambda i: (0, i, 0))
    head_shape = shape((heads, frames, LANES), LOW)
    normed1, query, key, value = pl.pallas_call(
        functools.partial(project_kernel, share),
        grid=(group,),
        in_specs=[
            per_rows(width), whole((1, width)), whole((1, width)),
            whole(w_tiles.shape), whole(bias_tiles.shape),
        ],
        out_specs=[per_rows(width), head_rows, head_rows, head_rows],
        out_shape=[shape((frames, width), LOW), head_shape, head_shape, head_shape],
        compiler_params=params(1),
        cost_estimate=cost(2 * frames * width * 9 * LANES, 12_000_000),
        name="project",
    )(x_all, row(norm1_gain), row(norm1_bias), w_tiles, bias_tiles)

    half = frames // 2
    steps = half // block
    head_block = lambda shift: pl.BlockSpec((heads, block, LANES), lambda i: (0, i + shift, 0))
    head_whole = whole((heads, frames, LANES))
    half_shape = shape((heads, half, LANES), LOW)
    mixed, query_a, query_b = pl.pallas_call(
        attend_kernel,
        grid=(steps,),
        in_specs=[head_block(0), head_block(steps), head_whole, head_whole],
        out_specs=[pl.BlockSpec((block, 2 * local), lambda i: (i, 0)), head_block(0), head_block(0)],
        out_shape=[shape((half, 2 * local), LOW), half_shape, half_shape],
        compiler_params=params(1),
        cost_estimate=cost(4 * heads * frames * frames * 256, 5_000_000, heads * frames * frames),
        name="attend",
    )(query, query, key, value)
    query_back = jnp.concatenate([query_a, query_b], axis=1)

    def slot(packed, j):
        return packed[(j % 2) * rows :, (j // 2) * local :][:rows, :local]

    mixed_parts = gather(mixed)
    mixed_own = jnp.concatenate([slot(mixed, j) for j in range(group)], axis=0)
    mixed_all = jnp.concatenate(
        [
            jnp.concatenate([slot(mixed_parts[k], j ^ k) for k in range(group)], axis=1)
            for j in range(group)
        ],
        axis=0,
    )

    low_rows = shape((frames, hidden), LOW)
    hidden1, normed2, active, pre_low, normed2_part, fc1_bias_grad = pl.pallas_call(
        feed_kernel,
        grid=(group,),
        in_specs=[
            per_rows(width), per_rows(width), whole((width, width)), whole((1, width)),
            whole((1, width)), whole((1, width)), whole((width, hidden)), whole((1, hidden)),
            whole((hidden, width)), per_rows(width),
        ],
        out_specs=[
            whole((rows, width)), per_rows(width), per_rows(hidden), per_rows(hidden),
            per_rows(width), whole((1, hidden)),
        ],
        out_shape=[
            shape((rows, width), F32), shape((frames, width), LOW), low_rows, low_rows,
            shape((frames, width), LOW), shape((1, hidden), F32),
        ],
        compiler_params=params(1),
        cost_estimate=cost(8 * frames * width * hidden, 20_000_000, frames * hidden),
        name="feed",
    )(
        x_all, mixed_all, wo_all, row(bias_out), row(norm2_gain), row(norm2_bias),
        w_fc1, row(bias_fc1), w_fc2, g_all,
    )
    split = lambda value: [value[j * rows : (j + 1) * rows] for j in range(group)]
    first, second, third = scatter(split(normed2_part))
    hidden1_grad, hidden1_low, sums2 = pl.pallas_call(
        middle_kernel,
        out_shape=[
            shape((rows, width), F32), shape((rows, width), LOW), shape((4, width), F32),
        ],
        compiler_params=params(),
        cost_estimate=cost(20 * rows * width, 8 * rows * width),
        name="middle",
    )(hidden1, first, second, third, g_pad, row(norm2_gain))
    hidden1_rows = jnp.concatenate(gather(hidden1_low), axis=0)

    mlp_part = jnp.dot(active, w_fc2, preferred_element_type=F32).astype(LOW)
    mlp = [part.astype(F32) for part in scatter(split(mlp_part))]
    layer_out = (hidden1 + (mlp[0] + mlp[1] + mlp[2]) + bias_fc2)[None, :share].astype(LOW)
    tn = lambda left, right: lax.dot_general(
        left, right, (((0,), (0,)), ((), ())), preferred_element_type=F32
    )
    over_clips = lambda value: lax.psum(value.astype(LOW), "dp").astype(F32)
    fc2_grad = over_clips(tn(active, g_all))
    fc1_grad = over_clips(tn(normed2, pre_low))
    w_out_grad = over_clips(tn(mixed_own, hidden1_rows))

    wo_tiles = jnp.pad(
        w_out.reshape(heads, HEAD_DIM, width), ((0, 0), (0, LANES - HEAD_DIM), (0, 0))
    ).reshape(heads * LANES, width)
    by_block = lambda n: pl.BlockSpec((block, n), lambda i: (i, 0))
    query_grad, key_grad, value_grad = pl.pallas_call(
        attend_back_kernel,
        grid=(frames // block,),
        in_specs=[
            by_block(width), by_block(local), head_block(0), head_whole, head_whole,
            whole(wo_tiles.shape),
        ],
        out_specs=[by_block(local), whole((frames, local)), whole((frames, local))],
        out_shape=[shape((frames, local), LOW)] * 3,
        scratch_shapes=[
            pltpu.VMEM((heads, HEAD_DIM, frames), LOW),
            pltpu.VMEM((heads, frames, LANES), F32),
            pltpu.VMEM((heads, frames, LANES), F32),
        ],
        compiler_params=params(1),
        cost_estimate=cost(10 * heads * frames * frames * 256, 9_000_000, heads * frames * frames),
        name="attend_back",
    )(hidden1_rows, mixed_own, query_back, key, value, wo_tiles)

    stack_grad = jnp.concatenate([query_grad, key_grad, value_grad], axis=1)
    w_stack = jnp.concatenate([w_query, w_key, w_value], axis=1)
    normed1_part = lax.dot_general(stack_grad, w_stack, NT, preferred_element_type=F32).astype(LOW)
    first, second, third = scatter(split(normed1_part))
    features_grad, sums1 = pl.pallas_call(
        last_kernel,
        out_shape=[shape((share, width), LOW), shape((2, width), F32)],
        compiler_params=params(),
        cost_estimate=cost(20 * rows * width, 8 * rows * width),
        name="last",
    )(x_own, first, second, third, hidden1_grad, row(norm1_gain))

    weights_grad = over_clips(tn(normed1, stack_grad))
    total = jnp.sum(stack_grad.astype(F32), axis=0)
    mine = jnp.concatenate([total[:local], total[2 * local :], fc1_bias_grad[0]])
    spread = jnp.arange(group)[:, None] == lax.axis_index("tensor")
    mine = jnp.where(spread, mine[None], 0.0)
    sums = lax.psum(
        jnp.concatenate([mine.reshape(-1), sums1.reshape(-1), sums2.reshape(-1)]), ("dp", "tensor")
    )
    count = 2 * local + hidden
    mine = lax.dynamic_slice(sums, (lax.axis_index("tensor") * count,), (count,))
    shared = sums[group * count :].reshape(6, width)
    return (
        layer_out,
        features_grad[None],
        weights_grad[:, :local],
        mine[:local],
        weights_grad[:, local : 2 * local],
        weights_grad[:, 2 * local :],
        mine[local : 2 * local],
        w_out_grad,
        shared[4],
        shared[0],
        shared[1],
        shared[2],
        shared[3],
        fc1_grad,
        mine[2 * local :],
        fc2_grad,
        shared[5],
    )


def solution(mesh):
    rows = P("dp", "tensor", None)
    columns, lines, vector, same = P(None, "tensor"), P("tensor", None), P("tensor"), P()
    in_specs = (
        rows, rows, columns, vector, columns, columns, vector, lines, same,
        same, same, same, same, columns, vector, lines, same,
    )
    out_specs = (
        rows, rows, columns, vector, columns, columns, vector, lines, same,
        same, same, same, same, columns, vector, lines, same,
    )
    return jax.shard_map(
        on_device, mesh=mesh, in_specs=in_specs, out_specs=out_specs, check_vma=False
    )
```

```python
import functools

import jax
import jax.numpy as jnp
from jax import lax
from jax.experimental import pallas as pl
from jax.experimental.pallas import tpu as pltpu
from jax.sharding import PartitionSpec as P

HEAD_DIM = 64
LANES = 128
F32 = jnp.float32
LOW = jnp.bfloat16
MASK = -1e30
CORE, CHIP = 1, 2
ROOM = 56 * 1024 * 1024
NT = (((1,), (1,)), ((), ()))


def params(steps=0):
    semantics = ("arbitrary",) * steps if steps else None
    return pltpu.CompilerParams(vmem_limit_bytes=ROOM, dimension_semantics=semantics)


def cost(flops, moved, exps=0):
    return pl.CostEstimate(flops=flops, bytes_accessed=moved, transcendentals=exps)


def whole(shape):
    return pl.BlockSpec(shape, lambda *_: (0,) * len(shape))


def swap(value, partner):
    size = lax.axis_size("tensor")
    return lax.ppermute(value, "tensor", [(i, i ^ partner) for i in range(size)])


def gather(own):
    across = swap(own, CHIP)
    beside = swap(own, CORE)
    return [own, beside, across, swap(across, CORE)]


def scatter(parts):
    far = parts[2] + swap(parts[3], CORE)
    far = swap(far, CHIP)
    return parts[0], swap(parts[1], CORE), far


def thirds(value):
    high = value.astype(LOW)
    rest = value - high.astype(F32)
    mid = rest.astype(LOW)
    return high, mid, (rest - mid.astype(F32)).astype(LOW)


def place(base, lane, first, pieces):
    for offset, piece in enumerate(pieces):
        base = jnp.where(lane == first + offset, piece, base)
    return base


def norm(values):
    mean = jnp.mean(values, axis=-1, keepdims=True)
    centred = values - mean
    spread = jnp.mean(centred * centred, axis=-1, keepdims=True)
    scaler = lax.rsqrt(spread + 1e-05)
    return centred * scaler, scaler


def norm_back(grad, unit, scaler, gain):
    scaled = grad * gain
    return scaler * (
        scaled
        - jnp.mean(scaled, axis=-1, keepdims=True)
        - unit * jnp.mean(scaled * unit, axis=-1, keepdims=True)
    )


def pick(step, refs, rows):
    size = refs[0].shape[0]
    count = rows.shape[0] // size
    for turn in range(len(refs) // count):

        @pl.when(step == turn)
        def _():
            for at in range(count):
                rows[at * size : (at + 1) * size] = refs[turn * count + at][...]


def project_kernel(half, share, group, aliased, *refs):
    x_refs = refs[:group]
    vec_ref, bias_ref, wq_ref, wk_ref, wv_ref = refs[group : group + 5]
    n_ref, q_ref, k_ref, v_ref, rows, w_tiles, b_tiles = refs[group + 5 + aliased :]
    step = pl.program_id(0)
    heads = q_ref.shape[0]
    size = x_refs[0].shape[0]

    @pl.when(step == 0)
    def _():
        w_tiles[...] = jnp.zeros_like(w_tiles)
        b_tiles[...] = jnp.zeros_like(b_tiles)
        spot = lax.broadcasted_iota(jnp.int32, (1, LANES), 1) - HEAD_DIM
        ones = (
            jnp.where(spot == 0, HEAD_DIM**0.5, 0.0),
            jnp.where((spot >= 1) & (spot <= 3), 1.0, 0.0),
            jnp.where((spot >= 0) & (spot <= 2), 1.0, 0.0),
        )
        for which, w_ref in enumerate((wq_ref, wk_ref, wv_ref)):
            for head in range(heads):
                at = (which * heads + head) * LANES
                own = slice(head * HEAD_DIM, (head + 1) * HEAD_DIM)
                w_tiles[:, at : at + HEAD_DIM] = w_ref[:, own]
                b_tiles[:, at : at + LANES] = ones[which]
                b_tiles[:, at : at + HEAD_DIM] = bias_ref[which : which + 1, own]

    pick(step, x_refs, rows)
    unit, _ = norm(rows[...].astype(F32))
    normed = (unit * vec_ref[0:1] + vec_ref[1:2]).astype(LOW)
    n_ref[...] = normed
    out = jnp.dot(normed, w_tiles[...], preferred_element_type=F32) + b_tiles[...]
    row = lax.broadcasted_iota(jnp.int32, (out.shape[0], LANES), 0)
    lane = lax.broadcasted_iota(jnp.int32, (out.shape[0], LANES), 1)
    absent = (lax.rem(row, size) + half * size >= share) & (lane == HEAD_DIM)
    scale = HEAD_DIM ** (-0.5)
    for head in range(heads):
        part = lambda which: out[:, (which * heads + head) * LANES :][:, :LANES]
        q_ref[head] = (part(0).astype(LOW).astype(F32) * scale).astype(LOW)
        k_ref[head] = jnp.where(absent, MASK, part(1)).astype(LOW)
        v_ref[head] = part(2).astype(LOW)


def attend_kernel(aliased, slots, q_ref, k_ref, v_ref, *refs):
    o_ref, m_ref, full_ref, q_out = refs[aliased:]
    heads, block, _ = q_ref.shape
    quarter = block // slots // 2
    lane = lax.broadcasted_iota(jnp.int32, (block, LANES), 1)
    for head in range(heads):
        query = q_ref[head]
        scores = lax.dot_general(query, k_ref[head], NT, preferred_element_type=F32)
        top = jnp.max(scores, axis=-1, keepdims=True)
        weights = jnp.exp(scores - top).astype(LOW)
        out = jnp.dot(weights, v_ref[head], preferred_element_type=F32)
        total = out[:, HEAD_DIM : HEAD_DIM + 1]
        out = out / total
        full_ref[:, head * LANES : (head + 1) * LANES] = out
        low = out[:, :HEAD_DIM].astype(LOW)
        m_ref[:, head * HEAD_DIM : (head + 1) * HEAD_DIM] = low
        for part in range(2 * slots):
            at = ((part % 2) * heads + head) * HEAD_DIM
            o_ref[part // 2 * quarter : (part // 2 + 1) * quarter, at : at + HEAD_DIM] = low[
                part * quarter : (part + 1) * quarter
            ]
        logsum = top + jnp.log(total)
        q_out[head] = place(query, lane, HEAD_DIM + 1, thirds(-logsum))


def feed_kernel(group, aliased, *refs):
    x_refs, m_refs, wo_refs = refs[:group], refs[group : 3 * group], refs[3 * group : 4 * group]
    g_refs = refs[4 * group : 5 * group]
    vec_ref, w1_ref, w2_ref = refs[5 * group : 5 * group + 3]
    outs = refs[5 * group + 3 + aliased :]
    h_ref, n_ref, a_ref, p_ref, c_ref, db_ref = outs[:6]
    d_refs = outs[6 : 6 + group]
    rows, mixed = outs[6 + group :]
    step = pl.program_id(0)
    size = x_refs[0].shape[0]
    slots = rows.shape[0] // size
    quarter = size // 2
    pick(step, x_refs, rows)
    pick(step, g_refs, c_ref)
    local = wo_refs[0].shape[0]
    for source in range(group):
        for at in range(slots):
            packed = m_refs[source * slots + at][...]
            for part in range(2):
                first = at * size + part * quarter
                mixed[first : first + quarter, source * local : (source + 1) * local] = packed[
                    :, part * local : (part + 1) * local
                ]
    hidden = rows[...].astype(F32) + vec_ref[2:3]
    for source in range(group):
        hidden += jnp.dot(
            mixed[:, source * local : (source + 1) * local],
            wo_refs[source][...],
            preferred_element_type=F32,
        )

    @pl.when(step == 0)
    def _():
        h_ref[...] = hidden[:size]
        db_ref[...] = jnp.zeros_like(db_ref)

    unit, _ = norm(hidden)
    normed = (unit * vec_ref[3:4] + vec_ref[4:5]).astype(LOW)
    n_ref[...] = normed
    pre = jnp.dot(normed, w1_ref[...], preferred_element_type=F32) + vec_ref[5:6]
    active_grad = lax.dot_general(c_ref[...], w2_ref[...], NT, preferred_element_type=F32)
    size_of = jnp.abs(pre)
    bell = jnp.exp(-0.5 * pre * pre)
    t = 1.0 / (1.0 + (0.3275911 * 0.5**0.5) * size_of)
    poly = t * (
        0.127414796 + t * (-0.142248368 + t * (0.7107068705 + t * (-0.7265760135 + t * 0.5307027145)))
    )
    tail = poly * bell
    gate = jnp.where(pre >= 0, 1.0 - tail, tail)
    a_ref[...] = (pre * gate).astype(LOW)
    pre_grad = active_grad * (gate + pre * bell * 0.3989422804014327)
    db_ref[...] += jnp.sum(pre_grad, axis=0, keepdims=True)
    pre_low = pre_grad.astype(LOW)
    p_ref[...] = pre_low
    back = lax.dot_general(pre_low, w1_ref[...], NT, preferred_element_type=F32).astype(LOW)
    for turn in range(group // slots):

        @pl.when(step == turn)
        def _():
            for at in range(slots):
                d_refs[turn * slots + at][...] = back[at * size : (at + 1) * size]


def middle_kernel(h_ref, d0_ref, d1_ref, d2_ref, g_ref, vec_ref, out_ref, low_ref, sums_ref):
    grad = d0_ref[...].astype(F32) + d1_ref[...].astype(F32) + d2_ref[...].astype(F32)
    unit, scaler = norm(h_ref[...])
    cot = g_ref[...].astype(F32)
    hidden_grad = cot + norm_back(grad, unit, scaler, vec_ref[3:4])
    out_ref[...] = hidden_grad
    low_ref[...] = hidden_grad.astype(LOW)
    add = lambda value: jnp.sum(value, axis=0, keepdims=True)
    sums_ref[...] = jnp.concatenate(
        [add(grad * unit), add(grad), add(hidden_grad), add(cot)], axis=0
    )


def attend_back_kernel(parts, *refs):
    h_refs = refs[:parts]
    m_ref, full_ref, q_ref, k_ref, v_ref, wo_ref = refs[parts : parts + 6]
    dq_ref, dk_ref, dv_ref, dw_ref, sum_ref = refs[parts + 6 : parts + 11]
    rows, wo_tiles, kt_ref, dk_sum, dv_sum = refs[parts + 11 :]
    step = pl.program_id(0)
    heads, block, _ = q_ref.shape

    @pl.when(step == 0)
    def _():
        size = h_refs[0].shape[0]
        for part in range(parts):
            rows[part * size : (part + 1) * size] = h_refs[part][...]
        wo_tiles[...] = jnp.zeros_like(wo_tiles)
        dw_ref[...] = jnp.zeros_like(dw_ref)
        sum_ref[...] = jnp.zeros_like(sum_ref)
        dk_sum[...] = jnp.zeros_like(dk_sum)
        dv_sum[...] = jnp.zeros_like(dv_sum)
        for head in range(heads):
            wo_tiles[head * LANES : head * LANES + HEAD_DIM] = wo_ref[
                head * HEAD_DIM : (head + 1) * HEAD_DIM
            ]
            kt_ref[head] = k_ref[head].astype(F32).T[:HEAD_DIM].astype(LOW)

    scale = HEAD_DIM ** (-0.5)
    lane = lax.broadcasted_iota(jnp.int32, (block, LANES), 1)
    hidden_grad = rows[pl.ds(pl.multiple_of(step * block, block), block)]
    mixed_grad = lax.dot_general(
        hidden_grad, wo_tiles[...], NT, preferred_element_type=F32
    ).astype(LOW)
    dw_ref[...] += lax.dot_general(
        m_ref[...], hidden_grad, (((0,), (0,)), ((), ())), preferred_element_type=F32
    )
    for head in range(heads):
        at = head * HEAD_DIM
        tile = slice(head * LANES, (head + 1) * LANES)
        out_grad = mixed_grad[:, tile]
        delta = jnp.sum(out_grad.astype(F32) * full_ref[:, tile], axis=-1, keepdims=True)
        out_grad = place(out_grad, lane, HEAD_DIM, thirds(-delta))
        query = q_ref[head]
        scores = lax.dot_general(k_ref[head], query, NT, preferred_element_type=F32)
        probs = jnp.exp(scores)
        prob_grad = lax.dot_general(v_ref[head], out_grad, NT, preferred_element_type=F32)
        score_grad = (probs * prob_grad).astype(LOW)
        dv_sum[head] += jnp.dot(probs.astype(LOW), out_grad, preferred_element_type=F32)
        dk_sum[head] += jnp.dot(score_grad, query, preferred_element_type=F32)
        turned = jnp.dot(kt_ref[head], score_grad, preferred_element_type=F32)
        query_grad = (turned.T * scale).astype(LOW)
        dq_ref[:, at : at + HEAD_DIM] = query_grad
        sum_ref[0:1, at : at + HEAD_DIM] += jnp.sum(
            query_grad.astype(F32), axis=0, keepdims=True
        )

    @pl.when(step == pl.num_programs(0) - 1)
    def _():
        for head in range(heads):
            at = head * HEAD_DIM
            for index, (ref, total) in enumerate(((dk_ref, dk_sum), (dv_ref, dv_sum))):
                low = total[head][:, :HEAD_DIM].astype(LOW)
                ref[:, at : at + HEAD_DIM] = low
                sum_ref[index + 1 : index + 2, at : at + HEAD_DIM] = jnp.sum(
                    low.astype(F32), axis=0, keepdims=True
                )


def spread_kernel(dq_ref, dk_ref, dv_ref, wq_ref, wk_ref, wv_ref, *outs):
    total = sum(
        lax.dot_general(grad[...], weight[...], NT, preferred_element_type=F32)
        for grad, weight in ((dq_ref, wq_ref), (dk_ref, wk_ref), (dv_ref, wv_ref))
    ).astype(LOW)
    size = outs[0].shape[0]
    slots = total.shape[0] // size
    step = pl.program_id(0)
    for turn in range(len(outs) // slots):

        @pl.when(step == turn)
        def _():
            for at in range(slots):
                outs[turn * slots + at][...] = total[at * size : (at + 1) * size]


def last_kernel(aliased, x_ref, d0_ref, d1_ref, d2_ref, h_ref, vec_ref, *refs):
    out_ref = refs[aliased]
    grad = d0_ref[...].astype(F32) + d1_ref[...].astype(F32) + d2_ref[...].astype(F32)
    unit, scaler = norm(x_ref[...].astype(F32))
    out_ref[...] = (h_ref[...] + norm_back(grad, unit, scaler, vec_ref[0:1])).astype(LOW)


def output_kernel(ha_ref, hb_ref, d0_ref, d1_ref, d2_ref, vec_ref, out_ref):
    size = ha_ref.shape[0]
    share = out_ref.shape[0]
    for part, h_ref in enumerate((ha_ref, hb_ref)):
        mlp = d0_ref[part].astype(F32) + d1_ref[part].astype(F32) + d2_ref[part].astype(F32)
        value = (h_ref[...] + mlp + vec_ref[6:7]).astype(LOW)
        count = min(size, share - part * size)
        out_ref[part * size : part * size + count] = value[:count]


def sum_over(value, axis):
    size = lax.axis_size(axis)
    if size & (size - 1):
        return lax.psum(value, axis)
    step = 1
    while step < size:
        value = value + lax.ppermute(value, axis, [(i, i ^ step) for i in range(size)])
        step *= 2
    return value


def after(value, *others):
    return lax.optimization_barrier((value, *others))[0]


def on_device(
    features, cotangent, w_query, bias_query, w_key, w_value, bias_value, w_out, bias_out,
    norm1_gain, norm1_bias, norm2_gain, norm2_bias, w_fc1, bias_fc1, w_fc2, bias_fc2,
):
    _, share, width = features.shape
    local = w_query.shape[1]
    heads = local // HEAD_DIM
    hidden = w_fc1.shape[1]
    group = lax.axis_size("tensor")
    rows = -(-share // LANES) * LANES
    size = rows // 2
    frames = group * rows
    part_rows = group * size
    slots = 2
    block = slots * size
    steps = group // slots
    shape = jax.ShapeDtypeStruct
    halves = range(2)

    def cut(value):
        low = value[0, :size]
        high = jnp.pad(value[0, size:], ((0, rows - share), (0, 0)))
        return [low, high]

    x_own, g_own = cut(features), cut(cotangent)
    x_all = [gather(x_own[0])]
    x_all.append(gather(after(x_own[1], x_all[0][2])))
    g_all = [gather(after(g_own[half], x_all[1][2])) for half in halves]
    wo_all = gather(after(w_out, x_all[1][2]))
    row = lambda value: value.astype(F32)
    vectors = jnp.stack(
        [norm1_gain, norm1_bias, bias_out, norm2_gain, norm2_bias, row(bias_fc1), bias_fc2]
    )
    biases = jnp.stack([row(bias_query), jnp.zeros((local,), F32), row(bias_value)])

    slot_spec = whole((size, width))
    any_spec = pl.BlockSpec(memory_space=pl.ANY)
    at_half = lambda half, n: pl.BlockSpec((block, n), lambda i: (half * steps + i, 0))
    head_half = lambda half: pl.BlockSpec((heads, block, LANES), lambda i: (0, half * steps + i, 0))
    head_shape = shape((heads, frames, LANES), LOW)

    made = []
    for half in halves:
        made = pl.pallas_call(
            functools.partial(project_kernel, half, share, group, len(made)),
            grid=(steps,),
            in_specs=[slot_spec] * group
            + [whole(vectors.shape), whole(biases.shape)]
            + [whole((width, local))] * 3
            + [any_spec] * len(made),
            out_specs=[at_half(half, width)] + [head_half(half)] * 3,
            out_shape=[shape((frames, width), LOW)] + [head_shape] * 3,
            scratch_shapes=[
                pltpu.VMEM((block, width), LOW),
                pltpu.VMEM((width, 3 * heads * LANES), LOW),
                pltpu.VMEM((1, 3 * heads * LANES), F32),
            ],
            input_output_aliases={group + 5 + i: i for i in range(len(made))},
            compiler_params=params(1),
            cost_estimate=cost(2 * part_rows * width * 9 * LANES, 6_000_000),
            name="project",
        )(*x_all[half], vectors, biases, w_query, w_key, w_value, *made)
    normed1, query, key, value = made

    head_whole = whole((heads, frames, LANES))
    made, packed = [], []
    for half in halves:
        made = pl.pallas_call(
            functools.partial(attend_kernel, len(made), slots),
            grid=(steps,),
            in_specs=[head_half(half), head_whole, head_whole] + [any_spec] * len(made),
            out_specs=[
                pl.BlockSpec((block // 2, 2 * local), lambda i: (i, 0)),
                at_half(half, local), at_half(half, heads * LANES), head_half(half),
            ],
            out_shape=[
                shape((part_rows // 2, 2 * local), LOW), shape((frames, local), LOW),
                shape((frames, heads * LANES), F32), head_shape,
            ],
            input_output_aliases={3 + i: 1 + i for i in range(len(made))},
            compiler_params=params(1),
            cost_estimate=cost(
                2 * heads * frames * frames * 256, 5_000_000, heads * frames * frames // 2
            ),
            name="attend",
        )(query, key, value, *made)
        packed.append(gather(made[0]))
        made = made[1:]
    mixed, mixed_full, query_back = made

    low_rows = shape((frames, hidden), LOW)
    made, hidden1, fc1_bias_grad, normed2_parts = [], [], 0.0, []
    for half in halves:
        packed_specs, packed_args = [], []
        for source in range(group):
            for at in range(slots):
                packed_args.append(packed[half][source])
                packed_specs.append(
                    pl.BlockSpec(
                        (size // 2, 2 * local),
                        lambda i, source=source, at=at: ((i * slots + at) ^ source, 0),
                    )
                )
        made = pl.pallas_call(
            functools.partial(feed_kernel, group, len(made)),
            grid=(steps,),
            in_specs=[slot_spec] * group
            + packed_specs
            + [whole((local, width))] * group
            + [slot_spec] * group
            + [whole(vectors.shape), whole((width, hidden)), whole((hidden, width))]
            + [any_spec] * len(made),
            out_specs=[slot_spec]
            + [at_half(half, n) for n in (width, hidden, hidden, width)]
            + [whole((1, hidden))]
            + [slot_spec] * group,
            out_shape=[
                shape((size, width), F32), shape((frames, width), LOW), low_rows, low_rows,
                shape((frames, width), LOW), shape((1, hidden), F32),
            ]
            + [shape((size, width), LOW)] * group,
            scratch_shapes=[pltpu.VMEM((block, width), LOW)] * 2,
            input_output_aliases={5 * group + 3 + i: 1 + i for i in range(len(made))},
            compiler_params=params(1),
            cost_estimate=cost(4 * frames * width * hidden, 12_000_000, frames * hidden // 2),
            name="feed",
        )(
            *x_all[half], *packed_args, *wo_all, *g_all[half], vectors, w_fc1, w_fc2, *made
        )
        hidden1.append(made[0])
        fc1_bias_grad = fc1_bias_grad + made[5]
        normed2_parts.append(scatter(made[6:]))
        made = made[1:5]
    normed2, active, pre_low, cot_rows = made

    hidden1_grad, sums2, hidden1_rows = [], 0.0, []
    for half in halves:
        grad, low, sums = pl.pallas_call(
            middle_kernel,
            out_shape=[
                shape((size, width), F32), shape((size, width), LOW), shape((4, width), F32),
            ],
            compiler_params=params(),
            cost_estimate=cost(20 * size * width, 16 * size * width),
            name="middle",
        )(hidden1[half], *normed2_parts[half], g_own[half], vectors)
        hidden1_grad.append(grad)
        sums2 = sums2 + sums
        hidden1_rows += gather(low)

    tn = lambda left, right: lax.dot_general(
        left, right, (((0,), (0,)), ((), ())), preferred_element_type=F32
    )
    fc2_grad = lax.psum(tn(active, cot_rows).astype(LOW), "dp")
    fc1_grad = lax.psum_scatter(
        tn(normed2, pre_low).astype(LOW), "dp", scatter_dimension=0, tiled=True
    )
    fc1_grad = lax.all_gather(fc1_grad, "dp", axis=0, tiled=True)
    mlp_part = jnp.dot(active, w_fc2, preferred_element_type=F32).astype(LOW)
    mlp_part = mlp_part.reshape(2, group, size, width)
    mlp = scatter([after(mlp_part[:, j], hidden1_rows[-2]) for j in range(group)])
    layer_out = pl.pallas_call(
        output_kernel,
        out_shape=shape((share, width), LOW),
        compiler_params=params(),
        cost_estimate=cost(8 * rows * width, 12 * rows * width),
        name="output",
    )(*hidden1, *mlp, vectors)

    back = 256
    by_block = lambda n: pl.BlockSpec((back, n), lambda i: (i, 0))
    line = shape((frames, local), LOW)
    query_grad, key_grad, value_grad, w_out_grad, sums0 = pl.pallas_call(
        functools.partial(attend_back_kernel, 2 * group),
        grid=(frames // back,),
        in_specs=[slot_spec] * (2 * group)
        + [
            by_block(local), by_block(heads * LANES),
            pl.BlockSpec((heads, back, LANES), lambda i: (0, i, 0)),
            head_whole, head_whole, whole((local, width)),
        ],
        out_specs=[by_block(local)]
        + [whole((frames, local))] * 2
        + [whole((local, width)), whole((3, local))],
        out_shape=[line, line, line, shape((local, width), F32), shape((3, local), F32)],
        scratch_shapes=[
            pltpu.VMEM((frames, width), LOW),
            pltpu.VMEM((heads * LANES, width), LOW),
            pltpu.VMEM((heads, HEAD_DIM, frames), LOW),
            pltpu.VMEM((heads, frames, LANES), F32),
            pltpu.VMEM((heads, frames, LANES), F32),
        ],
        compiler_params=params(1),
        cost_estimate=cost(10 * heads * frames * frames * 256, 9_000_000, heads * frames * frames),
        name="attend_back",
    )(*hidden1_rows, mixed, mixed_full, query_back, key, value, w_out)

    features_grad = []
    normed1_parts = pl.pallas_call(
        spread_kernel,
        grid=(2 * steps,),
        in_specs=[pl.BlockSpec((block, local), lambda i: (i, 0))] * 3 + [whole((width, local))] * 3,
        out_specs=[slot_spec] * (2 * group),
        out_shape=[shape((size, width), LOW)] * (2 * group),
        compiler_params=params(1),
        cost_estimate=cost(2 * frames * width * 3 * local, 6_000_000),
        name="spread",
    )(query_grad, key_grad, value_grad, w_query, w_key, w_value)
    for half in halves:
        features_grad = [
            pl.pallas_call(
                functools.partial(last_kernel, len(features_grad)),
                grid=(1,),
                in_specs=[slot_spec] * 5
                + [whole(vectors.shape)]
                + [any_spec] * len(features_grad),
                out_specs=pl.BlockSpec((size, width), lambda i, half=half: (half, 0)),
                out_shape=shape((share, width), LOW),
                input_output_aliases={6: 0} if features_grad else {},
                compiler_params=params(1),
                cost_estimate=cost(20 * size * width, 14 * size * width),
                name="last",
            )(
                x_own[half],
                *scatter(normed1_parts[half * group : (half + 1) * group]),
                hidden1_grad[half],
                vectors,
                *features_grad,
            )
        ]

    stack_grad = jnp.concatenate([query_grad, key_grad, value_grad], axis=1)
    weights_own = tn(normed1, stack_grad)
    weights_low = after(weights_own.astype(LOW), fc2_grad)
    weights_grad, w_out_grad = lax.psum((weights_low, w_out_grad.astype(LOW)), "dp")
    w_stack = jnp.concatenate([w_query, w_key, w_value], axis=1).astype(F32)
    shift1_grad = jnp.sum(w_stack * sums0.reshape(1, -1), axis=1)
    gain1_grad = (jnp.sum(w_stack * weights_own, axis=1) - norm1_bias * shift1_grad) / norm1_gain
    small = jnp.concatenate(
        [
            sums0[0], sums0[2], fc1_bias_grad[0], gain1_grad, shift1_grad, sums2.reshape(-1),
        ]
    )
    small = sum_over(small, "dp")
    count = 2 * local + hidden
    mine = small[:count]
    shared = sum_over(small[count:], "tensor").reshape(6, width)
    weights_grad = weights_grad.astype(F32)
    return (
        layer_out[None],
        features_grad[0][None],
        weights_grad[:, :local],
        mine[:local],
        weights_grad[:, local : 2 * local],
        weights_grad[:, 2 * local :],
        mine[local : 2 * local],
        w_out_grad.astype(F32),
        shared[4],
        shared[0],
        shared[1],
        shared[2],
        shared[3],
        fc1_grad.astype(F32),
        mine[2 * local :],
        fc2_grad.astype(F32),
        shared[5],
    )


def solution(mesh):
    rows = P("dp", "tensor", None)
    columns, lines, vector, same = P(None, "tensor"), P("tensor", None), P("tensor"), P()
    in_specs = (
        rows, rows, columns, vector, columns, columns, vector, lines, same,
        same, same, same, same, columns, vector, lines, same,
    )
    out_specs = (
        rows, rows, columns, vector, columns, columns, vector, lines, same,
        same, same, same, same, columns, vector, lines, same,
    )
    return jax.shard_map(
        on_device, mesh=mesh, in_specs=in_specs, out_specs=out_specs, check_vma=False
    )
```

```python
import functools

import jax
import jax.numpy as jnp
from jax import lax
from jax.experimental import pallas as pl
from jax.experimental.pallas import tpu as pltpu
from jax.sharding import PartitionSpec as P

HEAD_DIM = 64
LANES = 128
F32 = jnp.float32
LOW = jnp.bfloat16
MASK = -1e30
CORE, CHIP = 1, 2
ROOM = 56 * 1024 * 1024
NT = (((1,), (1,)), ((), ()))


def params(steps=0):
    semantics = ("arbitrary",) * steps if steps else None
    return pltpu.CompilerParams(vmem_limit_bytes=ROOM, dimension_semantics=semantics)


def cost(flops, moved, exps=0):
    return pl.CostEstimate(flops=flops, bytes_accessed=moved, transcendentals=exps)


def whole(shape):
    return pl.BlockSpec(shape, lambda *_: (0,) * len(shape))


def swap(value, partner):
    size = lax.axis_size("tensor")
    return lax.ppermute(value, "tensor", [(i, i ^ partner) for i in range(size)])


def gather(own):
    across = swap(own, CHIP)
    beside = swap(own, CORE)
    return [own, beside, across, swap(across, CORE)]


def scatter_direct(parts):
    return [parts[0]] + [swap(parts[j], j) for j in range(1, len(parts))]


def scatter(parts):
    far = parts[2] + swap(parts[3], CORE)
    far = swap(far, CHIP)
    return [parts[0], swap(parts[1], CORE), far]


def thirds(value):
    high = value.astype(LOW)
    rest = value - high.astype(F32)
    mid = rest.astype(LOW)
    return high, mid, (rest - mid.astype(F32)).astype(LOW)


def place(base, lane, first, pieces):
    for offset, piece in enumerate(pieces):
        base = jnp.where(lane == first + offset, piece, base)
    return base


def norm(values):
    mean = jnp.mean(values, axis=-1, keepdims=True)
    centred = values - mean
    spread = jnp.mean(centred * centred, axis=-1, keepdims=True)
    scaler = lax.rsqrt(spread + 1e-05)
    return centred * scaler, scaler


def norm_back(grad, unit, scaler, gain):
    scaled = grad * gain
    return scaler * (
        scaled
        - jnp.mean(scaled, axis=-1, keepdims=True)
        - unit * jnp.mean(scaled * unit, axis=-1, keepdims=True)
    )


def present(value, count):
    if count == value.shape[0]:
        return value
    row = lax.broadcasted_iota(jnp.int32, value.shape, 0)
    return jnp.where(row < count, value.astype(F32), 0.0).astype(value.dtype)


def pick(step, refs, rows, count):
    size = refs[0].shape[0]
    slots = rows.shape[0] // size
    for turn in range(len(refs) // slots):

        @pl.when(step == turn)
        def _():
            for at in range(slots):
                block = present(refs[turn * slots + at][...], count)
                rows[at * size : (at + 1) * size] = block


def project_kernel(share, slots, aliased, *refs):
    x_refs = refs[:slots]
    vec_ref, bias_ref, wq_ref, wk_ref, wv_ref = refs[slots : slots + 5]
    n_ref, q_ref, k_ref, v_ref, rows, w_tiles, b_tiles = refs[slots + 5 + aliased :]
    half = pl.program_id(0)
    heads = q_ref.shape[0]
    size = x_refs[0].shape[0]

    @pl.when(half == 0)
    def _():
        w_tiles[...] = jnp.zeros_like(w_tiles)
        b_tiles[...] = jnp.zeros_like(b_tiles)
        spot = lax.broadcasted_iota(jnp.int32, (1, LANES), 1) - HEAD_DIM
        ones = (
            jnp.where(spot == 0, HEAD_DIM**0.5, 0.0),
            jnp.where((spot >= 1) & (spot <= 3), 1.0, 0.0),
            jnp.where((spot >= 0) & (spot <= 2), 1.0, 0.0),
        )
        for which, w_ref in enumerate((wq_ref, wk_ref, wv_ref)):
            for head in range(heads):
                at = (which * heads + head) * LANES
                own = slice(head * HEAD_DIM, (head + 1) * HEAD_DIM)
                w_tiles[at : at + HEAD_DIM] = w_ref[own]
                b_tiles[:, at : at + LANES] = ones[which]
                b_tiles[:, at : at + HEAD_DIM] = bias_ref[which : which + 1, own]

    row = lax.broadcasted_iota(jnp.int32, (size, rows.shape[1]), 0) + half * size
    for at in range(slots):
        block = jnp.where(row < share, x_refs[at][...].astype(F32), 0.0)
        rows[at * size : (at + 1) * size] = block
    unit, _ = norm(rows[...])
    normed = (unit * vec_ref[0:1] + vec_ref[1:2]).astype(LOW)
    n_ref[...] = normed
    out = lax.dot_general(normed, w_tiles[...], NT, preferred_element_type=F32) + b_tiles[...]
    row = lax.broadcasted_iota(jnp.int32, (out.shape[0], LANES), 0)
    lane = lax.broadcasted_iota(jnp.int32, (out.shape[0], LANES), 1)
    absent = (lax.rem(row, size) + half * size >= share) & (lane == HEAD_DIM)
    scale = HEAD_DIM ** (-0.5)
    for head in range(heads):
        part = lambda which: out[:, (which * heads + head) * LANES :][:, :LANES]
        q_ref[head] = (part(0).astype(LOW).astype(F32) * scale).astype(LOW)
        k_ref[head] = jnp.where(absent, MASK, part(1)).astype(LOW)
        v_ref[head] = part(2).astype(LOW)


def attend_kernel(aliased, slots, q_ref, k_ref, v_ref, *refs):
    o_ref, m_ref, full_ref, q_out = refs[aliased:]
    heads, block, _ = q_ref.shape
    quarter = block // slots // 2
    lane = lax.broadcasted_iota(jnp.int32, (block, LANES), 1)
    for head in range(heads):
        query = q_ref[head]
        scores = lax.dot_general(query, k_ref[head], NT, preferred_element_type=F32)
        top = jnp.max(scores, axis=-1, keepdims=True)
        weights = jnp.exp(scores - top).astype(LOW)
        out = jnp.dot(weights, v_ref[head], preferred_element_type=F32)
        total = out[:, HEAD_DIM : HEAD_DIM + 1]
        out = out / total
        full_ref[:, head * LANES : (head + 1) * LANES] = out
        low = out[:, :HEAD_DIM].astype(LOW)
        m_ref[:, head * HEAD_DIM : (head + 1) * HEAD_DIM] = low
        for part in range(2 * slots):
            at = ((part % 2) * heads + head) * HEAD_DIM
            o_ref[part // 2 * quarter : (part // 2 + 1) * quarter, at : at + HEAD_DIM] = low[
                part * quarter : (part + 1) * quarter
            ]
        logsum = top + jnp.log(total)
        q_out[head] = place(query, lane, HEAD_DIM + 1, thirds(-logsum))


def feed_kernel(half, share, group, aliased, *refs):
    x_refs, m_refs, wo_refs = refs[:group], refs[group : 3 * group], refs[3 * group : 4 * group]
    g_refs = refs[4 * group : 5 * group]
    vec_ref, w1_ref, w2_ref = refs[5 * group : 5 * group + 3]
    outs = refs[5 * group + 3 + aliased :]
    h_ref, n_ref, a_ref, p_ref, c_ref, db_ref = outs[:6]
    d_refs = outs[6 : 6 + group]
    rows, mixed = outs[6 + group :]
    step = pl.program_id(0)
    size = x_refs[0].shape[0]
    slots = rows.shape[0] // size
    quarter = size // 2
    count = min(size, share - half * size)
    pick(step, x_refs, rows, count)
    pick(step, g_refs, c_ref, count)
    local = wo_refs[0].shape[0]
    for source in range(group):
        for at in range(slots):
            packed = m_refs[source * slots + at][...]
            for part in range(2):
                first = at * size + part * quarter
                mixed[first : first + quarter, source * local : (source + 1) * local] = packed[
                    :, part * local : (part + 1) * local
                ]
    hidden = rows[...].astype(F32) + vec_ref[2:3]
    for source in range(group):
        hidden += jnp.dot(
            mixed[:, source * local : (source + 1) * local],
            wo_refs[source][...],
            preferred_element_type=F32,
        )

    @pl.when(step == 0)
    def _():
        h_ref[...] = hidden[:size]
        db_ref[...] = jnp.zeros_like(db_ref)

    unit, _ = norm(hidden)
    normed = (unit * vec_ref[3:4] + vec_ref[4:5]).astype(LOW)
    n_ref[...] = normed
    pre = jnp.dot(normed, w1_ref[...], preferred_element_type=F32) + vec_ref[5:6]
    active_grad = lax.dot_general(c_ref[...], w2_ref[...], NT, preferred_element_type=F32)
    size_of = jnp.abs(pre)
    bell = jnp.exp(-0.5 * pre * pre)
    t = 1.0 / (1.0 + (0.3275911 * 0.5**0.5) * size_of)
    poly = t * (
        0.127414796 + t * (-0.142248368 + t * (0.7107068705 + t * (-0.7265760135 + t * 0.5307027145)))
    )
    tail = poly * bell
    gate = jnp.where(pre >= 0, 1.0 - tail, tail)
    a_ref[...] = (pre * gate).astype(LOW)
    pre_grad = active_grad * (gate + pre * bell * 0.3989422804014327)
    db_ref[...] += jnp.sum(pre_grad, axis=0, keepdims=True)
    pre_low = pre_grad.astype(LOW)
    p_ref[...] = pre_low
    back = lax.dot_general(pre_low, w1_ref[...], NT, preferred_element_type=F32).astype(LOW)
    for turn in range(group // slots):

        @pl.when(step == turn)
        def _():
            for at in range(slots):
                d_refs[turn * slots + at][...] = back[at * size : (at + 1) * size]


def middle_kernel(count, h_ref, g_ref, vec_ref, *refs):
    out_ref, low_ref, sums_ref = refs[-3:]
    grad = sum(ref[...].astype(F32) for ref in refs[:-3])
    unit, scaler = norm(h_ref[...])
    cot = present(g_ref[...], count).astype(F32)
    hidden_grad = cot + norm_back(grad, unit, scaler, vec_ref[3:4])
    out_ref[...] = hidden_grad
    low_ref[...] = hidden_grad.astype(LOW)
    add = lambda value: jnp.sum(value, axis=0, keepdims=True)
    sums_ref[...] = jnp.concatenate(
        [add(grad * unit), add(grad), add(hidden_grad), add(cot)], axis=0
    )


def attend_back_kernel(parts, first, *refs):
    h_refs = refs[:parts]
    m_ref, full_ref, q_ref, k_ref, v_ref, wo_ref = refs[parts : parts + 6]
    if first:
        dq_ref, dk_sum, dv_sum, dw_ref, sum_ref, kt_ref = refs[parts + 6 : parts + 12]
        rows, wo_tiles = refs[parts + 12 :]
    else:
        dk_old, dv_old, dw_old, sum_old, kt_ref, _ = refs[parts + 6 : parts + 12]
        dq_ref, dk_ref, dv_ref, dw_ref, sum_ref = refs[parts + 12 : parts + 17]
        rows, wo_tiles, dk_sum, dv_sum = refs[parts + 17 :]
    step = pl.program_id(0)
    heads, block, _ = q_ref.shape

    @pl.when(step == 0)
    def _():
        size = h_refs[0].shape[0]
        for part in range(parts):
            rows[part * size : (part + 1) * size] = h_refs[part][...]
        wo_tiles[...] = jnp.zeros_like(wo_tiles)
        for head in range(heads):
            wo_tiles[head * LANES : head * LANES + HEAD_DIM] = wo_ref[
                head * HEAD_DIM : (head + 1) * HEAD_DIM
            ]
        if first:
            for total in (dk_sum, dv_sum, dw_ref, sum_ref):
                total[...] = jnp.zeros_like(total)
            for head in range(heads):
                kt_ref[head] = k_ref[head].astype(F32).T[:HEAD_DIM].astype(LOW)
        else:
            olds = (dk_old, dv_old, dw_old, sum_old)
            for total, old in zip((dk_sum, dv_sum, dw_ref, sum_ref), olds):
                total[...] = old[...]

    scale = HEAD_DIM ** (-0.5)
    lane = lax.broadcasted_iota(jnp.int32, (block, LANES), 1)
    hidden_grad = rows[pl.ds(pl.multiple_of(step * block, block), block)]
    mixed_grad = lax.dot_general(
        hidden_grad, wo_tiles[...], NT, preferred_element_type=F32
    ).astype(LOW)
    dw_ref[...] += lax.dot_general(
        m_ref[...], hidden_grad, (((0,), (0,)), ((), ())), preferred_element_type=F32
    )
    for head in range(heads):
        at = head * HEAD_DIM
        tile = slice(head * LANES, (head + 1) * LANES)
        out_grad = mixed_grad[:, tile]
        delta = jnp.sum(out_grad.astype(F32) * full_ref[:, tile], axis=-1, keepdims=True)
        out_grad = place(out_grad, lane, HEAD_DIM, thirds(-delta))
        query = q_ref[head]
        scores = lax.dot_general(k_ref[head], query, NT, preferred_element_type=F32)
        probs = jnp.exp(scores)
        prob_grad = lax.dot_general(v_ref[head], out_grad, NT, preferred_element_type=F32)
        score_grad = (probs * prob_grad).astype(LOW)
        dv_sum[head] += jnp.dot(probs.astype(LOW), out_grad, preferred_element_type=F32)
        dk_sum[head] += jnp.dot(score_grad, query, preferred_element_type=F32)
        turned = jnp.dot(kt_ref[head], score_grad, preferred_element_type=F32)
        query_grad = (turned.T * scale).astype(LOW)
        dq_ref[:, at : at + HEAD_DIM] = query_grad
        sum_ref[0:1, at : at + HEAD_DIM] += jnp.sum(
            query_grad.astype(F32), axis=0, keepdims=True
        )

    if not first:

        @pl.when(step == pl.num_programs(0) - 1)
        def _():
            for head in range(heads):
                at = head * HEAD_DIM
                for index, (ref, total) in enumerate(((dk_ref, dk_sum), (dv_ref, dv_sum))):
                    low = total[head][:, :HEAD_DIM].astype(LOW)
                    ref[:, at : at + HEAD_DIM] = low
                    sum_ref[index + 1 : index + 2, at : at + HEAD_DIM] = jnp.sum(
                        low.astype(F32), axis=0, keepdims=True
                    )


def weigh_kernel(orders, me_ref, n_ref, dq_ref, dk_ref, dv_ref, wq_ref, wk_ref, wv_ref, dw_ref,
                 sum_ref, vec_ref, *refs):
    outs, (stacks,) = refs[:-1], refs[-1:]
    gain_ref = outs[-1]
    local = dq_ref.shape[1]
    gain = jnp.zeros(vec_ref[0:1].shape, F32)
    shift = gain
    for which, (grad, w_ref) in enumerate(((dq_ref, wq_ref), (dk_ref, wk_ref), (dv_ref, wv_ref))):
        own = lax.dot_general(
            grad[...], n_ref[...], (((0,), (0,)), ((), ())), preferred_element_type=F32
        )
        stacks[which * local : (which + 1) * local] = own
        weights = w_ref[...].astype(F32)
        gain += jnp.sum(weights * own, axis=0, keepdims=True)
        shift += jnp.dot(
            sum_ref[which : which + 1],
            weights,
            precision=lax.Precision.HIGHEST,
            preferred_element_type=F32,
        )
    stacks[3 * local : 4 * local] = dw_ref[...]
    gain_ref[0:1] = (gain - vec_ref[1:2] * shift) / vec_ref[0:1]
    gain_ref[1:2] = shift
    if orders is None:
        outs[0][...] = stacks[: 2 * local].astype(LOW)
        outs[1][...] = stacks[2 * local :].astype(LOW)
        return
    for stack, order in enumerate(orders):
        size = 2 * local // len(order)
        for spot, slot in enumerate(order):
            which, at = divmod(spot, len(order) // 2)
            start = stack * 2 * local + jnp.bitwise_xor(me_ref[0], slot) * size
            piece = stacks[pl.ds(pl.multiple_of(start, size), size)]
            outs[2 * stack + which][at * size : (at + 1) * size] = piece.astype(LOW)


def settle_kernel(orders, me_ref, *refs):
    outs = refs[-4:]
    local = outs[0].shape[0]
    for stack, order in enumerate(orders):
        size = 2 * local // len(order)
        per = local // size
        for spot, slot in enumerate(order):
            which, at = divmod(spot, len(order) // 2)
            value = refs[2 * stack + which][at * size : (at + 1) * size].astype(F32)
            place_at = jnp.bitwise_xor(me_ref[0], slot)
            start = pl.multiple_of(lax.rem(place_at, per) * size, size)
            for side in range(2):

                @pl.when(lax.div(place_at, per) == side)
                def _():
                    outs[2 * stack + side][pl.ds(start, size)] = value


def spread_kernel(dq_ref, dk_ref, dv_ref, wq_ref, wk_ref, wv_ref, *outs):
    total = sum(
        jnp.dot(grad[...], weight[...], preferred_element_type=F32)
        for grad, weight in ((dq_ref, wq_ref), (dk_ref, wk_ref), (dv_ref, wv_ref))
    ).astype(LOW)
    size = outs[0].shape[0]
    slots = total.shape[0] // size
    step = pl.program_id(0)
    for turn in range(len(outs) // slots):

        @pl.when(step == turn)
        def _():
            for at in range(slots):
                outs[turn * slots + at][...] = total[at * size : (at + 1) * size]


def last_kernel(aliased, x_ref, d0_ref, d1_ref, d2_ref, h_ref, vec_ref, *refs):
    out_ref = refs[aliased]
    grad = d0_ref[...].astype(F32) + d1_ref[...].astype(F32) + d2_ref[...].astype(F32)
    unit, scaler = norm(x_ref[...].astype(F32))
    out_ref[...] = (h_ref[...] + norm_back(grad, unit, scaler, vec_ref[0:1])).astype(LOW)


def output_kernel(ha_ref, hb_ref, vec_ref, *refs):
    out_ref = refs[-1]
    size = ha_ref.shape[0]
    share = out_ref.shape[0]
    for part, h_ref in enumerate((ha_ref, hb_ref)):
        mlp = sum(ref[part].astype(F32) for ref in refs[:-1])
        value = (h_ref[...] + mlp + vec_ref[6:7]).astype(LOW)
        count = min(size, share - part * size)
        out_ref[part * size : part * size + count] = value[:count]


def pair(value, axis, step):
    size = lax.axis_size(axis)
    return lax.ppermute(value, axis, [(i, i ^ step) for i in range(size)])


def sum_over(value, axis):
    size = lax.axis_size(axis)
    if size & (size - 1):
        return lax.psum(value, axis)
    step = 1
    while step < size:
        value = value + pair(value, axis, step)
        step *= 2
    return value


def exchange_order(bits):
    order = [0]
    for bit in reversed(bits):
        order = order + [slot | bit for slot in order]
    return order


def exchange(keep, send, axis, bits):
    for turn, bit in enumerate(bits):
        keep = keep + pair(send, axis, bit)
        if turn < len(bits) - 1:
            keep, send = jnp.split(keep, 2)
    for bit in reversed(bits[1:]):
        keep = jnp.concatenate([keep, pair(keep, axis, bit)])
    return keep, pair(keep, axis, bits[0])


def after(value, *others):
    return lax.optimization_barrier((value, *others))[0]


def on_device(
    features, cotangent, w_query, bias_query, w_key, w_value, bias_value, w_out, bias_out,
    norm1_gain, norm1_bias, norm2_gain, norm2_bias, w_fc1, bias_fc1, w_fc2, bias_fc2,
):
    _, share, width = features.shape
    local = w_query.shape[1]
    heads = local // HEAD_DIM
    hidden = w_fc1.shape[1]
    group = lax.axis_size("tensor")
    clips = lax.axis_size("dp")
    rows = -(-share // LANES) * LANES
    size = rows // 2
    frames = group * rows
    part_rows = group * size
    slots = 2
    block = slots * size
    steps = group // slots
    shape = jax.ShapeDtypeStruct
    halves = range(2)
    count = lambda half: min(size, share - half * size)

    x_own, g_own = features[0], cotangent[0]
    x_all = gather(x_own)
    g_all = gather(after(g_own, x_all[2]))
    wo_all = gather(after(w_out, g_all[2]))
    row = lambda value: value.astype(F32)
    vectors = jnp.stack(
        [norm1_gain, norm1_bias, bias_out, norm2_gain, norm2_bias, row(bias_fc1), bias_fc2]
    )
    biases = jnp.stack([row(bias_query), jnp.zeros((local,), F32), row(bias_value)])
    turned = [w_query.T, w_key.T, w_value.T]

    slot_spec = whole((size, width))
    turned_spec = whole((local, width))
    any_spec = pl.BlockSpec(memory_space=pl.ANY)
    at_half = lambda half, n: pl.BlockSpec((block, n), lambda i: (half * steps + i, 0))
    own_half = lambda half: pl.BlockSpec((size, width), lambda *_: (half, 0))
    head_half = lambda half: pl.BlockSpec((heads, block, LANES), lambda i: (0, half * steps + i, 0))
    head_shape = shape((heads, frames, LANES), LOW)

    made = []
    for turn in range(steps):
        made = pl.pallas_call(
            functools.partial(project_kernel, share, slots, len(made)),
            grid=(2,),
            in_specs=[pl.BlockSpec((size, width), lambda i: (i, 0))] * slots
            + [whole(vectors.shape), whole(biases.shape)]
            + [turned_spec] * 3
            + [any_spec] * len(made),
            out_specs=[pl.BlockSpec((block, width), lambda i, turn=turn: (i * steps + turn, 0))]
            + [
                pl.BlockSpec((heads, block, LANES), lambda i, turn=turn: (0, i * steps + turn, 0))
            ]
            * 3,
            out_shape=[shape((frames, width), LOW)] + [head_shape] * 3,
            scratch_shapes=[
                pltpu.VMEM((block, width), F32),
                pltpu.VMEM((3 * heads * LANES, width), LOW),
                pltpu.VMEM((1, 3 * heads * LANES), F32),
            ],
            input_output_aliases={slots + 5 + i: i for i in range(len(made))},
            compiler_params=params(1),
            cost_estimate=cost(2 * part_rows * width * 9 * LANES, 6_000_000),
            name="project",
        )(*x_all[turn * slots : (turn + 1) * slots], vectors, biases, *turned, *made)
    normed1, query, key, value = made

    head_whole = whole((heads, frames, LANES))
    made, packed = [], []
    for half in halves:
        made = pl.pallas_call(
            functools.partial(attend_kernel, len(made), slots),
            grid=(steps,),
            in_specs=[head_half(half), head_whole, head_whole] + [any_spec] * len(made),
            out_specs=[
                pl.BlockSpec((block // 2, 2 * local), lambda i: (i, 0)),
                at_half(half, local), at_half(half, heads * LANES), head_half(half),
            ],
            out_shape=[
                shape((part_rows // 2, 2 * local), LOW), shape((frames, local), LOW),
                shape((frames, heads * LANES), F32), head_shape,
            ],
            input_output_aliases={3 + i: 1 + i for i in range(len(made))},
            compiler_params=params(1),
            cost_estimate=cost(
                2 * heads * frames * frames * 256, 5_000_000, heads * frames * frames // 2
            ),
            name="attend",
        )(query, key, value, *made)
        packed.append(made[0])
        made = made[1:]
    mixed, mixed_full, query_back = made

    low_rows = shape((frames, hidden), LOW)
    made, hidden1, fc1_bias_grad, normed2_parts = [], [], 0.0, []
    for half in halves:
        across = swap(packed[half], CHIP)
        beside = swap(packed[half], CORE)
        if made:
            across = after(across, made[0])
        sources = [packed[half], beside, across, swap(across, CORE)]
        packed_specs, packed_args = [], []
        for source in range(group):
            for at in range(slots):
                packed_args.append(sources[source])
                packed_specs.append(
                    pl.BlockSpec(
                        (size // 2, 2 * local),
                        lambda i, source=source, at=at: ((i * slots + at) ^ source, 0),
                    )
                )
        made = pl.pallas_call(
            functools.partial(feed_kernel, half, share, group, len(made)),
            grid=(steps,),
            in_specs=[own_half(half)] * group
            + packed_specs
            + [whole((local, width))] * group
            + [own_half(half)] * group
            + [whole(vectors.shape), whole((width, hidden)), whole((hidden, width))]
            + [any_spec] * len(made),
            out_specs=[slot_spec]
            + [at_half(half, n) for n in (width, hidden, hidden, width)]
            + [whole((1, hidden))]
            + [slot_spec] * group,
            out_shape=[
                shape((size, width), F32), shape((frames, width), LOW), low_rows, low_rows,
                shape((frames, width), LOW), shape((1, hidden), F32),
            ]
            + [shape((size, width), LOW)] * group,
            scratch_shapes=[pltpu.VMEM((block, width), LOW)] * 2,
            input_output_aliases={5 * group + 3 + i: 1 + i for i in range(len(made))},
            compiler_params=params(1),
            cost_estimate=cost(4 * frames * width * hidden, 12_000_000, frames * hidden // 2),
            name="feed",
        )(*x_all, *packed_args, *wo_all, *g_all, vectors, w_fc1, w_fc2, *made)
        hidden1.append(made[0])
        fc1_bias_grad = fc1_bias_grad + made[5]
        normed2_parts.append(made[6:])
        made = made[1:5]
    normed2, active, pre_low, cot_rows = made

    hidden1_grad, sums2, hidden1_rows = [], 0.0, []
    for half in halves:
        terms = (scatter if half else scatter_direct)(normed2_parts[half])
        grad, low, sums = pl.pallas_call(
            functools.partial(middle_kernel, count(half)),
            grid=(1,),
            in_specs=[slot_spec, own_half(half), whole(vectors.shape)] + [slot_spec] * len(terms),
            out_specs=[slot_spec, slot_spec, whole((4, width))],
            out_shape=[
                shape((size, width), F32), shape((size, width), LOW), shape((4, width), F32),
            ],
            compiler_params=params(1),
            cost_estimate=cost(20 * size * width, 16 * size * width),
            name="middle",
        )(hidden1[half], g_own, vectors, *terms)
        hidden1_grad.append(grad)
        sums2 = sums2 + sums
        hidden1_rows.append(gather(low))

    tn = lambda left, right: lax.dot_general(
        left, right, (((0,), (0,)), ((), ())), preferred_element_type=F32
    )
    fc2_grad, fc1_grad = lax.psum(
        (tn(active, cot_rows).astype(LOW), tn(normed2, pre_low).astype(LOW)), "dp"
    )
    mlp_part = jnp.dot(active, w_fc2, preferred_element_type=F32).astype(LOW)
    mlp_part = mlp_part.reshape(2, group, size, width)
    mlp = scatter_direct([after(mlp_part[:, j], hidden1_rows[1][2]) for j in range(group)])
    layer_out = pl.pallas_call(
        output_kernel,
        out_shape=shape((share, width), LOW),
        compiler_params=params(),
        cost_estimate=cost(8 * rows * width, 12 * rows * width),
        name="output",
    )(*hidden1, vectors, *mlp)

    back = 256
    turns = part_rows // back
    line = shape((frames, local), LOW)
    state = []
    sums_shape = [shape((heads, frames, LANES), F32)] * 2
    side_shape = [shape((local, width), F32), shape((3, local), F32)]
    side_spec = [turned_spec, whole((3, local))]
    kt_spec = whole((heads, HEAD_DIM, frames))
    for half in halves:
        first = half == 0
        by_block = lambda n, half=half: pl.BlockSpec((back, n), lambda i: (half * turns + i, 0))
        made = pl.pallas_call(
            functools.partial(attend_back_kernel, group, first),
            grid=(turns,),
            in_specs=[slot_spec] * group
            + [
                by_block(local), by_block(heads * LANES),
                pl.BlockSpec((heads, back, LANES), lambda i, half=half: (0, half * turns + i, 0)),
                head_whole, head_whole, turned_spec,
            ]
            + ([] if first else [head_whole] * 2 + side_spec + [kt_spec, any_spec]),
            out_specs=[by_block(local)]
            + ([head_whole] * 2 if first else [whole((frames, local))] * 2)
            + side_spec
            + ([kt_spec] if first else []),
            out_shape=[line]
            + (sums_shape if first else [line, line])
            + side_shape
            + ([shape((heads, HEAD_DIM, frames), LOW)] if first else []),
            scratch_shapes=[
                pltpu.VMEM((part_rows, width), LOW), pltpu.VMEM((heads * LANES, width), LOW),
            ]
            + ([] if first else [pltpu.VMEM((heads, frames, LANES), F32)] * 2),
            input_output_aliases={} if first else {group + 11: 0},
            compiler_params=params(1),
            cost_estimate=cost(
                5 * heads * frames * frames * 256, 9_000_000, heads * frames * frames // 2
            ),
            name="attend_back",
        )(*hidden1_rows[half], mixed, mixed_full, query_back, key, value, w_out, *state)
        state = [*made[1:], made[0]]
    query_grad, key_grad, value_grad, w_out_grad, sums0 = made

    me = lax.axis_index("dp").astype(jnp.int32).reshape(1)
    me_spec = pl.BlockSpec(memory_space=pltpu.SMEM)
    bits = ((1, 2, 4), (2, 1, 4)) if clips == 8 else None
    orders = [exchange_order(order) for order in bits] if bits else None
    stack_rows = [local] * 4 if bits else [2 * local] * 2
    *stacks, sums1 = pl.pallas_call(
        functools.partial(weigh_kernel, orders),
        in_specs=[me_spec] + [pl.BlockSpec(memory_space=pltpu.VMEM)] * 10,
        out_shape=[shape((n, width), LOW) for n in stack_rows] + [shape((2, width), F32)],
        scratch_shapes=[pltpu.VMEM((4 * local, width), F32)],
        compiler_params=params(),
        cost_estimate=cost(2 * frames * width * 3 * local, 8_000_000),
        name="weigh",
    )(me, normed1, query_grad, key_grad, value_grad, *turned, w_out_grad, sums0, vectors)
    if bits:
        ends = []
        for index, order in enumerate(bits):
            ends += exchange(stacks[2 * index], stacks[2 * index + 1], "dp", order)
        grads = pl.pallas_call(
            functools.partial(settle_kernel, orders),
            in_specs=[me_spec] + [pl.BlockSpec(memory_space=pltpu.VMEM)] * 4,
            out_shape=[shape((local, width), F32)] * 4,
            compiler_params=params(),
            cost_estimate=cost(0, 12 * local * width),
            name="settle",
        )(me, *ends)
    else:
        grads = jnp.concatenate(lax.psum(tuple(stacks), "dp")).astype(F32)
        grads = jnp.split(grads, 4)

    normed1_parts = pl.pallas_call(
        spread_kernel,
        grid=(2 * steps,),
        in_specs=[pl.BlockSpec((block, local), lambda i: (i, 0))] * 3 + [turned_spec] * 3,
        out_specs=[slot_spec] * (2 * group),
        out_shape=[shape((size, width), LOW)] * (2 * group),
        compiler_params=params(1),
        cost_estimate=cost(2 * frames * width * 3 * local, 6_000_000),
        name="spread",
    )(query_grad, key_grad, value_grad, *turned)
    features_grad = []
    for half in halves:
        features_grad = [
            pl.pallas_call(
                functools.partial(last_kernel, len(features_grad)),
                grid=(1,),
                in_specs=[own_half(half)]
                + [slot_spec] * 4
                + [whole(vectors.shape)]
                + [any_spec] * len(features_grad),
                out_specs=own_half(half),
                out_shape=shape((share, width), LOW),
                input_output_aliases={6: 0} if features_grad else {},
                compiler_params=params(1),
                cost_estimate=cost(20 * size * width, 14 * size * width),
                name="last",
            )(
                x_own,
                *scatter(normed1_parts[half * group : (half + 1) * group]),
                hidden1_grad[half],
                vectors,
                *features_grad,
            )
        ]

    small = jnp.concatenate(
        [sums0[0], sums0[2], fc1_bias_grad[0], sums1.reshape(-1), sums2.reshape(-1)]
    )
    small = sum_over(small, "dp")
    mine = small[: 2 * local + hidden]
    shared = sum_over(small[2 * local + hidden :], "tensor").reshape(6, width)
    return (
        layer_out[None],
        features_grad[0][None],
        grads[0].T,
        mine[:local],
        grads[1].T,
        grads[2].T,
        mine[local : 2 * local],
        grads[3],
        shared[4],
        shared[0],
        shared[1],
        shared[2],
        shared[3],
        fc1_grad.astype(F32),
        mine[2 * local :],
        fc2_grad.astype(F32),
        shared[5],
    )


def solution(mesh):
    rows = P("dp", "tensor", None)
    columns, lines, vector, same = P(None, "tensor"), P("tensor", None), P("tensor"), P()
    in_specs = (
        rows, rows, columns, vector, columns, columns, vector, lines, same,
        same, same, same, same, columns, vector, lines, same,
    )
    out_specs = (
        rows, rows, columns, vector, columns, columns, vector, lines, same,
        same, same, same, same, columns, vector, lines, same,
    )
    return jax.shard_map(
        on_device, mesh=mesh, in_specs=in_specs, out_specs=out_specs, check_vma=False
    )
```

```python
import functools

import jax
import jax.numpy as jnp
from jax import lax
from jax.experimental import pallas as pl
from jax.experimental.pallas import tpu as pltpu
from jax.sharding import PartitionSpec as P

HEAD_DIM = 64
LANES = 128
F32 = jnp.float32
LOW = jnp.bfloat16
MASK = -1e30
CORE, CHIP = 1, 2
ROOM = 56 * 1024 * 1024
NT = (((1,), (1,)), ((), ()))


def params(steps=0):
    semantics = ("arbitrary",) * steps if steps else None
    return pltpu.CompilerParams(vmem_limit_bytes=ROOM, dimension_semantics=semantics)


def cost(flops, moved, exps=0):
    return pl.CostEstimate(flops=flops, bytes_accessed=moved, transcendentals=exps)


def whole(shape):
    return pl.BlockSpec(shape, lambda *_: (0,) * len(shape))


def swap(value, partner):
    size = lax.axis_size("tensor")
    return lax.ppermute(value, "tensor", [(i, i ^ partner) for i in range(size)])


def after(value, *others):
    return lax.optimization_barrier((value, *others))[0]


def gather(own):
    return [own, swap(own, CORE), swap(own, CHIP)]


def finish(parts, *others):
    across = after(parts[2], *others) if others else parts[2]
    return [*parts[:2], across, swap(across, CORE)]


def scatter_direct(parts):
    return [parts[0]] + [swap(parts[j], j) for j in range(1, len(parts))]


def thirds(value):
    high = value.astype(LOW)
    rest = value - high.astype(F32)
    mid = rest.astype(LOW)
    return high, mid, (rest - mid.astype(F32)).astype(LOW)


def place(base, lane, first, pieces):
    for offset, piece in enumerate(pieces):
        base = jnp.where(lane == first + offset, piece, base)
    return base


def norm(values):
    mean = jnp.mean(values, axis=-1, keepdims=True)
    centred = values - mean
    spread = jnp.mean(centred * centred, axis=-1, keepdims=True)
    scaler = lax.rsqrt(spread + 1e-05)
    return centred * scaler, scaler


def norm_back(grad, unit, scaler, gain):
    scaled = grad * gain
    return scaler * (
        scaled
        - jnp.mean(scaled, axis=-1, keepdims=True)
        - unit * jnp.mean(scaled * unit, axis=-1, keepdims=True)
    )


def present(value, count):
    if count == value.shape[0]:
        return value
    row = lax.broadcasted_iota(jnp.int32, value.shape, 0)
    return jnp.where(row < count, value.astype(F32), 0.0).astype(value.dtype)


def pick(step, refs, rows, count):
    size = refs[0].shape[0]
    slots = rows.shape[0] // size
    for turn in range(len(refs) // slots):

        @pl.when(step == turn)
        def _():
            for at in range(slots):
                block = present(refs[turn * slots + at][...], count)
                rows[at * size : (at + 1) * size] = block


def project_kernel(share, slots, aliased, *refs):
    x_refs = refs[:slots]
    vec_ref, bias_ref, wq_ref, wk_ref, wv_ref = refs[slots : slots + 5]
    n_ref, q_ref, k_ref, v_ref, rows, w_tiles, b_tiles = refs[slots + 5 + aliased :]
    half = pl.program_id(0)
    heads = q_ref.shape[0]
    size = x_refs[0].shape[0]

    @pl.when(half == 0)
    def _():
        w_tiles[...] = jnp.zeros_like(w_tiles)
        b_tiles[...] = jnp.zeros_like(b_tiles)
        spot = lax.broadcasted_iota(jnp.int32, (1, LANES), 1) - HEAD_DIM
        ones = (
            jnp.where(spot == 0, HEAD_DIM**0.5, 0.0),
            jnp.where((spot >= 1) & (spot <= 3), 1.0, 0.0),
            jnp.where((spot >= 0) & (spot <= 2), 1.0, 0.0),
        )
        for which, w_ref in enumerate((wq_ref, wk_ref, wv_ref)):
            for head in range(heads):
                at = (which * heads + head) * LANES
                own = slice(head * HEAD_DIM, (head + 1) * HEAD_DIM)
                w_tiles[at : at + HEAD_DIM] = w_ref[own]
                b_tiles[:, at : at + LANES] = ones[which]
                b_tiles[:, at : at + HEAD_DIM] = bias_ref[which : which + 1, own]

    row = lax.broadcasted_iota(jnp.int32, (size, rows.shape[1]), 0) + half * size
    for at in range(slots):
        block = jnp.where(row < share, x_refs[at][...].astype(F32), 0.0)
        rows[at * size : (at + 1) * size] = block
    unit, _ = norm(rows[...])
    normed = (unit * vec_ref[0:1] + vec_ref[1:2]).astype(LOW)
    n_ref[...] = normed
    out = lax.dot_general(normed, w_tiles[...], NT, preferred_element_type=F32) + b_tiles[...]
    row = lax.broadcasted_iota(jnp.int32, (out.shape[0], LANES), 0)
    lane = lax.broadcasted_iota(jnp.int32, (out.shape[0], LANES), 1)
    absent = (lax.rem(row, size) + half * size >= share) & (lane == HEAD_DIM)
    scale = HEAD_DIM ** (-0.5)
    for head in range(heads):
        part = lambda which: out[:, (which * heads + head) * LANES :][:, :LANES]
        q_ref[head] = (part(0).astype(LOW).astype(F32) * scale).astype(LOW)
        k_ref[head] = jnp.where(absent, MASK, part(1)).astype(LOW)
        v_ref[head] = part(2).astype(LOW)


def attend_kernel(aliased, slots, q_ref, k_ref, v_ref, *refs):
    o_ref, m_ref, full_ref, q_out = refs[aliased:]
    heads, block, _ = q_ref.shape
    quarter = block // slots // 2
    lane = lax.broadcasted_iota(jnp.int32, (block, LANES), 1)
    for head in range(heads):
        query = q_ref[head]
        scores = lax.dot_general(query, k_ref[head], NT, preferred_element_type=F32)
        top = jnp.max(scores, axis=-1, keepdims=True)
        weights = jnp.exp(scores - top).astype(LOW)
        out = jnp.dot(weights, v_ref[head], preferred_element_type=F32)
        total = out[:, HEAD_DIM : HEAD_DIM + 1]
        out = out / total
        full_ref[:, head * LANES : (head + 1) * LANES] = out
        low = out[:, :HEAD_DIM].astype(LOW)
        m_ref[:, head * HEAD_DIM : (head + 1) * HEAD_DIM] = low
        for part in range(2 * slots):
            at = ((part % 2) * heads + head) * HEAD_DIM
            o_ref[part // 2 * quarter : (part // 2 + 1) * quarter, at : at + HEAD_DIM] = low[
                part * quarter : (part + 1) * quarter
            ]
        logsum = top + jnp.log(total)
        q_out[head] = place(query, lane, HEAD_DIM + 1, thirds(-logsum))


def feed_kernel(half, share, group, aliased, *refs):
    x_refs, m_refs, wo_refs = refs[:group], refs[group : 3 * group], refs[3 * group : 4 * group]
    g_refs = refs[4 * group : 5 * group]
    vec_ref, w1_ref, w2_ref = refs[5 * group : 5 * group + 3]
    outs = refs[5 * group + 3 + aliased :]
    h_ref, n_ref, a_ref, p_ref, c_ref, db_ref = outs[:6]
    d_refs = outs[6 : 6 + group]
    rows, mixed = outs[6 + group :]
    step = pl.program_id(0)
    size = x_refs[0].shape[0]
    slots = rows.shape[0] // size
    quarter = size // 2
    count = min(size, share - half * size)
    pick(step, x_refs, rows, count)
    pick(step, g_refs, c_ref, count)
    local = wo_refs[0].shape[0]
    for source in range(group):
        for at in range(slots):
            packed = m_refs[source * slots + at][...]
            for part in range(2):
                first = at * size + part * quarter
                mixed[first : first + quarter, source * local : (source + 1) * local] = packed[
                    :, part * local : (part + 1) * local
                ]
    hidden = rows[...].astype(F32) + vec_ref[2:3]
    for source in range(group):
        hidden += jnp.dot(
            mixed[:, source * local : (source + 1) * local],
            wo_refs[source][...],
            preferred_element_type=F32,
        )

    @pl.when(step == 0)
    def _():
        h_ref[...] = hidden[:size]
        db_ref[...] = jnp.zeros_like(db_ref)

    unit, _ = norm(hidden)
    normed = (unit * vec_ref[3:4] + vec_ref[4:5]).astype(LOW)
    n_ref[...] = normed
    pre = jnp.dot(normed, w1_ref[...], preferred_element_type=F32) + vec_ref[5:6]
    active_grad = lax.dot_general(c_ref[...], w2_ref[...], NT, preferred_element_type=F32)
    size_of = jnp.abs(pre)
    bell = jnp.exp(-0.5 * pre * pre)
    t = 1.0 / (1.0 + (0.3275911 * 0.5**0.5) * size_of)
    poly = t * (
        0.127414796 + t * (-0.142248368 + t * (0.7107068705 + t * (-0.7265760135 + t * 0.5307027145)))
    )
    tail = poly * bell
    gate = jnp.where(pre >= 0, 1.0 - tail, tail)
    a_ref[...] = (pre * gate).astype(LOW)
    pre_grad = active_grad * (gate + pre * bell * 0.3989422804014327)
    db_ref[...] += jnp.sum(pre_grad, axis=0, keepdims=True)
    pre_low = pre_grad.astype(LOW)
    p_ref[...] = pre_low
    back = lax.dot_general(pre_low, w1_ref[...], NT, preferred_element_type=F32).astype(LOW)
    for turn in range(group // slots):

        @pl.when(step == turn)
        def _():
            for at in range(slots):
                d_refs[turn * slots + at][...] = back[at * size : (at + 1) * size]


def middle_kernel(count, h_ref, g_ref, vec_ref, *refs):
    out_ref, low_ref, sums_ref = refs[-3:]
    grad = sum(ref[...].astype(F32) for ref in refs[:-3])
    unit, scaler = norm(h_ref[...])
    cot = present(g_ref[...], count).astype(F32)
    hidden_grad = cot + norm_back(grad, unit, scaler, vec_ref[3:4])
    out_ref[...] = hidden_grad
    low_ref[...] = hidden_grad.astype(LOW)
    add = lambda value: jnp.sum(value, axis=0, keepdims=True)
    sums_ref[...] = jnp.concatenate(
        [add(grad * unit), add(grad), add(hidden_grad), add(cot)], axis=0
    )


def attend_back_kernel(parts, first, *refs):
    h_refs = refs[:parts]
    m_ref, full_ref, q_ref, k_ref, v_ref, wo_ref = refs[parts : parts + 6]
    if first:
        dq_ref, dk_sum, dv_sum, dw_ref, sum_ref, kt_ref = refs[parts + 6 : parts + 12]
        rows, wo_tiles = refs[parts + 12 :]
    else:
        dk_old, dv_old, dw_old, sum_old, kt_ref, _ = refs[parts + 6 : parts + 12]
        dq_ref, dk_ref, dv_ref, dw_ref, sum_ref = refs[parts + 12 : parts + 17]
        rows, wo_tiles, dk_sum, dv_sum = refs[parts + 17 :]
    step = pl.program_id(0)
    heads, block, _ = q_ref.shape

    @pl.when(step == 0)
    def _():
        size = h_refs[0].shape[0]
        for part in range(parts):
            rows[part * size : (part + 1) * size] = h_refs[part][...]
        wo_tiles[...] = jnp.zeros_like(wo_tiles)
        for head in range(heads):
            wo_tiles[head * LANES : head * LANES + HEAD_DIM] = wo_ref[
                head * HEAD_DIM : (head + 1) * HEAD_DIM
            ]
        if first:
            for total in (dk_sum, dv_sum, dw_ref, sum_ref):
                total[...] = jnp.zeros_like(total)
            for head in range(heads):
                kt_ref[head] = k_ref[head].astype(F32).T[:HEAD_DIM].astype(LOW)
        else:
            olds = (dk_old, dv_old, dw_old, sum_old)
            for total, old in zip((dk_sum, dv_sum, dw_ref, sum_ref), olds):
                total[...] = old[...]

    scale = HEAD_DIM ** (-0.5)
    lane = lax.broadcasted_iota(jnp.int32, (block, LANES), 1)
    hidden_grad = rows[pl.ds(pl.multiple_of(step * block, block), block)]
    mixed_grad = lax.dot_general(
        hidden_grad, wo_tiles[...], NT, preferred_element_type=F32
    ).astype(LOW)
    dw_ref[...] += lax.dot_general(
        m_ref[...], hidden_grad, (((0,), (0,)), ((), ())), preferred_element_type=F32
    )
    for head in range(heads):
        at = head * HEAD_DIM
        tile = slice(head * LANES, (head + 1) * LANES)
        out_grad = mixed_grad[:, tile]
        delta = jnp.sum(out_grad.astype(F32) * full_ref[:, tile], axis=-1, keepdims=True)
        out_grad = place(out_grad, lane, HEAD_DIM, thirds(-delta))
        query = q_ref[head]
        scores = lax.dot_general(k_ref[head], query, NT, preferred_element_type=F32)
        probs = jnp.exp(scores)
        prob_grad = lax.dot_general(v_ref[head], out_grad, NT, preferred_element_type=F32)
        score_grad = (probs * prob_grad).astype(LOW)
        dv_sum[head] += jnp.dot(probs.astype(LOW), out_grad, preferred_element_type=F32)
        dk_sum[head] += jnp.dot(score_grad, query, preferred_element_type=F32)
        turned = jnp.dot(kt_ref[head], score_grad, preferred_element_type=F32)
        query_grad = (turned.T * scale).astype(LOW)
        dq_ref[:, at : at + HEAD_DIM] = query_grad
        sum_ref[0:1, at : at + HEAD_DIM] += jnp.sum(
            query_grad.astype(F32), axis=0, keepdims=True
        )

    if not first:

        @pl.when(step == pl.num_programs(0) - 1)
        def _():
            for head in range(heads):
                at = head * HEAD_DIM
                for index, (ref, total) in enumerate(((dk_ref, dk_sum), (dv_ref, dv_sum))):
                    low = total[head][:, :HEAD_DIM].astype(LOW)
                    ref[:, at : at + HEAD_DIM] = low
                    sum_ref[index + 1 : index + 2, at : at + HEAD_DIM] = jnp.sum(
                        low.astype(F32), axis=0, keepdims=True
                    )


def weigh_kernel(orders, me_ref, n_ref, dq_ref, dk_ref, dv_ref, wq_ref, wk_ref, wv_ref, dw_ref,
                 sum_ref, vec_ref, *refs):
    outs, (stacks,) = refs[:-1], refs[-1:]
    gain_ref = outs[-1]
    local = dq_ref.shape[1]
    gain = jnp.zeros(vec_ref[0:1].shape, F32)
    shift = gain
    for which, (grad, w_ref) in enumerate(((dq_ref, wq_ref), (dk_ref, wk_ref), (dv_ref, wv_ref))):
        own = lax.dot_general(
            grad[...], n_ref[...], (((0,), (0,)), ((), ())), preferred_element_type=F32
        )
        stacks[which * local : (which + 1) * local] = own
        weights = w_ref[...].astype(F32)
        gain += jnp.sum(weights * own, axis=0, keepdims=True)
        shift += jnp.dot(
            sum_ref[which : which + 1],
            weights,
            precision=lax.Precision.HIGHEST,
            preferred_element_type=F32,
        )
    stacks[3 * local : 4 * local] = dw_ref[...]
    gain_ref[0:1] = (gain - vec_ref[1:2] * shift) / vec_ref[0:1]
    gain_ref[1:2] = shift
    if orders is None:
        outs[0][...] = stacks[: 2 * local].astype(LOW)
        outs[1][...] = stacks[2 * local :].astype(LOW)
        return
    for stack, order in enumerate(orders):
        size = 2 * local // len(order)
        for spot, slot in enumerate(order):
            which, at = divmod(spot, len(order) // 2)
            start = stack * 2 * local + jnp.bitwise_xor(me_ref[0], slot) * size
            piece = stacks[pl.ds(pl.multiple_of(start, size), size)]
            outs[2 * stack + which][at * size : (at + 1) * size] = piece.astype(LOW)


def outer_kernel(order, me_ref, left_ref, right_ref, keep_ref, send_ref, total):
    step = pl.program_id(0)

    @pl.when(step == 0)
    def _():
        total[...] = jnp.zeros_like(total)

    total[...] += lax.dot_general(
        left_ref[...], right_ref[...], (((0,), (0,)), ((), ())), preferred_element_type=F32
    )

    @pl.when(step == pl.num_programs(0) - 1)
    def _():
        size = total.shape[0] // len(order)
        for spot, slot in enumerate(order):
            which, at = divmod(spot, len(order) // 2)
            start = jnp.bitwise_xor(me_ref[0], slot) * size
            piece = total[pl.ds(pl.multiple_of(start, size), size)].astype(LOW)
            (keep_ref, send_ref)[which][at * size : (at + 1) * size] = piece


def settle_kernel(orders, me_ref, *refs):
    outs = refs[2 * len(orders) :]
    sides = len(outs) // len(orders)
    for stack, order in enumerate(orders):
        halves = refs[2 * stack : 2 * stack + 2]
        size = 2 * halves[0].shape[0] // len(order)
        per = len(order) // sides
        for spot, slot in enumerate(order):
            which, at = divmod(spot, len(order) // 2)
            value = halves[which][at * size : (at + 1) * size].astype(F32)
            place_at = jnp.bitwise_xor(me_ref[0], slot)
            start = pl.multiple_of(lax.rem(place_at, per) * size, size)
            for side in range(sides):

                @pl.when(lax.div(place_at, per) == side)
                def _():
                    outs[sides * stack + side][pl.ds(start, size)] = value


def spread_kernel(dq_ref, dk_ref, dv_ref, wq_ref, wk_ref, wv_ref, *outs):
    total = sum(
        jnp.dot(grad[...], weight[...], preferred_element_type=F32)
        for grad, weight in ((dq_ref, wq_ref), (dk_ref, wk_ref), (dv_ref, wv_ref))
    ).astype(LOW)
    size = outs[0].shape[0]
    slots = total.shape[0] // size
    step = pl.program_id(0)
    for turn in range(len(outs) // slots):

        @pl.when(step == turn)
        def _():
            for at in range(slots):
                outs[turn * slots + at][...] = total[at * size : (at + 1) * size]


def last_kernel(aliased, x_ref, d0_ref, d1_ref, d2_ref, h_ref, vec_ref, *refs):
    out_ref = refs[aliased]
    grad = d0_ref[...].astype(F32) + d1_ref[...].astype(F32) + d2_ref[...].astype(F32)
    unit, scaler = norm(x_ref[...].astype(F32))
    out_ref[...] = (h_ref[...] + norm_back(grad, unit, scaler, vec_ref[0:1])).astype(LOW)


def output_kernel(ha_ref, hb_ref, vec_ref, *refs):
    out_ref = refs[-1]
    size = ha_ref.shape[0]
    share = out_ref.shape[0]
    for part, h_ref in enumerate((ha_ref, hb_ref)):
        mlp = sum(ref[part].astype(F32) for ref in refs[:-1])
        value = (h_ref[...] + mlp + vec_ref[6:7]).astype(LOW)
        count = min(size, share - part * size)
        out_ref[part * size : part * size + count] = value[:count]


def pair(value, axis, step):
    size = lax.axis_size(axis)
    return lax.ppermute(value, axis, [(i, i ^ step) for i in range(size)])


def sum_over(value, axis):
    size = lax.axis_size(axis)
    if size & (size - 1):
        return lax.psum(value, axis)
    step = 1
    while step < size:
        value = value + pair(value, axis, step)
        step *= 2
    return value


def exchange_order(bits):
    order = [0]
    for bit in reversed(bits):
        order = order + [slot | bit for slot in order]
    return order


def halve(parts, axis, bit):
    keep, send = parts
    return tuple(jnp.split(keep + pair(send, axis, bit), 2))


def double(parts, axis, bits):
    keep = parts[0] + pair(parts[1], axis, bits[-1])
    for bit in reversed(bits[1:]):
        keep = jnp.concatenate([keep, pair(keep, axis, bit)])
    return [keep, pair(keep, axis, bits[0])]


def on_device(
    features, cotangent, w_query, bias_query, w_key, w_value, bias_value, w_out, bias_out,
    norm1_gain, norm1_bias, norm2_gain, norm2_bias, w_fc1, bias_fc1, w_fc2, bias_fc2,
):
    _, share, width = features.shape
    local = w_query.shape[1]
    heads = local // HEAD_DIM
    hidden = w_fc1.shape[1]
    group = lax.axis_size("tensor")
    clips = lax.axis_size("dp")
    rows = -(-share // LANES) * LANES
    size = rows // 2
    frames = group * rows
    part_rows = group * size
    slots = 2
    block = slots * size
    steps = group // slots
    shape = jax.ShapeDtypeStruct
    halves = range(2)
    count = lambda half: min(size, share - half * size)

    x_own, g_own = features[0], cotangent[0]
    x_all = gather(x_own)
    g_all = gather(after(g_own, x_all[2]))
    wo_all = gather(after(w_out, g_all[2]))
    row = lambda value: value.astype(F32)
    vectors = jnp.concatenate(
        [norm1_gain, norm1_bias, bias_out, norm2_gain, norm2_bias, row(bias_fc1), bias_fc2]
    ).reshape(-1, width)
    biases = [row(bias_query), jnp.zeros((local,), F32), row(bias_value)]
    biases = jnp.concatenate(biases).reshape(3, local)
    turned = [w_query.T, w_key.T, w_value.T]

    slot_spec = whole((size, width))
    turned_spec = whole((local, width))
    any_spec = pl.BlockSpec(memory_space=pl.ANY)
    at_half = lambda half, n: pl.BlockSpec((block, n), lambda i: (half * steps + i, 0))
    own_half = lambda half: pl.BlockSpec((size, width), lambda *_: (half, 0))
    head_half = lambda half: pl.BlockSpec((heads, block, LANES), lambda i: (0, half * steps + i, 0))
    head_shape = shape((heads, frames, LANES), LOW)

    made = []
    for turn in range(steps):
        if turn:
            x_all = finish(x_all, made[0])
        made = pl.pallas_call(
            functools.partial(project_kernel, share, slots, len(made)),
            grid=(2,),
            in_specs=[pl.BlockSpec((size, width), lambda i: (i, 0))] * slots
            + [whole(vectors.shape), whole(biases.shape)]
            + [turned_spec] * 3
            + [any_spec] * len(made),
            out_specs=[pl.BlockSpec((block, width), lambda i, turn=turn: (i * steps + turn, 0))]
            + [
                pl.BlockSpec((heads, block, LANES), lambda i, turn=turn: (0, i * steps + turn, 0))
            ]
            * 3,
            out_shape=[shape((frames, width), LOW)] + [head_shape] * 3,
            scratch_shapes=[
                pltpu.VMEM((block, width), F32),
                pltpu.VMEM((3 * heads * LANES, width), LOW),
                pltpu.VMEM((1, 3 * heads * LANES), F32),
            ],
            input_output_aliases={slots + 5 + i: i for i in range(len(made))},
            compiler_params=params(1),
            cost_estimate=cost(2 * part_rows * width * 9 * LANES, 6_000_000),
            name="project",
        )(*x_all[turn * slots : (turn + 1) * slots], vectors, biases, *turned, *made)
    normed1, query, key, value = made

    head_whole = whole((heads, frames, LANES))
    made, packed = [], []
    for half in halves:
        made = pl.pallas_call(
            functools.partial(attend_kernel, len(made), slots),
            grid=(steps,),
            in_specs=[head_half(half), head_whole, head_whole] + [any_spec] * len(made),
            out_specs=[
                pl.BlockSpec((block // 2, 2 * local), lambda i: (i, 0)),
                at_half(half, local), at_half(half, heads * LANES), head_half(half),
            ],
            out_shape=[
                shape((part_rows // 2, 2 * local), LOW), shape((frames, local), LOW),
                shape((frames, heads * LANES), F32), head_shape,
            ],
            input_output_aliases={3 + i: 1 + i for i in range(len(made))},
            compiler_params=params(1),
            cost_estimate=cost(
                2 * heads * frames * frames * 256, 5_000_000, heads * frames * frames // 2
            ),
            name="attend",
        )(query, key, value, *made)
        packed.append(gather(made[0]))
        made = made[1:]
        if half == 0:
            g_all = finish(g_all, made[0])
    mixed, mixed_full, query_back = made
    packed[0] = finish(packed[0], mixed)
    wo_all = finish(wo_all, mixed)

    low_rows = shape((frames, hidden), LOW)
    made, hidden1, fc1_bias_grad, normed2_parts = [], [], 0.0, []
    for half in halves:
        if half:
            packed[half] = finish(packed[half], made[0])
        sources = packed[half]
        packed_specs, packed_args = [], []
        for source in range(group):
            for at in range(slots):
                packed_args.append(sources[source])
                packed_specs.append(
                    pl.BlockSpec(
                        (size // 2, 2 * local),
                        lambda i, source=source, at=at: ((i * slots + at) ^ source, 0),
                    )
                )
        made = pl.pallas_call(
            functools.partial(feed_kernel, half, share, group, len(made)),
            grid=(steps,),
            in_specs=[own_half(half)] * group
            + packed_specs
            + [whole((local, width))] * group
            + [own_half(half)] * group
            + [whole(vectors.shape), whole((width, hidden)), whole((hidden, width))]
            + [any_spec] * len(made),
            out_specs=[slot_spec]
            + [at_half(half, n) for n in (width, hidden, hidden, width)]
            + [whole((1, hidden))]
            + [slot_spec] * group,
            out_shape=[
                shape((size, width), F32), shape((frames, width), LOW), low_rows, low_rows,
                shape((frames, width), LOW), shape((1, hidden), F32),
            ]
            + [shape((size, width), LOW)] * group,
            scratch_shapes=[pltpu.VMEM((block, width), LOW)] * 2,
            input_output_aliases={5 * group + 3 + i: 1 + i for i in range(len(made))},
            compiler_params=params(1),
            cost_estimate=cost(4 * frames * width * hidden, 12_000_000, frames * hidden // 2),
            name="feed",
        )(*x_all, *packed_args, *wo_all, *g_all, vectors, w_fc1, w_fc2, *made)
        hidden1.append(made[0])
        fc1_bias_grad = fc1_bias_grad + made[5]
        normed2_parts.append(made[6:])
        made = made[1:5]
    normed2, active, pre_low, cot_rows = made

    hidden1_grad, sums2, hidden1_rows = [], 0.0, []
    far = normed2_parts[1][2] + swap(normed2_parts[1][3], CORE)
    all_terms = [
        scatter_direct(normed2_parts[0]),
        [normed2_parts[1][0], swap(normed2_parts[1][1], CORE), swap(far, CHIP)],
    ]
    all_terms[0][0] = after(all_terms[0][0], far)
    for half in halves:
        terms = all_terms[half]
        grad, low, sums = pl.pallas_call(
            functools.partial(middle_kernel, count(half)),
            grid=(1,),
            in_specs=[slot_spec, own_half(half), whole(vectors.shape)] + [slot_spec] * len(terms),
            out_specs=[slot_spec, slot_spec, whole((4, width))],
            out_shape=[
                shape((size, width), F32), shape((size, width), LOW), shape((4, width), F32),
            ],
            compiler_params=params(1),
            cost_estimate=cost(20 * size * width, 16 * size * width),
            name="middle",
        )(hidden1[half], g_own, vectors, *terms)
        hidden1_grad.append(grad)
        sums2 = sums2 + sums
        hidden1_rows.append(gather(low))

    tn = lambda left, right: lax.dot_general(
        left, right, (((0,), (0,)), ((), ())), preferred_element_type=F32
    )
    me = lax.axis_index("dp").astype(jnp.int32).reshape(1)
    me_spec = pl.BlockSpec(memory_space=pltpu.SMEM)
    bits = ((1, 2, 4), (2, 1, 4)) if clips == 8 else None
    orders = [exchange_order(order) for order in bits] if bits else None
    hidden1_rows[0] = finish(hidden1_rows[0])
    if bits:
        fc = []
        active, normed2 = after(active, hidden1_rows[0][0]), after(normed2, hidden1_rows[0][0])
        for index, (left, right) in enumerate(((active, cot_rows), (normed2, pre_low))):
            fc.append(
                pl.pallas_call(
                    functools.partial(outer_kernel, orders[index]),
                    grid=(2 * steps,),
                    in_specs=[me_spec]
                    + [pl.BlockSpec((block, part.shape[1]), lambda i: (i, 0)) for part in (left, right)],
                    out_specs=[whole((left.shape[1] // 2, right.shape[1]))] * 2,
                    out_shape=[shape((left.shape[1] // 2, right.shape[1]), LOW)] * 2,
                    scratch_shapes=[pltpu.VMEM((left.shape[1], right.shape[1]), F32)],
                    compiler_params=params(1),
                    cost_estimate=cost(2 * frames * width * hidden, 8_000_000),
                    name="outer",
                )(me, left, right)
            )
        fc[0] = halve(fc[0], "dp", bits[0][0])
        hidden1_rows[0][0] = after(hidden1_rows[0][0], fc[0][1], fc[1][1])
    else:
        fc_own = (tn(active, cot_rows).astype(LOW), tn(normed2, pre_low).astype(LOW))
        fc2_grad, fc1_grad = [total.astype(F32) for total in lax.psum(fc_own, "dp")]
    mlp_part = jnp.dot(active, w_fc2, preferred_element_type=F32).astype(LOW)
    mlp_part = mlp_part.reshape(2, group, size, width)
    mlp_far = mlp_part[:, 2] + swap(mlp_part[:, 3], CORE)
    hidden1_rows[0][0] = after(hidden1_rows[0][0], mlp_part)
    hidden1_rows[1][0] = after(hidden1_rows[1][0], mlp_far)
    mlp_far = swap(after(mlp_far, hidden1_rows[1][2]), CHIP)
    mlp = [mlp_part[:, 0], swap(mlp_part[:, 1], CORE), mlp_far]
    layer_out = pl.pallas_call(
        output_kernel,
        out_shape=shape((share, width), LOW),
        compiler_params=params(),
        cost_estimate=cost(8 * rows * width, 12 * rows * width),
        name="output",
    )(*hidden1, vectors, *mlp)

    back = 256
    turns = part_rows // back
    line = shape((frames, local), LOW)
    state = []
    sums_shape = [shape((heads, frames, LANES), F32)] * 2
    side_shape = [shape((local, width), F32), shape((3, local), F32)]
    side_spec = [turned_spec, whole((3, local))]
    kt_spec = whole((heads, HEAD_DIM, frames))
    for half in halves:
        first = half == 0
        if not first:
            hidden1_rows[1] = finish(hidden1_rows[1], made[0])
            if bits:
                fc[0] = halve(fc[0], "dp", bits[0][1])
                fc[1] = halve(fc[1], "dp", bits[1][0])
                hidden1_rows[1][0] = after(hidden1_rows[1][0], fc[0][1], fc[1][1])
        by_block = lambda n, half=half: pl.BlockSpec((back, n), lambda i: (half * turns + i, 0))
        made = pl.pallas_call(
            functools.partial(attend_back_kernel, group, first),
            grid=(turns,),
            in_specs=[slot_spec] * group
            + [
                by_block(local), by_block(heads * LANES),
                pl.BlockSpec((heads, back, LANES), lambda i, half=half: (0, half * turns + i, 0)),
                head_whole, head_whole, turned_spec,
            ]
            + ([] if first else [head_whole] * 2 + side_spec + [kt_spec, any_spec]),
            out_specs=[by_block(local)]
            + ([head_whole] * 2 if first else [whole((frames, local))] * 2)
            + side_spec
            + ([kt_spec] if first else []),
            out_shape=[line]
            + (sums_shape if first else [line, line])
            + side_shape
            + ([shape((heads, HEAD_DIM, frames), LOW)] if first else []),
            scratch_shapes=[
                pltpu.VMEM((part_rows, width), LOW), pltpu.VMEM((heads * LANES, width), LOW),
            ]
            + ([] if first else [pltpu.VMEM((heads, frames, LANES), F32)] * 2),
            input_output_aliases={} if first else {group + 11: 0},
            compiler_params=params(1),
            cost_estimate=cost(
                5 * heads * frames * frames * 256, 9_000_000, heads * frames * frames // 2
            ),
            name="attend_back",
        )(*hidden1_rows[half], mixed, mixed_full, query_back, key, value, w_out, *state)
        state = [*made[1:], made[0]]
    query_grad, key_grad, value_grad, w_out_grad, sums0 = made

    w_out_grad = after(w_out_grad, *mlp[1:])
    if bits:
        fc[1] = halve(fc[1], "dp", bits[1][1])
        w_out_grad = after(w_out_grad, fc[1][1])
    stack_rows = [local] * 4 if bits else [2 * local] * 2
    *stacks, sums1 = pl.pallas_call(
        functools.partial(weigh_kernel, orders),
        in_specs=[me_spec] + [pl.BlockSpec(memory_space=pltpu.VMEM)] * 10,
        out_shape=[shape((n, width), LOW) for n in stack_rows] + [shape((2, width), F32)],
        scratch_shapes=[pltpu.VMEM((4 * local, width), F32)],
        compiler_params=params(),
        cost_estimate=cost(2 * frames * width * 3 * local, 8_000_000),
        name="weigh",
    )(me, normed1, query_grad, key_grad, value_grad, *turned, w_out_grad, sums0, vectors)
    if bits:
        def settle(ends, count, size):
            return pl.pallas_call(
                functools.partial(settle_kernel, orders),
                in_specs=[me_spec] + [pl.BlockSpec(memory_space=pltpu.VMEM)] * 4,
                out_shape=[shape((size, width), F32)] * count,
                compiler_params=params(),
                cost_estimate=cost(0, 6 * count * size * width),
                name="settle",
            )(me, *ends)

        fc_ends, ends = [], []
        for index, order in enumerate(bits):
            fc_ends += double(fc[index], "dp", order)
        for index, order in enumerate(bits):
            parts = (stacks[2 * index], stacks[2 * index + 1])
            for bit in order[:-1]:
                parts = halve(parts, "dp", bit)
            ends += double(parts, "dp", order)
        fc2_grad, fc1_grad = settle(fc_ends, 2, hidden)
        grads = settle(ends, 4, local)
    else:
        grads = jnp.concatenate(lax.psum(tuple(stacks), "dp")).astype(F32)
        grads = jnp.split(grads, 4)

    normed1_parts = pl.pallas_call(
        spread_kernel,
        grid=(2 * steps,),
        in_specs=[pl.BlockSpec((block, local), lambda i: (i, 0))] * 3 + [turned_spec] * 3,
        out_specs=[slot_spec] * (2 * group),
        out_shape=[shape((size, width), LOW)] * (2 * group),
        compiler_params=params(1),
        cost_estimate=cost(2 * frames * width * 3 * local, 6_000_000),
        name="spread",
    )(query_grad, key_grad, value_grad, *turned)
    features_grad, normed1_terms = [], []
    for half in halves:
        parts = normed1_parts[half * group : (half + 1) * group]
        far = parts[2] + swap(parts[3], CORE)
        normed1_terms.append([parts[0], swap(parts[1], CORE), swap(far, CHIP)])
    for half in halves:
        features_grad = [
            pl.pallas_call(
                functools.partial(last_kernel, len(features_grad)),
                grid=(1,),
                in_specs=[own_half(half)]
                + [slot_spec] * 4
                + [whole(vectors.shape)]
                + [any_spec] * len(features_grad),
                out_specs=own_half(half),
                out_shape=shape((share, width), LOW),
                input_output_aliases={6: 0} if features_grad else {},
                compiler_params=params(1),
                cost_estimate=cost(20 * size * width, 14 * size * width),
                name="last",
            )(
                x_own,
                *normed1_terms[half],
                hidden1_grad[half],
                vectors,
                *features_grad,
            )
        ]

    small = jnp.concatenate(
        [sums0[0], sums0[2], fc1_bias_grad[0], sums1.reshape(-1), sums2.reshape(-1)]
    )
    small = sum_over(small, "dp")
    mine = small[: 2 * local + hidden]
    shared = sum_over(small[2 * local + hidden :], "tensor").reshape(6, width)
    return (
        layer_out[None],
        features_grad[0][None],
        grads[0].T,
        mine[:local],
        grads[1].T,
        grads[2].T,
        mine[local : 2 * local],
        grads[3],
        shared[4],
        shared[0],
        shared[1],
        shared[2],
        shared[3],
        fc1_grad,
        mine[2 * local :],
        fc2_grad,
        shared[5],
    )


def solution(mesh):
    rows = P("dp", "tensor", None)
    columns, lines, vector, same = P(None, "tensor"), P("tensor", None), P("tensor"), P()
    in_specs = (
        rows, rows, columns, vector, columns, columns, vector, lines, same,
        same, same, same, same, columns, vector, lines, same,
    )
    out_specs = (
        rows, rows, columns, vector, columns, columns, vector, lines, same,
        same, same, same, same, columns, vector, lines, same,
    )
    return jax.shard_map(
        on_device, mesh=mesh, in_specs=in_specs, out_specs=out_specs, check_vma=False
    )
```

```python
import functools

import jax
import jax.numpy as jnp
from jax import lax
from jax.experimental import pallas as pl
from jax.experimental.pallas import tpu as pltpu
from jax.sharding import PartitionSpec as P

HEAD_DIM = 64
LANES = 128
F32 = jnp.float32
LOW = jnp.bfloat16
MASK = -1e30
CORE, CHIP = 1, 2
ROOM = 56 * 1024 * 1024
NT = (((1,), (1,)), ((), ()))


def params(steps=0):
    semantics = ("arbitrary",) * steps if steps else None
    return pltpu.CompilerParams(vmem_limit_bytes=ROOM, dimension_semantics=semantics)


def cost(flops, moved, exps=0):
    return pl.CostEstimate(flops=flops, bytes_accessed=moved, transcendentals=exps)


def whole(shape):
    return pl.BlockSpec(shape, lambda *_: (0,) * len(shape))


def swap(value, partner):
    size = lax.axis_size("tensor")
    return lax.ppermute(value, "tensor", [(i, i ^ partner) for i in range(size)])


def after(value, *others):
    return lax.optimization_barrier((value, *others))[0]


def gather(own):
    return [own, swap(own, CORE), swap(own, CHIP)]


def finish(parts, *others):
    across = after(parts[2], *others) if others else parts[2]
    return [*parts[:2], across, swap(across, CORE)]


def scatter_direct(parts):
    return [parts[0]] + [swap(parts[j], j) for j in range(1, len(parts))]


def thirds(value):
    high = value.astype(LOW)
    rest = value - high.astype(F32)
    mid = rest.astype(LOW)
    return high, mid, (rest - mid.astype(F32)).astype(LOW)


def place(base, lane, first, pieces):
    for offset, piece in enumerate(pieces):
        base = jnp.where(lane == first + offset, piece, base)
    return base


def norm(values):
    mean = jnp.mean(values, axis=-1, keepdims=True)
    centred = values - mean
    spread = jnp.mean(centred * centred, axis=-1, keepdims=True)
    scaler = lax.rsqrt(spread + 1e-05)
    return centred * scaler, scaler


def norm_back(grad, unit, scaler, gain):
    scaled = grad * gain
    return scaler * (
        scaled
        - jnp.mean(scaled, axis=-1, keepdims=True)
        - unit * jnp.mean(scaled * unit, axis=-1, keepdims=True)
    )


def present(value, count):
    if count == value.shape[0]:
        return value
    row = lax.broadcasted_iota(jnp.int32, value.shape, 0)
    return jnp.where(row < count, value.astype(F32), 0.0).astype(value.dtype)


def pick(step, refs, rows, count):
    size = refs[0].shape[0]
    slots = rows.shape[0] // size
    for turn in range(len(refs) // slots):

        @pl.when(step == turn)
        def _():
            for at in range(slots):
                block = present(refs[turn * slots + at][...], count)
                rows[at * size : (at + 1) * size] = block


def stack_kernel(*refs):
    vec_ref, bias_ref = refs[-2:]
    for index, ref in enumerate(refs[:7]):
        vec_ref[index : index + 1] = ref[...].astype(F32).reshape(1, -1)
    bias_ref[...] = jnp.zeros_like(bias_ref)
    for index, ref in ((0, refs[7]), (2, refs[8])):
        bias_ref[index : index + 1] = ref[...].astype(F32).reshape(1, -1)


def project_kernel(share, slots, aliased, *refs):
    x_refs = refs[:slots]
    vec_ref, bias_ref, wq_ref, wk_ref, wv_ref = refs[slots : slots + 5]
    n_ref, q_ref, k_ref, v_ref, rows, w_tiles, b_tiles = refs[slots + 5 + aliased :]
    half = pl.program_id(0)
    heads = q_ref.shape[0]
    size = x_refs[0].shape[0]

    @pl.when(half == 0)
    def _():
        w_tiles[...] = jnp.zeros_like(w_tiles)
        b_tiles[...] = jnp.zeros_like(b_tiles)
        spot = lax.broadcasted_iota(jnp.int32, (1, LANES), 1) - HEAD_DIM
        ones = (
            jnp.where(spot == 0, HEAD_DIM**0.5, 0.0),
            jnp.where((spot >= 1) & (spot <= 3), 1.0, 0.0),
            jnp.where((spot >= 0) & (spot <= 2), 1.0, 0.0),
        )
        for which, w_ref in enumerate((wq_ref, wk_ref, wv_ref)):
            for head in range(heads):
                at = (which * heads + head) * LANES
                own = slice(head * HEAD_DIM, (head + 1) * HEAD_DIM)
                w_tiles[at : at + HEAD_DIM] = w_ref[own]
                b_tiles[:, at : at + LANES] = ones[which]
                b_tiles[:, at : at + HEAD_DIM] = bias_ref[which : which + 1, own]

    row = lax.broadcasted_iota(jnp.int32, (size, rows.shape[1]), 0) + half * size
    for at in range(slots):
        block = jnp.where(row < share, x_refs[at][...].astype(F32), 0.0)
        rows[at * size : (at + 1) * size] = block
    unit, _ = norm(rows[...])
    normed = (unit * vec_ref[0:1] + vec_ref[1:2]).astype(LOW)
    n_ref[...] = normed
    out = lax.dot_general(normed, w_tiles[...], NT, preferred_element_type=F32) + b_tiles[...]
    row = lax.broadcasted_iota(jnp.int32, (out.shape[0], LANES), 0)
    lane = lax.broadcasted_iota(jnp.int32, (out.shape[0], LANES), 1)
    absent = (lax.rem(row, size) + half * size >= share) & (lane == HEAD_DIM)
    scale = HEAD_DIM ** (-0.5)
    for head in range(heads):
        part = lambda which: out[:, (which * heads + head) * LANES :][:, :LANES]
        q_ref[head] = (part(0).astype(LOW).astype(F32) * scale).astype(LOW)
        k_ref[head] = jnp.where(absent, MASK, part(1)).astype(LOW)
        v_ref[head] = part(2).astype(LOW)


def attend_kernel(aliased, slots, q_ref, k_ref, v_ref, *refs):
    o_ref, m_ref, full_ref, q_out = refs[aliased:]
    heads, block, _ = q_ref.shape
    quarter = block // slots // 2
    lane = lax.broadcasted_iota(jnp.int32, (block, LANES), 1)
    for head in range(heads):
        query = q_ref[head]
        scores = lax.dot_general(query, k_ref[head], NT, preferred_element_type=F32)
        top = jnp.max(scores, axis=-1, keepdims=True)
        weights = jnp.exp(scores - top).astype(LOW)
        out = jnp.dot(weights, v_ref[head], preferred_element_type=F32)
        total = out[:, HEAD_DIM : HEAD_DIM + 1]
        out = out / total
        full_ref[:, head * LANES : (head + 1) * LANES] = out
        low = out[:, :HEAD_DIM].astype(LOW)
        m_ref[:, head * HEAD_DIM : (head + 1) * HEAD_DIM] = low
        for part in range(2 * slots):
            at = ((part % 2) * heads + head) * HEAD_DIM
            o_ref[part // 2 * quarter : (part // 2 + 1) * quarter, at : at + HEAD_DIM] = low[
                part * quarter : (part + 1) * quarter
            ]
        logsum = top + jnp.log(total)
        q_out[head] = place(query, lane, HEAD_DIM + 1, thirds(-logsum))


def feed_kernel(half, share, group, aliased, *refs):
    x_refs, m_refs, wo_refs = refs[:group], refs[group : 3 * group], refs[3 * group : 4 * group]
    g_refs = refs[4 * group : 5 * group]
    vec_ref, w1_ref, w2_ref = refs[5 * group : 5 * group + 3]
    outs = refs[5 * group + 3 + aliased :]
    h_ref, n_ref, a_ref, p_ref, c_ref, db_ref = outs[:6]
    d_refs = outs[6 : 6 + group]
    rows, mixed = outs[6 + group :]
    step = pl.program_id(0)
    size = x_refs[0].shape[0]
    slots = rows.shape[0] // size
    quarter = size // 2
    count = min(size, share - half * size)
    pick(step, x_refs, rows, count)
    pick(step, g_refs, c_ref, count)
    local = wo_refs[0].shape[0]
    for source in range(group):
        for at in range(slots):
            packed = m_refs[source * slots + at][...]
            for part in range(2):
                first = at * size + part * quarter
                mixed[first : first + quarter, source * local : (source + 1) * local] = packed[
                    :, part * local : (part + 1) * local
                ]
    hidden = rows[...].astype(F32) + vec_ref[2:3]
    for source in range(group):
        hidden += jnp.dot(
            mixed[:, source * local : (source + 1) * local],
            wo_refs[source][...],
            preferred_element_type=F32,
        )

    @pl.when(step == 0)
    def _():
        h_ref[...] = hidden[:size]
        db_ref[...] = jnp.zeros_like(db_ref)

    unit, _ = norm(hidden)
    normed = (unit * vec_ref[3:4] + vec_ref[4:5]).astype(LOW)
    n_ref[...] = normed
    pre = jnp.dot(normed, w1_ref[...], preferred_element_type=F32) + vec_ref[5:6]
    active_grad = lax.dot_general(c_ref[...], w2_ref[...], NT, preferred_element_type=F32)
    size_of = jnp.abs(pre)
    bell = jnp.exp(-0.5 * pre * pre)
    t = 1.0 / (1.0 + (0.3275911 * 0.5**0.5) * size_of)
    poly = t * (
        0.127414796 + t * (-0.142248368 + t * (0.7107068705 + t * (-0.7265760135 + t * 0.5307027145)))
    )
    tail = poly * bell
    gate = jnp.where(pre >= 0, 1.0 - tail, tail)
    a_ref[...] = (pre * gate).astype(LOW)
    pre_grad = active_grad * (gate + pre * bell * 0.3989422804014327)
    db_ref[...] += jnp.sum(pre_grad, axis=0, keepdims=True)
    pre_low = pre_grad.astype(LOW)
    p_ref[...] = pre_low
    back = lax.dot_general(pre_low, w1_ref[...], NT, preferred_element_type=F32).astype(LOW)
    for turn in range(group // slots):

        @pl.when(step == turn)
        def _():
            for at in range(slots):
                d_refs[turn * slots + at][...] = back[at * size : (at + 1) * size]


def middle_kernel(count, h_ref, g_ref, vec_ref, *refs):
    out_ref, low_ref, sums_ref = refs[-3:]
    grad = sum(ref[...].astype(F32) for ref in refs[:-3])
    unit, scaler = norm(h_ref[...])
    cot = present(g_ref[...], count).astype(F32)
    hidden_grad = cot + norm_back(grad, unit, scaler, vec_ref[3:4])
    out_ref[...] = hidden_grad
    low_ref[...] = hidden_grad.astype(LOW)
    add = lambda value: jnp.sum(value, axis=0, keepdims=True)
    sums_ref[...] = jnp.concatenate(
        [add(grad * unit), add(grad), add(hidden_grad), add(cot)], axis=0
    )


def attend_back_kernel(parts, first, *refs):
    h_refs = refs[:parts]
    m_ref, full_ref, q_ref, k_ref, v_ref, wo_ref = refs[parts : parts + 6]
    if first:
        dq_ref, dk_sum, dv_sum, dw_ref, sum_ref, kt_ref = refs[parts + 6 : parts + 12]
        rows, wo_tiles = refs[parts + 12 :]
    else:
        dk_old, dv_old, dw_old, sum_old, kt_ref, _ = refs[parts + 6 : parts + 12]
        dq_ref, dk_ref, dv_ref, dw_ref, sum_ref = refs[parts + 12 : parts + 17]
        rows, wo_tiles, dk_sum, dv_sum = refs[parts + 17 :]
    step = pl.program_id(0)
    heads, block, _ = q_ref.shape

    @pl.when(step == 0)
    def _():
        size = h_refs[0].shape[0]
        for part in range(parts):
            rows[part * size : (part + 1) * size] = h_refs[part][...]
        wo_tiles[...] = jnp.zeros_like(wo_tiles)
        for head in range(heads):
            wo_tiles[head * LANES : head * LANES + HEAD_DIM] = wo_ref[
                head * HEAD_DIM : (head + 1) * HEAD_DIM
            ]
        if first:
            for total in (dk_sum, dv_sum, dw_ref, sum_ref):
                total[...] = jnp.zeros_like(total)
            for head in range(heads):
                kt_ref[head] = k_ref[head].astype(F32).T[:HEAD_DIM].astype(LOW)
        else:
            olds = (dk_old, dv_old, dw_old, sum_old)
            for total, old in zip((dk_sum, dv_sum, dw_ref, sum_ref), olds):
                total[...] = old[...]

    scale = HEAD_DIM ** (-0.5)
    lane = lax.broadcasted_iota(jnp.int32, (block, LANES), 1)
    hidden_grad = rows[pl.ds(pl.multiple_of(step * block, block), block)]
    mixed_grad = lax.dot_general(
        hidden_grad, wo_tiles[...], NT, preferred_element_type=F32
    ).astype(LOW)
    dw_ref[...] += lax.dot_general(
        m_ref[...], hidden_grad, (((0,), (0,)), ((), ())), preferred_element_type=F32
    )
    for head in range(heads):
        at = head * HEAD_DIM
        tile = slice(head * LANES, (head + 1) * LANES)
        out_grad = mixed_grad[:, tile]
        delta = jnp.sum(out_grad.astype(F32) * full_ref[:, tile], axis=-1, keepdims=True)
        out_grad = place(out_grad, lane, HEAD_DIM, thirds(-delta))
        query = q_ref[head]
        scores = lax.dot_general(k_ref[head], query, NT, preferred_element_type=F32)
        probs = jnp.exp(scores)
        prob_grad = lax.dot_general(v_ref[head], out_grad, NT, preferred_element_type=F32)
        score_grad = (probs * prob_grad).astype(LOW)
        dv_sum[head] += jnp.dot(probs.astype(LOW), out_grad, preferred_element_type=F32)
        dk_sum[head] += jnp.dot(score_grad, query, preferred_element_type=F32)
        turned = jnp.dot(kt_ref[head], score_grad, preferred_element_type=F32)
        query_grad = (turned.T * scale).astype(LOW)
        dq_ref[:, at : at + HEAD_DIM] = query_grad
        sum_ref[0:1, at : at + HEAD_DIM] += jnp.sum(
            query_grad.astype(F32), axis=0, keepdims=True
        )

    if not first:

        @pl.when(step == pl.num_programs(0) - 1)
        def _():
            for head in range(heads):
                at = head * HEAD_DIM
                for index, (ref, total) in enumerate(((dk_ref, dk_sum), (dv_ref, dv_sum))):
                    low = total[head][:, :HEAD_DIM].astype(LOW)
                    ref[:, at : at + HEAD_DIM] = low
                    sum_ref[index + 1 : index + 2, at : at + HEAD_DIM] = jnp.sum(
                        low.astype(F32), axis=0, keepdims=True
                    )


def weigh_kernel(orders, me_ref, n_ref, dq_ref, dk_ref, dv_ref, wq_ref, wk_ref, wv_ref, dw_ref,
                 sum_ref, vec_ref, *refs):
    outs, stacks = refs[:-1], refs[-1]
    gain_ref = outs[-1]
    local = dq_ref.shape[1]
    step = pl.program_id(0)

    @pl.when(step == 0)
    def _():
        stacks[: 3 * local] = jnp.zeros((3 * local, stacks.shape[1]), F32)
        stacks[3 * local :] = dw_ref[...]

    for which, grad in enumerate((dq_ref, dk_ref, dv_ref)):
        stacks[which * local : (which + 1) * local] += lax.dot_general(
            grad[...], n_ref[...], (((0,), (0,)), ((), ())), preferred_element_type=F32
        )

    @pl.when(step == pl.num_programs(0) - 1)
    def _():
        gain = jnp.zeros(vec_ref[0:1].shape, F32)
        shift = gain
        for which, w_ref in enumerate((wq_ref, wk_ref, wv_ref)):
            weights = w_ref[...].astype(F32)
            own = stacks[which * local : (which + 1) * local]
            gain += jnp.sum(weights * own, axis=0, keepdims=True)
            shift += jnp.dot(
                sum_ref[which : which + 1],
                weights,
                precision=lax.Precision.HIGHEST,
                preferred_element_type=F32,
            )
        gain_ref[0:1] = (gain - vec_ref[1:2] * shift) / vec_ref[0:1]
        gain_ref[1:2] = shift
        if orders is None:
            outs[0][...] = stacks[: 2 * local].astype(LOW)
            outs[1][...] = stacks[2 * local :].astype(LOW)
            return
        for stack, order in enumerate(orders):
            size = 2 * local // len(order)
            for spot, slot in enumerate(order):
                which, at = divmod(spot, len(order) // 2)
                start = stack * 2 * local + jnp.bitwise_xor(me_ref[0], slot) * size
                piece = stacks[pl.ds(pl.multiple_of(start, size), size)]
                outs[2 * stack + which][at * size : (at + 1) * size] = piece.astype(LOW)


def outer_kernel(order, me_ref, left_ref, right_ref, keep_ref, send_ref, total):
    step = pl.program_id(0)

    @pl.when(step == 0)
    def _():
        total[...] = jnp.zeros_like(total)

    total[...] += lax.dot_general(
        left_ref[...], right_ref[...], (((0,), (0,)), ((), ())), preferred_element_type=F32
    )

    @pl.when(step == pl.num_programs(0) - 1)
    def _():
        size = total.shape[0] // len(order)
        for spot, slot in enumerate(order):
            which, at = divmod(spot, len(order) // 2)
            start = jnp.bitwise_xor(me_ref[0], slot) * size
            piece = total[pl.ds(pl.multiple_of(start, size), size)].astype(LOW)
            (keep_ref, send_ref)[which][at * size : (at + 1) * size] = piece


def settle_kernel(orders, me_ref, *refs):
    outs = refs[2 * len(orders) :]
    sides = len(outs) // len(orders)
    for stack, order in enumerate(orders):
        halves = refs[2 * stack : 2 * stack + 2]
        size = 2 * halves[0].shape[0] // len(order)
        per = len(order) // sides
        for spot, slot in enumerate(order):
            which, at = divmod(spot, len(order) // 2)
            value = halves[which][at * size : (at + 1) * size].astype(F32)
            place_at = jnp.bitwise_xor(me_ref[0], slot)
            start = pl.multiple_of(lax.rem(place_at, per) * size, size)
            for side in range(sides):

                @pl.when(lax.div(place_at, per) == side)
                def _():
                    outs[sides * stack + side][pl.ds(start, size)] = value


def spread_kernel(dq_ref, dk_ref, dv_ref, wq_ref, wk_ref, wv_ref, *outs):
    total = sum(
        jnp.dot(grad[...], weight[...], preferred_element_type=F32)
        for grad, weight in ((dq_ref, wq_ref), (dk_ref, wk_ref), (dv_ref, wv_ref))
    ).astype(LOW)
    size = outs[0].shape[0]
    slots = total.shape[0] // size
    step = pl.program_id(0)
    for turn in range(len(outs) // slots):

        @pl.when(step == turn)
        def _():
            for at in range(slots):
                outs[turn * slots + at][...] = total[at * size : (at + 1) * size]


def last_kernel(aliased, x_ref, d0_ref, d1_ref, d2_ref, h_ref, vec_ref, *refs):
    out_ref = refs[aliased]
    grad = d0_ref[...].astype(F32) + d1_ref[...].astype(F32) + d2_ref[...].astype(F32)
    unit, scaler = norm(x_ref[...].astype(F32))
    out_ref[...] = (h_ref[...] + norm_back(grad, unit, scaler, vec_ref[0:1])).astype(LOW)


def output_kernel(ha_ref, hb_ref, vec_ref, *refs):
    out_ref = refs[-1]
    size = ha_ref.shape[0]
    share = out_ref.shape[0]
    for part, h_ref in enumerate((ha_ref, hb_ref)):
        mlp = sum(ref[part].astype(F32) for ref in refs[:-1])
        value = (h_ref[...] + mlp + vec_ref[6:7]).astype(LOW)
        count = min(size, share - part * size)
        out_ref[part * size : part * size + count] = value[:count]


def pair(value, axis, step):
    size = lax.axis_size(axis)
    return lax.ppermute(value, axis, [(i, i ^ step) for i in range(size)])


def sum_over(value, axis):
    size = lax.axis_size(axis)
    if size & (size - 1):
        return lax.psum(value, axis)
    step = 1
    while step < size:
        value = value + pair(value, axis, step)
        step *= 2
    return value


def exchange_order(bits):
    order = [0]
    for bit in reversed(bits):
        order = order + [slot | bit for slot in order]
    return order


def halve(parts, axis, bit):
    keep, send = parts
    return tuple(jnp.split(keep + pair(send, axis, bit), 2))


def on_device(
    features, cotangent, w_query, bias_query, w_key, w_value, bias_value, w_out, bias_out,
    norm1_gain, norm1_bias, norm2_gain, norm2_bias, w_fc1, bias_fc1, w_fc2, bias_fc2,
):
    _, share, width = features.shape
    local = w_query.shape[1]
    heads = local // HEAD_DIM
    hidden = w_fc1.shape[1]
    group = lax.axis_size("tensor")
    clips = lax.axis_size("dp")
    rows = -(-share // LANES) * LANES
    size = rows // 2
    frames = group * rows
    part_rows = group * size
    slots = 2
    block = slots * size
    steps = group // slots
    shape = jax.ShapeDtypeStruct
    halves = range(2)
    count = lambda half: min(size, share - half * size)

    x_own, g_own = features[0], cotangent[0]
    x_all = gather(x_own)
    wo_all = gather(after(w_out, x_all[2]))
    g_all = gather(after(g_own, x_all[2]))
    vectors, biases = pl.pallas_call(
        stack_kernel,
        out_shape=[shape((7, width), F32), shape((3, local), F32)],
        compiler_params=params(),
        cost_estimate=cost(0, 12 * width * 8),
        name="stack",
    )(
        norm1_gain, norm1_bias, bias_out, norm2_gain, norm2_bias, bias_fc1, bias_fc2,
        bias_query, bias_value,
    )
    turned = [w_query.T, w_key.T, w_value.T]

    slot_spec = whole((size, width))
    turned_spec = whole((local, width))
    any_spec = pl.BlockSpec(memory_space=pl.ANY)
    at_half = lambda half, n: pl.BlockSpec((block, n), lambda i: (half * steps + i, 0))
    own_half = lambda half: pl.BlockSpec((size, width), lambda *_: (half, 0))
    head_half = lambda half: pl.BlockSpec((heads, block, LANES), lambda i: (0, half * steps + i, 0))
    head_shape = shape((heads, frames, LANES), LOW)

    made = []
    for turn in range(steps):
        if turn:
            x_all = finish(x_all, made[0])
        made = pl.pallas_call(
            functools.partial(project_kernel, share, slots, len(made)),
            grid=(2,),
            in_specs=[pl.BlockSpec((size, width), lambda i: (i, 0))] * slots
            + [whole(vectors.shape), whole(biases.shape)]
            + [turned_spec] * 3
            + [any_spec] * len(made),
            out_specs=[pl.BlockSpec((block, width), lambda i, turn=turn: (i * steps + turn, 0))]
            + [
                pl.BlockSpec((heads, block, LANES), lambda i, turn=turn: (0, i * steps + turn, 0))
            ]
            * 3,
            out_shape=[shape((frames, width), LOW)] + [head_shape] * 3,
            scratch_shapes=[
                pltpu.VMEM((block, width), F32),
                pltpu.VMEM((3 * heads * LANES, width), LOW),
                pltpu.VMEM((1, 3 * heads * LANES), F32),
            ],
            input_output_aliases={slots + 5 + i: i for i in range(len(made))},
            compiler_params=params(1),
            cost_estimate=cost(2 * part_rows * width * 9 * LANES, 6_000_000),
            name="project",
        )(*x_all[turn * slots : (turn + 1) * slots], vectors, biases, *turned, *made)
    normed1, query, key, value = made

    head_whole = whole((heads, frames, LANES))
    made, packed = [], []
    for half in halves:
        made = pl.pallas_call(
            functools.partial(attend_kernel, len(made), slots),
            grid=(steps,),
            in_specs=[head_half(half), head_whole, head_whole] + [any_spec] * len(made),
            out_specs=[
                pl.BlockSpec((block // 2, 2 * local), lambda i: (i, 0)),
                at_half(half, local), at_half(half, heads * LANES), head_half(half),
            ],
            out_shape=[
                shape((part_rows // 2, 2 * local), LOW), shape((frames, local), LOW),
                shape((frames, heads * LANES), F32), head_shape,
            ],
            input_output_aliases={3 + i: 1 + i for i in range(len(made))},
            compiler_params=params(1),
            cost_estimate=cost(
                2 * heads * frames * frames * 256, 5_000_000, heads * frames * frames // 2
            ),
            name="attend",
        )(query, key, value, *made)
        packed.append(gather(made[0]))
        made = made[1:]
        if half == 0:
            g_all = finish(g_all, made[0])
            wo_all = finish(wo_all, made[0])
    mixed, mixed_full, query_back = made
    packed[0] = finish(packed[0], mixed)

    low_rows = shape((frames, hidden), LOW)
    made, hidden1, fc1_bias_grad, normed2_parts = [], [], 0.0, []
    for half in halves:
        if half:
            packed[half] = finish(packed[half], made[0])
        sources = packed[half]
        packed_specs, packed_args = [], []
        for source in range(group):
            for at in range(slots):
                packed_args.append(sources[source])
                packed_specs.append(
                    pl.BlockSpec(
                        (size // 2, 2 * local),
                        lambda i, source=source, at=at: ((i * slots + at) ^ source, 0),
                    )
                )
        made = pl.pallas_call(
            functools.partial(feed_kernel, half, share, group, len(made)),
            grid=(steps,),
            in_specs=[own_half(half)] * group
            + packed_specs
            + [whole((local, width))] * group
            + [own_half(half)] * group
            + [whole(vectors.shape), whole((width, hidden)), whole((hidden, width))]
            + [any_spec] * len(made),
            out_specs=[slot_spec]
            + [at_half(half, n) for n in (width, hidden, hidden, width)]
            + [whole((1, hidden))]
            + [slot_spec] * group,
            out_shape=[
                shape((size, width), F32), shape((frames, width), LOW), low_rows, low_rows,
                shape((frames, width), LOW), shape((1, hidden), F32),
            ]
            + [shape((size, width), LOW)] * group,
            scratch_shapes=[pltpu.VMEM((block, width), LOW)] * 2,
            input_output_aliases={5 * group + 3 + i: 1 + i for i in range(len(made))},
            compiler_params=params(1),
            cost_estimate=cost(4 * frames * width * hidden, 12_000_000, frames * hidden // 2),
            name="feed",
        )(*x_all, *packed_args, *wo_all, *g_all, vectors, w_fc1, w_fc2, *made)
        hidden1.append(made[0])
        fc1_bias_grad = fc1_bias_grad + made[5]
        normed2_parts.append(made[6:])
        made = made[1:5]
    normed2, active, pre_low, cot_rows = made

    hidden1_grad, sums2, hidden1_rows = [], 0.0, []
    far = normed2_parts[1][2] + swap(normed2_parts[1][3], CORE)
    all_terms = [
        scatter_direct(normed2_parts[0]),
        [normed2_parts[1][0], swap(normed2_parts[1][1], CORE), swap(far, CHIP)],
    ]
    for half in halves:
        terms = all_terms[half]
        grad, low, sums = pl.pallas_call(
            functools.partial(middle_kernel, count(half)),
            grid=(1,),
            in_specs=[slot_spec, own_half(half), whole(vectors.shape)] + [slot_spec] * len(terms),
            out_specs=[slot_spec, slot_spec, whole((4, width))],
            out_shape=[
                shape((size, width), F32), shape((size, width), LOW), shape((4, width), F32),
            ],
            compiler_params=params(1),
            cost_estimate=cost(20 * size * width, 16 * size * width),
            name="middle",
        )(hidden1[half], g_own, vectors, *terms)
        hidden1_grad.append(grad)
        sums2 = sums2 + sums
        hidden1_rows.append(gather(low if half else after(low, far)))

    tn = lambda left, right: lax.dot_general(
        left, right, (((0,), (0,)), ((), ())), preferred_element_type=F32
    )
    me = lax.axis_index("dp").astype(jnp.int32).reshape(1)
    me_spec = pl.BlockSpec(memory_space=pltpu.SMEM)
    bits = ((1, 2, 4), (2, 1, 4)) if clips == 8 else None
    orders = [exchange_order(order) for order in bits] if bits else None
    hidden1_rows[0] = finish(hidden1_rows[0])
    hidden1_rows[1].append(swap(hidden1_rows[1][0], CORE | CHIP))
    if bits:
        fc = []
        active, normed2 = after(active, hidden1_rows[0][0]), after(normed2, hidden1_rows[0][0])
        for index, (left, right) in enumerate(((active, cot_rows), (normed2, pre_low))):
            if index:
                left = after(left, fc[0][1])
            fc.append(
                pl.pallas_call(
                    functools.partial(outer_kernel, orders[index]),
                    grid=(2,),
                    in_specs=[me_spec]
                    + [
                        pl.BlockSpec((part_rows, part.shape[1]), lambda i: (i, 0))
                        for part in (left, right)
                    ],
                    out_specs=[whole((left.shape[1] // 2, right.shape[1]))] * 2,
                    out_shape=[shape((left.shape[1] // 2, right.shape[1]), LOW)] * 2,
                    scratch_shapes=[pltpu.VMEM((left.shape[1], right.shape[1]), F32)],
                    compiler_params=params(1),
                    cost_estimate=cost(2 * frames * width * hidden, 8_000_000),
                    name="outer",
                )(me, left, right)
            )
        fc[0] = halve(fc[0], "dp", bits[0][0])
        hidden1_rows[0][0] = after(hidden1_rows[0][0], fc[0][1], fc[1][1])
    else:
        fc_own = (tn(active, cot_rows).astype(LOW), tn(normed2, pre_low).astype(LOW))
        fc2_grad, fc1_grad = [total.astype(F32) for total in lax.psum(fc_own, "dp")]
    mlp_part = jnp.dot(active, w_fc2, preferred_element_type=F32).astype(LOW)
    mlp_part = mlp_part.reshape(2, group, size, width)
    mlp = [mlp_part[:, j] for j in range(group)]
    hidden1_rows[0][0] = after(hidden1_rows[0][0], *mlp)
    mlp = scatter_direct([after(part, hidden1_rows[1][3]) for part in mlp])
    layer_out = pl.pallas_call(
        output_kernel,
        out_shape=shape((share, width), LOW),
        compiler_params=params(),
        cost_estimate=cost(8 * rows * width, 12 * rows * width),
        name="output",
    )(*hidden1, vectors, *mlp)

    back = 256
    turns = part_rows // back
    line = shape((frames, local), LOW)
    state = []
    sums_shape = [shape((heads, frames, LANES), F32)] * 2
    side_shape = [shape((local, width), F32), shape((3, local), F32)]
    side_spec = [turned_spec, whole((3, local))]
    kt_spec = whole((heads, HEAD_DIM, frames))
    for half in halves:
        first = half == 0
        if not first:
            if bits:
                fc[0] = halve(fc[0], "dp", bits[0][1])
                fc[1] = halve(fc[1], "dp", bits[1][0])
                hidden1_rows[1][0] = after(hidden1_rows[1][0], fc[0][1], fc[1][1])
        by_block = lambda n, half=half: pl.BlockSpec((back, n), lambda i: (half * turns + i, 0))
        made = pl.pallas_call(
            functools.partial(attend_back_kernel, group, first),
            grid=(turns,),
            in_specs=[slot_spec] * group
            + [
                by_block(local), by_block(heads * LANES),
                pl.BlockSpec((heads, back, LANES), lambda i, half=half: (0, half * turns + i, 0)),
                head_whole, head_whole, turned_spec,
            ]
            + ([] if first else [head_whole] * 2 + side_spec + [kt_spec, any_spec]),
            out_specs=[by_block(local)]
            + ([head_whole] * 2 if first else [whole((frames, local))] * 2)
            + side_spec
            + ([kt_spec] if first else []),
            out_shape=[line]
            + (sums_shape if first else [line, line])
            + side_shape
            + ([shape((heads, HEAD_DIM, frames), LOW)] if first else []),
            scratch_shapes=[
                pltpu.VMEM((part_rows, width), LOW), pltpu.VMEM((heads * LANES, width), LOW),
            ]
            + ([] if first else [pltpu.VMEM((heads, frames, LANES), F32)] * 2),
            input_output_aliases={} if first else {group + 11: 0},
            compiler_params=params(1),
            cost_estimate=cost(
                5 * heads * frames * frames * 256, 9_000_000, heads * frames * frames // 2
            ),
            name="attend_back",
        )(*hidden1_rows[half], mixed, mixed_full, query_back, key, value, w_out, *state)
        state = [*made[1:], made[0]]
    query_grad, key_grad, value_grad, w_out_grad, sums0 = made

    w_out_grad = after(w_out_grad, *mlp[1:3])
    if bits:
        fc[0] = [fc[0][0] + pair(fc[0][1], "dp", bits[0][2])]
        fc[1] = halve(fc[1], "dp", bits[1][1])
        w_out_grad = after(w_out_grad, fc[0][0], fc[1][1])
    stack_rows = [local] * 4 if bits else [2 * local] * 2
    block_rows = lambda n: pl.BlockSpec((block, n), lambda i: (i, 0))
    *stacks, sums1 = pl.pallas_call(
        functools.partial(weigh_kernel, orders),
        grid=(2 * steps,),
        in_specs=[me_spec, block_rows(width)]
        + [block_rows(local)] * 3
        + [turned_spec] * 4
        + [whole((3, local)), whole(vectors.shape)],
        out_specs=[whole((n, width)) for n in stack_rows] + [whole((2, width))],
        out_shape=[shape((n, width), LOW) for n in stack_rows] + [shape((2, width), F32)],
        scratch_shapes=[pltpu.VMEM((4 * local, width), F32)],
        compiler_params=params(1),
        cost_estimate=cost(2 * frames * width * 3 * local, 8_000_000),
        name="weigh",
    )(me, normed1, query_grad, key_grad, value_grad, *turned, w_out_grad, sums0, vectors)
    normed1_parts = pl.pallas_call(
        spread_kernel,
        grid=(2 * steps,),
        in_specs=[block_rows(local)] * 3 + [turned_spec] * 3,
        out_specs=[slot_spec] * (2 * group),
        out_shape=[shape((size, width), LOW)] * (2 * group),
        compiler_params=params(1),
        cost_estimate=cost(2 * frames * width * 3 * local, 6_000_000),
        name="spread",
    )(after(query_grad, stacks[0], mlp[3]), key_grad, value_grad, *turned)
    small = jnp.concatenate(
        [sums0[0], sums0[2], fc1_bias_grad[0], sums1.reshape(-1), sums2.reshape(-1)]
    )
    parts = [normed1_parts[half * group : (half + 1) * group] for half in halves]
    count_own = 2 * local + hidden

    def settle(ends, order, count, size):
        return pl.pallas_call(
            functools.partial(settle_kernel, order),
            in_specs=[me_spec] + [pl.BlockSpec(memory_space=pltpu.VMEM)] * len(ends),
            out_shape=[shape((size, width), F32)] * count,
            compiler_params=params(),
            cost_estimate=cost(0, 6 * count * size * width),
            name="settle",
        )(me, *ends)

    hop = lambda value, bit: pair(value, "dp", bit)
    side = lambda index, turn: bits[index][turn]
    join = lambda *values: jnp.concatenate(values)
    together = lambda *values: lax.optimization_barrier(values)
    if bits:
        q = [(stacks[0], stacks[1]), (stacks[2], stacks[3])]
        f0 = fc[0][0]
        got = together(
            hop(q[0][1], side(0, 0)), hop(q[1][1], side(1, 0)), hop(f0, side(0, 2)),
            hop(fc[1][1], side(1, 2)), hop(small, 1), parts[0][0],
        )
        q = [tuple(jnp.split(q[i][0] + got[i], 2)) for i in range(2)]
        f0, f1, small = join(f0, got[2]), fc[1][0] + got[3], small + got[4]
        got = together(
            hop(q[0][1], side(0, 1)), hop(q[1][1], side(1, 1)), hop(f0, side(0, 1)),
            hop(f1, side(1, 2)), hop(small, 2),
            *[swap(parts[half][j], CORE) for half in halves for j in (3, 1)],
        )
        q = [tuple(jnp.split(q[i][0] + got[i], 2)) for i in range(2)]
        f0, f1, small = join(f0, got[2]), join(f1, got[3]), small + got[4]
        beside = [got[6], got[8]]
        far = [parts[half][2] + got[5 + 2 * half] for half in halves]
        f0_last = hop(f0, side(0, 0))
        f1_next = hop(f1, side(1, 1))
        far = [swap(value, CHIP) for value in far]
        got = together(hop(q[0][1], side(0, 2)), hop(q[1][1], side(1, 2)), hop(small, 4))
        q = [q[i][0] + got[i] for i in range(2)]
        small = small + got[2]
        mine, shared = small[:count_own], small[count_own:]
        got = together(
            hop(q[0], side(0, 2)), hop(q[1], side(1, 2)), f1_next, swap(shared, CORE), f0_last
        )
        q = [join(q[i], got[i]) for i in range(2)]
        f1, shared, f0_last = join(f1, got[2]), shared + got[3], got[4]
        f1_last = hop(f1, side(1, 0))
        got = together(
            hop(q[0], side(0, 1)), hop(q[1], side(1, 1)), swap(shared, CHIP), *far
        )
        q = [join(q[i], got[i]) for i in range(2)]
        shared = shared + got[2]
        far = got[3:]
        ends = [q[0], hop(q[0], side(0, 0)), q[1], hop(q[1], side(1, 0))]
        (fc2_grad,) = settle([f0, f0_last], orders[:1], 1, hidden)
        (fc1_grad,) = settle([f1, f1_last], orders[1:], 1, hidden)
        grads = settle(ends, orders, 4, local)
    else:
        grads = jnp.concatenate(lax.psum(tuple(stacks), "dp")).astype(F32)
        grads = jnp.split(grads, 4)
        small = sum_over(small, "dp")
        mine, shared = small[:count_own], sum_over(small[count_own:], "tensor")
        beside = [swap(part[1], CORE) for part in parts]
        far = [swap(part[2] + swap(part[3], CORE), CHIP) for part in parts]
    shared = shared.reshape(6, width)

    features_grad = []
    for half in halves:
        features_grad = [
            pl.pallas_call(
                functools.partial(last_kernel, len(features_grad)),
                grid=(1,),
                in_specs=[own_half(half)]
                + [slot_spec] * 4
                + [whole(vectors.shape)]
                + [any_spec] * len(features_grad),
                out_specs=own_half(half),
                out_shape=shape((share, width), LOW),
                input_output_aliases={6: 0} if features_grad else {},
                compiler_params=params(1),
                cost_estimate=cost(20 * size * width, 14 * size * width),
                name="last",
            )(
                x_own,
                parts[half][0],
                beside[half],
                far[half],
                hidden1_grad[half],
                vectors,
                *features_grad,
            )
        ]
    return (
        layer_out[None],
        features_grad[0][None],
        grads[0].T,
        mine[:local],
        grads[1].T,
        grads[2].T,
        mine[local : 2 * local],
        grads[3],
        shared[4],
        shared[0],
        shared[1],
        shared[2],
        shared[3],
        fc1_grad,
        mine[2 * local :],
        fc2_grad,
        shared[5],
    )


def solution(mesh):
    rows = P("dp", "tensor", None)
    columns, lines, vector, same = P(None, "tensor"), P("tensor", None), P("tensor"), P()
    in_specs = (
        rows, rows, columns, vector, columns, columns, vector, lines, same,
        same, same, same, same, columns, vector, lines, same,
    )
    out_specs = (
        rows, rows, columns, vector, columns, columns, vector, lines, same,
        same, same, same, same, columns, vector, lines, same,
    )
    return jax.shard_map(
        on_device, mesh=mesh, in_specs=in_specs, out_specs=out_specs, check_vma=False
    )
```

```python
import functools

import jax
import jax.numpy as jnp
from jax import lax
from jax.experimental import pallas as pl
from jax.experimental.pallas import tpu as pltpu
from jax.sharding import PartitionSpec as P

HEAD_DIM = 64
LANES = 128
F32 = jnp.float32
LOW = jnp.bfloat16
MASK = -1e30
CORE, CHIP = 1, 2
ROOM = 56 * 1024 * 1024
NT = (((1,), (1,)), ((), ()))


def params(steps=0):
    semantics = ("arbitrary",) * steps if steps else None
    return pltpu.CompilerParams(vmem_limit_bytes=ROOM, dimension_semantics=semantics)


def cost(flops, moved, exps=0):
    return pl.CostEstimate(flops=flops, bytes_accessed=moved, transcendentals=exps)


def whole(shape):
    return pl.BlockSpec(shape, lambda *_: (0,) * len(shape))


def swap(value, partner):
    size = lax.axis_size("tensor")
    return lax.ppermute(value, "tensor", [(i, i ^ partner) for i in range(size)])


def after(value, *others):
    return lax.optimization_barrier((value, *others))[0]


def gather(own):
    return [own, swap(own, CORE), swap(own, CHIP)]


def finish(parts, *others):
    across = after(parts[2], *others) if others else parts[2]
    return [*parts[:2], across, swap(across, CORE)]


def scatter_direct(parts):
    return [parts[0]] + [swap(parts[j], j) for j in range(1, len(parts))]


def thirds(value):
    high = value.astype(LOW)
    rest = value - high.astype(F32)
    mid = rest.astype(LOW)
    return high, mid, (rest - mid.astype(F32)).astype(LOW)


def place(base, lane, first, pieces):
    for offset, piece in enumerate(pieces):
        base = jnp.where(lane == first + offset, piece, base)
    return base


def norm(values):
    mean = jnp.mean(values, axis=-1, keepdims=True)
    centred = values - mean
    spread = jnp.mean(centred * centred, axis=-1, keepdims=True)
    scaler = lax.rsqrt(spread + 1e-05)
    return centred * scaler, scaler


def norm_back(grad, unit, scaler, gain):
    scaled = grad * gain
    return scaler * (
        scaled
        - jnp.mean(scaled, axis=-1, keepdims=True)
        - unit * jnp.mean(scaled * unit, axis=-1, keepdims=True)
    )


def present(value, count):
    if count == value.shape[0]:
        return value
    row = lax.broadcasted_iota(jnp.int32, value.shape, 0)
    return jnp.where(row < count, value.astype(F32), 0.0).astype(value.dtype)


def pick(step, refs, rows, count):
    size = refs[0].shape[0]
    slots = rows.shape[0] // size
    for turn in range(len(refs) // slots):

        @pl.when(step == turn)
        def _():
            for at in range(slots):
                block = present(refs[turn * slots + at][...], count)
                rows[at * size : (at + 1) * size] = block


def stack_kernel(*refs):
    vec_ref, bias_ref = refs[-2:]
    for index, ref in enumerate(refs[:7]):
        vec_ref[index : index + 1] = ref[...].astype(F32).reshape(1, -1)
    bias_ref[...] = jnp.zeros_like(bias_ref)
    for index, ref in ((0, refs[7]), (2, refs[8])):
        bias_ref[index : index + 1] = ref[...].astype(F32).reshape(1, -1)


def project_kernel(share, slots, aliased, *refs):
    x_refs = refs[:slots]
    vec_ref, bias_ref, wq_ref, wk_ref, wv_ref = refs[slots : slots + 5]
    n_ref, q_ref, k_ref, v_ref, rows, w_tiles, b_tiles = refs[slots + 5 + aliased :]
    half = pl.program_id(0)
    heads = q_ref.shape[0]
    size = x_refs[0].shape[0]

    @pl.when(half == 0)
    def _():
        w_tiles[...] = jnp.zeros_like(w_tiles)
        b_tiles[...] = jnp.zeros_like(b_tiles)
        spot = lax.broadcasted_iota(jnp.int32, (1, LANES), 1) - HEAD_DIM
        ones = (
            jnp.where(spot == 0, HEAD_DIM**0.5, 0.0),
            jnp.where((spot >= 1) & (spot <= 3), 1.0, 0.0),
            jnp.where((spot >= 0) & (spot <= 2), 1.0, 0.0),
        )
        for which, w_ref in enumerate((wq_ref, wk_ref, wv_ref)):
            for head in range(heads):
                at = (which * heads + head) * LANES
                own = slice(head * HEAD_DIM, (head + 1) * HEAD_DIM)
                w_tiles[at : at + HEAD_DIM] = w_ref[own]
                b_tiles[:, at : at + LANES] = ones[which]
                b_tiles[:, at : at + HEAD_DIM] = bias_ref[which : which + 1, own]

    row = lax.broadcasted_iota(jnp.int32, (size, rows.shape[1]), 0) + half * size
    for at in range(slots):
        block = jnp.where(row < share, x_refs[at][...].astype(F32), 0.0)
        rows[at * size : (at + 1) * size] = block
    unit, _ = norm(rows[...])
    normed = (unit * vec_ref[0:1] + vec_ref[1:2]).astype(LOW)
    n_ref[...] = normed
    out = lax.dot_general(normed, w_tiles[...], NT, preferred_element_type=F32) + b_tiles[...]
    row = lax.broadcasted_iota(jnp.int32, (out.shape[0], LANES), 0)
    lane = lax.broadcasted_iota(jnp.int32, (out.shape[0], LANES), 1)
    absent = (lax.rem(row, size) + half * size >= share) & (lane == HEAD_DIM)
    scale = HEAD_DIM ** (-0.5)
    for head in range(heads):
        part = lambda which: out[:, (which * heads + head) * LANES :][:, :LANES]
        q_ref[head] = (part(0).astype(LOW).astype(F32) * scale).astype(LOW)
        k_ref[head] = jnp.where(absent, MASK, part(1)).astype(LOW)
        v_ref[head] = part(2).astype(LOW)


def attend_kernel(aliased, slots, q_ref, k_ref, v_ref, *refs):
    o_ref, m_ref, full_ref, q_out = refs[aliased:]
    heads, block, _ = q_ref.shape
    quarter = block // slots // 2
    lane = lax.broadcasted_iota(jnp.int32, (block, LANES), 1)
    for head in range(heads):
        query = q_ref[head]
        scores = lax.dot_general(query, k_ref[head], NT, preferred_element_type=F32)
        top = jnp.max(scores, axis=-1, keepdims=True)
        weights = jnp.exp(scores - top).astype(LOW)
        out = jnp.dot(weights, v_ref[head], preferred_element_type=F32)
        total = out[:, HEAD_DIM : HEAD_DIM + 1]
        out = out / total
        full_ref[:, head * LANES : (head + 1) * LANES] = out
        low = out[:, :HEAD_DIM].astype(LOW)
        m_ref[:, head * HEAD_DIM : (head + 1) * HEAD_DIM] = low
        for part in range(2 * slots):
            at = ((part % 2) * heads + head) * HEAD_DIM
            o_ref[part // 2 * quarter : (part // 2 + 1) * quarter, at : at + HEAD_DIM] = low[
                part * quarter : (part + 1) * quarter
            ]
        logsum = top + jnp.log(total)
        q_out[head] = place(query, lane, HEAD_DIM + 1, thirds(-logsum))


def chunked(rows, body):
    def step(index, _):
        body(pl.ds(pl.multiple_of(index * 16, 16), 16))

    lax.fori_loop(0, rows // 16, step, None)


def feed_kernel(half, share, group, aliased, *refs):
    x_refs, m_refs, wo_refs = refs[:group], refs[group : 3 * group], refs[3 * group : 4 * group]
    g_refs = refs[4 * group : 5 * group]
    vec_ref, w1_ref, w2_ref = refs[5 * group : 5 * group + 3]
    outs = refs[5 * group + 3 + aliased :]
    h_ref, n_ref, a_ref, p_ref, c_ref, db_ref = outs[:6]
    d_refs = outs[6 : 6 + group]
    rows, mixed, wo_all, first, second, db_sum = outs[6 + group :]
    step = pl.program_id(0)
    size = x_refs[0].shape[0]
    block, width = rows.shape
    slots = block // size
    quarter = size // 2
    local = wo_refs[0].shape[0]
    hidden = w1_ref.shape[1]

    @pl.when(step == 0)
    def _():
        for source in range(group):
            wo_all[source * local : (source + 1) * local] = wo_refs[source][...]
        db_sum[...] = jnp.zeros_like(db_sum)

    count = min(size, share - half * size)
    pick(step, x_refs, rows, count)
    pick(step, g_refs, c_ref, count)
    for source in range(group):
        for at in range(slots):
            packed = m_refs[source * slots + at][...]
            for part in range(2):
                start = at * size + part * quarter
                mixed[start : start + quarter, source * local : (source + 1) * local] = packed[
                    :, part * local : (part + 1) * local
                ]
    first[...] = jnp.dot(mixed[...], wo_all[...], preferred_element_type=F32)

    def norm_rows(at):
        value = rows[at].astype(F32) + first[at] + vec_ref[2:3]
        first[at] = value
        unit, _ = norm(value)
        n_ref[at] = (unit * vec_ref[3:4] + vec_ref[4:5]).astype(LOW)

    chunked(block, norm_rows)

    @pl.when(step == 0)
    def _():
        h_ref[...] = first[:size]

    first[...] = jnp.dot(n_ref[...], w1_ref[...], preferred_element_type=F32)
    second[...] = lax.dot_general(c_ref[...], w2_ref[...], NT, preferred_element_type=F32)

    def gelu_rows(at):
        for start in range(0, hidden, 3 * LANES):
            part = slice(start, start + 3 * LANES)
            pre = first[at, part] + vec_ref[5:6, part]
            bell = jnp.exp(-0.5 * pre * pre)
            t = 1.0 / (1.0 + (0.3275911 * 0.5**0.5) * jnp.abs(pre))
            poly = 0.7107068705 + t * (-0.7265760135 + t * 0.5307027145)
            tail = t * (0.127414796 + t * (-0.142248368 + t * poly)) * bell
            gate = jnp.where(pre >= 0, 1.0 - tail, tail)
            a_ref[at, part] = (pre * gate).astype(LOW)
            grad = second[at, part] * (gate + pre * bell * 0.3989422804014327)
            db_sum[:, part] += grad
            p_ref[at, part] = grad.astype(LOW)

    chunked(block, gelu_rows)
    back = lax.dot_general(p_ref[...], w1_ref[...], NT, preferred_element_type=F32).astype(LOW)
    for turn in range(group // slots):

        @pl.when(step == turn)
        def _():
            for at in range(slots):
                d_refs[turn * slots + at][...] = back[at * size : (at + 1) * size]

    @pl.when(step == pl.num_programs(0) - 1)
    def _():
        db_ref[...] = jnp.sum(db_sum[...], axis=0, keepdims=True)


def middle_kernel(count, h_ref, g_ref, vec_ref, *refs):
    out_ref, low_ref, sums_ref = refs[-3:]
    grad = sum(ref[...].astype(F32) for ref in refs[:-3])
    unit, scaler = norm(h_ref[...])
    cot = present(g_ref[...], count).astype(F32)
    hidden_grad = cot + norm_back(grad, unit, scaler, vec_ref[3:4])
    out_ref[...] = hidden_grad
    low_ref[...] = hidden_grad.astype(LOW)
    add = lambda value: jnp.sum(value, axis=0, keepdims=True)
    sums_ref[...] = jnp.concatenate(
        [add(grad * unit), add(grad), add(hidden_grad), add(cot)], axis=0
    )


def weigh(orders, me_ref, n_ref, grads, weights, dw_ref, sum_ref, vec_ref, gain_ref, outs, stacks):
    local = dw_ref.shape[0]
    gain = jnp.zeros(vec_ref[0:1].shape, F32)
    shift = gain
    for which, (grad, w_ref) in enumerate(zip(grads, weights)):
        own = lax.dot_general(
            grad[...], n_ref[...], (((0,), (0,)), ((), ())), preferred_element_type=F32
        )
        stacks[which * local : (which + 1) * local] = own
        weight = w_ref[...].astype(F32)
        gain += jnp.sum(weight * own, axis=0, keepdims=True)
        shift += jnp.dot(
            sum_ref[which : which + 1],
            weight,
            precision=lax.Precision.HIGHEST,
            preferred_element_type=F32,
        )
    stacks[3 * local :] = dw_ref[...]
    gain_ref[0:1] = (gain - vec_ref[1:2] * shift) / vec_ref[0:1]
    gain_ref[1:2] = shift
    if orders is None:
        outs[0][...] = stacks[: 2 * local].astype(LOW)
        outs[1][...] = stacks[2 * local :].astype(LOW)
        return
    for stack, order in enumerate(orders):
        size = 2 * local // len(order)
        for spot, slot in enumerate(order):
            which, at = divmod(spot, len(order) // 2)
            start = stack * 2 * local + jnp.bitwise_xor(me_ref[0], slot) * size
            piece = stacks[pl.ds(pl.multiple_of(start, size), size)]
            outs[2 * stack + which][at * size : (at + 1) * size] = piece.astype(LOW)


def attend_back_kernel(parts, first, orders, *refs):
    h_refs = refs[:parts]
    m_ref, full_ref, q_ref, k_ref, v_ref, wo_ref = refs[parts : parts + 6]
    if first:
        dq_ref, dk_sum, dv_sum, dw_ref, sum_ref, kt_ref = refs[parts + 6 : parts + 12]
        rows, wo_tiles = refs[parts + 12 :]
    else:
        dk_old, dv_old, dw_old, sum_old, kt_ref, dq_old = refs[parts + 6 : parts + 12]
        me_ref, n_ref, wq_ref, wk_ref, wv_ref, vec_ref = refs[parts + 12 : parts + 18]
        dq_ref, dk_ref, dv_ref, sum_ref, gain_ref = refs[parts + 18 : parts + 23]
        outs = refs[parts + 23 : -6]
        rows, wo_tiles, dk_sum, dv_sum, dw_ref, stacks = refs[-6:]
    step = pl.program_id(0)
    heads, block, _ = q_ref.shape

    @pl.when(step == 0)
    def _():
        size = h_refs[0].shape[0]
        for part in range(parts):
            rows[part * size : (part + 1) * size] = h_refs[part][...]
        wo_tiles[...] = jnp.zeros_like(wo_tiles)
        for head in range(heads):
            wo_tiles[head * LANES : head * LANES + HEAD_DIM] = wo_ref[
                head * HEAD_DIM : (head + 1) * HEAD_DIM
            ]
        if first:
            for total in (dk_sum, dv_sum, dw_ref, sum_ref):
                total[...] = jnp.zeros_like(total)
            for head in range(heads):
                kt_ref[head] = k_ref[head].astype(F32).T[:HEAD_DIM].astype(LOW)
        else:
            olds = (dk_old, dv_old, dw_old, sum_old)
            for total, old in zip((dk_sum, dv_sum, dw_ref, sum_ref), olds):
                total[...] = old[...]
            dq_ref[: dq_old.shape[0]] = dq_old[...]

    scale = HEAD_DIM ** (-0.5)
    lane = lax.broadcasted_iota(jnp.int32, (block, LANES), 1)
    hidden_grad = rows[pl.ds(pl.multiple_of(step * block, block), block)]
    mixed_grad = lax.dot_general(
        hidden_grad, wo_tiles[...], NT, preferred_element_type=F32
    ).astype(LOW)
    dw_ref[...] += lax.dot_general(
        m_ref[...], hidden_grad, (((0,), (0,)), ((), ())), preferred_element_type=F32
    )
    for head in range(heads):
        at = head * HEAD_DIM
        tile = slice(head * LANES, (head + 1) * LANES)
        out_grad = mixed_grad[:, tile]
        delta = jnp.sum(out_grad.astype(F32) * full_ref[:, tile], axis=-1, keepdims=True)
        out_grad = place(out_grad, lane, HEAD_DIM, thirds(-delta))
        query = q_ref[head]
        scores = lax.dot_general(k_ref[head], query, NT, preferred_element_type=F32)
        probs = jnp.exp(scores)
        prob_grad = lax.dot_general(v_ref[head], out_grad, NT, preferred_element_type=F32)
        score_grad = (probs * prob_grad).astype(LOW)
        dv_sum[head] += jnp.dot(probs.astype(LOW), out_grad, preferred_element_type=F32)
        dk_sum[head] += jnp.dot(score_grad, query, preferred_element_type=F32)
        turned = jnp.dot(kt_ref[head], score_grad, preferred_element_type=F32)
        query_grad = (turned.T * scale).astype(LOW)
        if first:
            dq_ref[:, at : at + HEAD_DIM] = query_grad
        else:
            start = pl.multiple_of(dq_old.shape[0] + step * block, block)
            dq_ref[pl.ds(start, block), at : at + HEAD_DIM] = query_grad
        sum_ref[0:1, at : at + HEAD_DIM] += jnp.sum(
            query_grad.astype(F32), axis=0, keepdims=True
        )

    if not first:

        @pl.when(step == pl.num_programs(0) - 1)
        def _():
            for head in range(heads):
                at = head * HEAD_DIM
                for index, (ref, total) in enumerate(((dk_ref, dk_sum), (dv_ref, dv_sum))):
                    low = total[head][:, :HEAD_DIM].astype(LOW)
                    ref[:, at : at + HEAD_DIM] = low
                    sum_ref[index + 1 : index + 2, at : at + HEAD_DIM] = jnp.sum(
                        low.astype(F32), axis=0, keepdims=True
                    )
            weigh(
                orders, me_ref, n_ref, (dq_ref, dk_ref, dv_ref), (wq_ref, wk_ref, wv_ref), dw_ref,
                sum_ref, vec_ref, gain_ref, outs, stacks,
            )


def outer_kernel(order, me_ref, left_ref, right_ref, keep_ref, send_ref, total):
    step = pl.program_id(0)

    @pl.when(step == 0)
    def _():
        total[...] = jnp.zeros_like(total)

    total[...] += lax.dot_general(
        left_ref[...], right_ref[...], (((0,), (0,)), ((), ())), preferred_element_type=F32
    )

    @pl.when(step == pl.num_programs(0) - 1)
    def _():
        size = total.shape[0] // len(order)
        for spot, slot in enumerate(order):
            which, at = divmod(spot, len(order) // 2)
            start = jnp.bitwise_xor(me_ref[0], slot) * size
            piece = total[pl.ds(pl.multiple_of(start, size), size)].astype(LOW)
            (keep_ref, send_ref)[which][at * size : (at + 1) * size] = piece


def settle_kernel(orders, me_ref, *refs):
    outs = refs[2 * len(orders) :]
    sides = len(outs) // len(orders)
    for stack, order in enumerate(orders):
        halves = refs[2 * stack : 2 * stack + 2]
        size = 2 * halves[0].shape[0] // len(order)
        per = len(order) // sides
        for spot, slot in enumerate(order):
            which, at = divmod(spot, len(order) // 2)
            value = halves[which][at * size : (at + 1) * size].astype(F32)
            place_at = jnp.bitwise_xor(me_ref[0], slot)
            start = pl.multiple_of(lax.rem(place_at, per) * size, size)
            for side in range(sides):

                @pl.when(lax.div(place_at, per) == side)
                def _():
                    outs[sides * stack + side][pl.ds(start, size)] = value


def spread_kernel(dq_ref, dk_ref, dv_ref, wq_ref, wk_ref, wv_ref, *outs):
    total = sum(
        jnp.dot(grad[...], weight[...], preferred_element_type=F32)
        for grad, weight in ((dq_ref, wq_ref), (dk_ref, wk_ref), (dv_ref, wv_ref))
    ).astype(LOW)
    size = outs[0].shape[0]
    slots = total.shape[0] // size
    step = pl.program_id(0)
    for turn in range(len(outs) // slots):

        @pl.when(step == turn)
        def _():
            for at in range(slots):
                outs[turn * slots + at][...] = total[at * size : (at + 1) * size]


def last_kernel(aliased, x_ref, d0_ref, d1_ref, d2_ref, h_ref, vec_ref, *refs):
    out_ref = refs[aliased]
    grad = d0_ref[...].astype(F32) + d1_ref[...].astype(F32) + d2_ref[...].astype(F32)
    unit, scaler = norm(x_ref[...].astype(F32))
    out_ref[...] = (h_ref[...] + norm_back(grad, unit, scaler, vec_ref[0:1])).astype(LOW)


def output_kernel(ha_ref, hb_ref, vec_ref, *refs):
    out_ref = refs[-1]
    size = ha_ref.shape[0]
    share = out_ref.shape[0]
    for part, h_ref in enumerate((ha_ref, hb_ref)):
        mlp = sum(ref[part].astype(F32) for ref in refs[:-1])
        value = (h_ref[...] + mlp + vec_ref[6:7]).astype(LOW)
        count = min(size, share - part * size)
        out_ref[part * size : part * size + count] = value[:count]


def pair(value, axis, step):
    size = lax.axis_size(axis)
    return lax.ppermute(value, axis, [(i, i ^ step) for i in range(size)])


def sum_over(value, axis):
    size = lax.axis_size(axis)
    if size & (size - 1):
        return lax.psum(value, axis)
    step = 1
    while step < size:
        value = value + pair(value, axis, step)
        step *= 2
    return value


def exchange_order(bits):
    order = [0]
    for bit in reversed(bits):
        order = order + [slot | bit for slot in order]
    return order


def halve(parts, axis, bit):
    keep, send = parts
    return tuple(jnp.split(keep + pair(send, axis, bit), 2))


def on_device(
    features, cotangent, w_query, bias_query, w_key, w_value, bias_value, w_out, bias_out,
    norm1_gain, norm1_bias, norm2_gain, norm2_bias, w_fc1, bias_fc1, w_fc2, bias_fc2,
):
    _, share, width = features.shape
    local = w_query.shape[1]
    heads = local // HEAD_DIM
    hidden = w_fc1.shape[1]
    group = lax.axis_size("tensor")
    clips = lax.axis_size("dp")
    rows = -(-share // LANES) * LANES
    size = rows // 2
    frames = group * rows
    part_rows = group * size
    slots = 2
    block = slots * size
    steps = group // slots
    shape = jax.ShapeDtypeStruct
    halves = range(2)
    count = lambda half: min(size, share - half * size)

    x_own, g_own = features[0], cotangent[0]
    x_all = gather(x_own)
    wo_all = gather(after(w_out, x_all[2]))
    g_all = gather(after(g_own, x_all[2]))
    vectors, biases = pl.pallas_call(
        stack_kernel,
        out_shape=[shape((7, width), F32), shape((3, local), F32)],
        compiler_params=params(),
        cost_estimate=cost(0, 12 * width * 8),
        name="stack",
    )(
        norm1_gain, norm1_bias, bias_out, norm2_gain, norm2_bias, bias_fc1, bias_fc2,
        bias_query, bias_value,
    )
    turned = [w_query.T, w_key.T, w_value.T]

    slot_spec = whole((size, width))
    turned_spec = whole((local, width))
    any_spec = pl.BlockSpec(memory_space=pl.ANY)
    at_half = lambda half, n: pl.BlockSpec((block, n), lambda i: (half * steps + i, 0))
    own_half = lambda half: pl.BlockSpec((size, width), lambda *_: (half, 0))
    head_half = lambda half: pl.BlockSpec((heads, block, LANES), lambda i: (0, half * steps + i, 0))
    head_shape = shape((heads, frames, LANES), LOW)

    made = []
    for turn in range(steps):
        if turn:
            x_all = finish(x_all, made[0])
        made = pl.pallas_call(
            functools.partial(project_kernel, share, slots, len(made)),
            grid=(2,),
            in_specs=[pl.BlockSpec((size, width), lambda i: (i, 0))] * slots
            + [whole(vectors.shape), whole(biases.shape)]
            + [turned_spec] * 3
            + [any_spec] * len(made),
            out_specs=[pl.BlockSpec((block, width), lambda i, turn=turn: (i * steps + turn, 0))]
            + [
                pl.BlockSpec((heads, block, LANES), lambda i, turn=turn: (0, i * steps + turn, 0))
            ]
            * 3,
            out_shape=[shape((frames, width), LOW)] + [head_shape] * 3,
            scratch_shapes=[
                pltpu.VMEM((block, width), F32),
                pltpu.VMEM((3 * heads * LANES, width), LOW),
                pltpu.VMEM((1, 3 * heads * LANES), F32),
            ],
            input_output_aliases={slots + 5 + i: i for i in range(len(made))},
            compiler_params=params(1),
            cost_estimate=cost(2 * part_rows * width * 9 * LANES, 6_000_000),
            name="project",
        )(*x_all[turn * slots : (turn + 1) * slots], vectors, biases, *turned, *made)
    normed1, query, key, value = made

    head_whole = whole((heads, frames, LANES))
    made, packed = [], []
    for half in halves:
        made = pl.pallas_call(
            functools.partial(attend_kernel, len(made), slots),
            grid=(steps,),
            in_specs=[head_half(half), head_whole, head_whole] + [any_spec] * len(made),
            out_specs=[
                pl.BlockSpec((block // 2, 2 * local), lambda i: (i, 0)),
                at_half(half, local), at_half(half, heads * LANES), head_half(half),
            ],
            out_shape=[
                shape((part_rows // 2, 2 * local), LOW), shape((frames, local), LOW),
                shape((frames, heads * LANES), F32), head_shape,
            ],
            input_output_aliases={3 + i: 1 + i for i in range(len(made))},
            compiler_params=params(1),
            cost_estimate=cost(
                2 * heads * frames * frames * 256, 5_000_000, heads * frames * frames // 2
            ),
            name="attend",
        )(query, key, value, *made)
        packed.append(gather(made[0]))
        made = made[1:]
        if half == 0:
            g_all = finish(g_all, made[0])
            wo_all = finish(wo_all, made[0])
    mixed, mixed_full, query_back = made
    packed[0] = finish(packed[0], mixed)

    low_rows = shape((frames, hidden), LOW)
    made, hidden1, fc1_bias_grad, normed2_parts = [], [], 0.0, []
    for half in halves:
        if half:
            packed[half] = finish(packed[half], made[0])
        sources = packed[half]
        packed_specs, packed_args = [], []
        for source in range(group):
            for at in range(slots):
                packed_args.append(sources[source])
                packed_specs.append(
                    pl.BlockSpec(
                        (size // 2, 2 * local),
                        lambda i, source=source, at=at: ((i * slots + at) ^ source, 0),
                    )
                )
        made = pl.pallas_call(
            functools.partial(feed_kernel, half, share, group, len(made)),
            grid=(steps,),
            in_specs=[own_half(half)] * group
            + packed_specs
            + [whole((local, width))] * group
            + [own_half(half)] * group
            + [whole(vectors.shape), whole((width, hidden)), whole((hidden, width))]
            + [any_spec] * len(made),
            out_specs=[slot_spec]
            + [at_half(half, n) for n in (width, hidden, hidden, width)]
            + [whole((1, hidden))]
            + [slot_spec] * group,
            out_shape=[
                shape((size, width), F32), shape((frames, width), LOW), low_rows, low_rows,
                shape((frames, width), LOW), shape((1, hidden), F32),
            ]
            + [shape((size, width), LOW)] * group,
            scratch_shapes=[pltpu.VMEM((block, width), LOW)] * 2
            + [
                pltpu.VMEM((width, width), LOW),
                pltpu.VMEM((block, max(width, hidden)), F32),
                pltpu.VMEM((block, hidden), F32),
                pltpu.VMEM((16, hidden), F32),
            ],
            input_output_aliases={5 * group + 3 + i: 1 + i for i in range(len(made))},
            compiler_params=params(1),
            cost_estimate=cost(4 * frames * width * hidden, 12_000_000, frames * hidden // 2),
            name="feed",
        )(*x_all, *packed_args, *wo_all, *g_all, vectors, w_fc1, w_fc2, *made)
        hidden1.append(made[0])
        fc1_bias_grad = fc1_bias_grad + made[5]
        normed2_parts.append(made[6:])
        made = made[1:5]
    normed2, active, pre_low, cot_rows = made

    hidden1_grad, sums2, hidden1_rows = [], 0.0, []
    far = normed2_parts[1][2] + swap(normed2_parts[1][3], CORE)
    all_terms = [
        scatter_direct(normed2_parts[0]),
        [normed2_parts[1][0], swap(normed2_parts[1][1], CORE), swap(far, CHIP)],
    ]
    for half in halves:
        terms = all_terms[half]
        grad, low, sums = pl.pallas_call(
            functools.partial(middle_kernel, count(half)),
            grid=(1,),
            in_specs=[slot_spec, own_half(half), whole(vectors.shape)] + [slot_spec] * len(terms),
            out_specs=[slot_spec, slot_spec, whole((4, width))],
            out_shape=[
                shape((size, width), F32), shape((size, width), LOW), shape((4, width), F32),
            ],
            compiler_params=params(1),
            cost_estimate=cost(20 * size * width, 16 * size * width),
            name="middle",
        )(hidden1[half], g_own, vectors, *terms)
        hidden1_grad.append(grad)
        sums2 = sums2 + sums
        hidden1_rows.append(gather(low if half else after(low, far)))

    tn = lambda left, right: lax.dot_general(
        left, right, (((0,), (0,)), ((), ())), preferred_element_type=F32
    )
    me = lax.axis_index("dp").astype(jnp.int32).reshape(1)
    me_spec = pl.BlockSpec(memory_space=pltpu.SMEM)
    bits = ((1, 2, 4), (2, 1, 4)) if clips == 8 else None
    orders = [exchange_order(order) for order in bits] if bits else None
    hidden1_rows[0] = finish(hidden1_rows[0])
    hidden1_rows[1].append(swap(hidden1_rows[1][0], CORE | CHIP))
    if bits:
        fc = []
        active, normed2 = after(active, hidden1_rows[0][0]), after(normed2, hidden1_rows[0][0])
        for index, (left, right) in enumerate(((active, cot_rows), (normed2, pre_low))):
            if index:
                left = after(left, fc[0][1])
            fc.append(
                pl.pallas_call(
                    functools.partial(outer_kernel, orders[index]),
                    grid=(2,),
                    in_specs=[me_spec]
                    + [
                        pl.BlockSpec((part_rows, part.shape[1]), lambda i: (i, 0))
                        for part in (left, right)
                    ],
                    out_specs=[whole((left.shape[1] // 2, right.shape[1]))] * 2,
                    out_shape=[shape((left.shape[1] // 2, right.shape[1]), LOW)] * 2,
                    scratch_shapes=[pltpu.VMEM((left.shape[1], right.shape[1]), F32)],
                    compiler_params=params(1),
                    cost_estimate=cost(2 * frames * width * hidden, 8_000_000),
                    name="outer",
                )(me, left, right)
            )
        fc = [halve(fc[index], "dp", bits[index][0]) for index in range(2)]
        hidden1_rows[0][0] = after(hidden1_rows[0][0], fc[0][1], fc[1][1])
    else:
        fc_own = (tn(active, cot_rows).astype(LOW), tn(normed2, pre_low).astype(LOW))
        fc2_grad, fc1_grad = [total.astype(F32) for total in lax.psum(fc_own, "dp")]
    mlp_part = jnp.dot(active, w_fc2, preferred_element_type=F32).astype(LOW)
    mlp_part = mlp_part.reshape(2, group, size, width)
    mlp_far = mlp_part[:, 2] + swap(mlp_part[:, 3], CORE)
    mlp = [mlp_part[:, 0], mlp_part[:, 1], mlp_far]
    hidden1_rows[0][0] = after(hidden1_rows[0][0], *mlp)
    back = 256
    turns = part_rows // back
    line = shape((frames, local), LOW)
    head_sums = shape((heads, frames, LANES), F32)
    side_shape = [shape((local, width), F32), shape((3, local), F32)]
    side_spec = [turned_spec, whole((3, local))]
    kt_spec = whole((heads, HEAD_DIM, frames))
    half_lines = whole((part_rows, local))
    stack_rows = [local] * 4 if bits else [2 * local] * 2
    for half in halves:
        first = half == 0
        if not first and bits:
            fc[0] = halve(fc[0], "dp", bits[0][1])
            fc[1] = halve(fc[1], "dp", bits[1][1])
            fc_keep, fc_send = [jnp.concatenate(pieces) for pieces in zip(*fc)]
            hidden1_rows[1][0] = after(hidden1_rows[1][0], fc_keep, fc_send)
        if not first:
            mlp = scatter_direct([after(part, made[0]) for part in mlp])
        by_block = lambda n, half=half: pl.BlockSpec((back, n), lambda i: (half * turns + i, 0))
        specs = [
            by_block(local), by_block(heads * LANES),
            pl.BlockSpec((heads, back, LANES), lambda i, half=half: (0, half * turns + i, 0)),
            head_whole, head_whole, turned_spec,
        ]
        args = [mixed, mixed_full, query_back, key, value, w_out]
        scratch = [pltpu.VMEM((part_rows, width), LOW), pltpu.VMEM((heads * LANES, width), LOW)]
        if first:
            out_specs = [pl.BlockSpec((back, local), lambda i: (i, 0)), head_whole, head_whole]
            out_specs += [*side_spec, kt_spec]
            out_shape = [shape((part_rows, local), LOW), head_sums, head_sums, *side_shape]
            out_shape += [shape((heads, HEAD_DIM, frames), LOW)]
        else:
            specs += [head_whole, head_whole, *side_spec, kt_spec, half_lines]
            specs += [me_spec, whole((frames, width)), *[turned_spec] * 3, whole(vectors.shape)]
            args += [*made[1:], made[0], me, normed1, *turned, vectors]
            out_specs = [whole((frames, local))] * 3 + [whole((3, local)), whole((2, width))]
            out_specs += [whole((n, width)) for n in stack_rows]
            out_shape = [line, line, line, shape((3, local), F32), shape((2, width), F32)]
            out_shape += [shape((n, width), LOW) for n in stack_rows]
            scratch += [pltpu.VMEM((heads, frames, LANES), F32)] * 2
            scratch += [pltpu.VMEM((local, width), F32), pltpu.VMEM((4 * local, width), F32)]
        made = pl.pallas_call(
            functools.partial(attend_back_kernel, group, first, orders),
            grid=(turns,),
            in_specs=[slot_spec] * group + specs,
            out_specs=out_specs,
            out_shape=out_shape,
            scratch_shapes=scratch,
            compiler_params=params(1),
            cost_estimate=cost(
                5 * heads * frames * frames * 256, 9_000_000, heads * frames * frames // 2
            ),
            name="attend_back",
        )(*hidden1_rows[half], *args)
    query_grad, key_grad, value_grad, sums0, sums1, *stacks = made

    block_rows = lambda n: pl.BlockSpec((block, n), lambda i: (i, 0))
    query_grad = after(query_grad, *mlp[1:])
    if bits:
        f = fc_keep + pair(fc_send, "dp", bits[0][2])
        query_grad = after(query_grad, f)
    normed1_parts = pl.pallas_call(
        spread_kernel,
        grid=(2 * steps,),
        in_specs=[block_rows(local)] * 3 + [turned_spec] * 3,
        out_specs=[slot_spec] * (2 * group),
        out_shape=[shape((size, width), LOW)] * (2 * group),
        compiler_params=params(1),
        cost_estimate=cost(2 * frames * width * 3 * local, 6_000_000),
        name="spread",
    )(query_grad, key_grad, value_grad, *turned)
    small = jnp.concatenate(
        [sums0[0], sums0[2], fc1_bias_grad[0], sums1.reshape(-1), sums2.reshape(-1)]
    )
    parts = [normed1_parts[half * group : (half + 1) * group] for half in halves]
    count_own = 2 * local + hidden

    def settle(ends, order, count, size):
        return pl.pallas_call(
            functools.partial(settle_kernel, order),
            in_specs=[me_spec] + [pl.BlockSpec(memory_space=pltpu.VMEM)] * len(ends),
            out_shape=[shape((size, width), F32)] * count,
            compiler_params=params(),
            cost_estimate=cost(0, 6 * count * size * width),
            name="settle",
        )(me, *ends)

    hop = lambda value, bit: pair(value, "dp", bit)
    side = lambda index, turn: bits[index][turn]
    join = lambda *values: jnp.concatenate(values)
    together = lambda *values: lax.optimization_barrier(values)
    if bits:
        q = [(stacks[0], stacks[1]), (stacks[2], stacks[3])]
        got = together(
            hop(q[0][1], side(0, 0)), hop(q[1][1], side(1, 0)), hop(f, side(0, 2)),
            hop(small, 1), parts[0][0],
        )
        q = [tuple(jnp.split(q[i][0] + got[i], 2)) for i in range(2)]
        f0, f1 = [join(*pieces) for pieces in zip(jnp.split(f, 2), jnp.split(got[2], 2))]
        small = small + got[3]
        f_next = [hop(f0, side(0, 1)), hop(f1, side(1, 1))]
        got = together(hop(q[0][1], side(0, 1)), hop(q[1][1], side(1, 1)))
        small = after(small, *got)
        parts = [[after(part, *got) for part in own] for own in parts]
        q = [tuple(jnp.split(q[i][0] + got[i], 2)) for i in range(2)]
        keep, send = [join(*pieces) for pieces in zip(*q)]
        got = together(
            hop(send, side(0, 2)), hop(small, 2), *f_next,
            *[swap(parts[half][j], CORE) for half in halves for j in (3, 1)],
        )
        keep = keep + got[0]
        small = small + got[1]
        f0, f1 = join(f0, got[2]), join(f1, got[3])
        beside = [got[5], got[7]]
        far = [swap(parts[half][2] + got[4 + 2 * half], CHIP) for half in halves]
        f_last = [hop(f0, side(0, 0)), hop(f1, side(1, 0))]
        got = together(hop(keep, side(0, 2)), hop(small, 4))
        q = [join(*pieces) for pieces in zip(jnp.split(keep, 2), jnp.split(got[0], 2))]
        small = small + got[1]
        mine, shared = small[:count_own], small[count_own:]
        got = together(
            hop(q[0], side(0, 1)), hop(q[1], side(1, 1)), swap(shared, CORE), *far, *f_last
        )
        q = [join(q[i], got[i]) for i in range(2)]
        shared = shared + got[2]
        far, f_last = got[3:5], got[5:]
        shared = shared + swap(shared, CHIP)
        ends = [q[0], hop(q[0], side(0, 0)), q[1], hop(q[1], side(1, 0))]
        (fc2_grad,) = settle([f0, f_last[0]], orders[:1], 1, hidden)
        (fc1_grad,) = settle([f1, f_last[1]], orders[1:], 1, hidden)
        grads = settle(ends, orders, 4, local)
    else:
        grads = jnp.concatenate(lax.psum(tuple(stacks), "dp")).astype(F32)
        grads = jnp.split(grads, 4)
        small = sum_over(small, "dp")
        mine, shared = small[:count_own], sum_over(small[count_own:], "tensor")
        beside = [swap(part[1], CORE) for part in parts]
        far = [swap(part[2] + swap(part[3], CORE), CHIP) for part in parts]
    shared = shared.reshape(6, width)

    layer_out = pl.pallas_call(
        output_kernel,
        out_shape=shape((share, width), LOW),
        compiler_params=params(),
        cost_estimate=cost(8 * rows * width, 12 * rows * width),
        name="output",
    )(*hidden1, vectors, *mlp)

    features_grad = []
    for half in halves:
        features_grad = [
            pl.pallas_call(
                functools.partial(last_kernel, len(features_grad)),
                grid=(1,),
                in_specs=[own_half(half)]
                + [slot_spec] * 4
                + [whole(vectors.shape)]
                + [any_spec] * len(features_grad),
                out_specs=own_half(half),
                out_shape=shape((share, width), LOW),
                input_output_aliases={6: 0} if features_grad else {},
                compiler_params=params(1),
                cost_estimate=cost(20 * size * width, 14 * size * width),
                name="last",
            )(
                x_own,
                parts[half][0],
                beside[half],
                far[half],
                hidden1_grad[half],
                vectors,
                *features_grad,
            )
        ]
    return (
        layer_out[None],
        features_grad[0][None],
        grads[0].T,
        mine[:local],
        grads[1].T,
        grads[2].T,
        mine[local : 2 * local],
        grads[3],
        shared[4],
        shared[0],
        shared[1],
        shared[2],
        shared[3],
        fc1_grad,
        mine[2 * local :],
        fc2_grad,
        shared[5],
    )


def solution(mesh):
    rows = P("dp", "tensor", None)
    columns, lines, vector, same = P(None, "tensor"), P("tensor", None), P("tensor"), P()
    in_specs = (
        rows, rows, columns, vector, columns, columns, vector, lines, same,
        same, same, same, same, columns, vector, lines, same,
    )
    out_specs = (
        rows, rows, columns, vector, columns, columns, vector, lines, same,
        same, same, same, same, columns, vector, lines, same,
    )
    return jax.shard_map(
        on_device, mesh=mesh, in_specs=in_specs, out_specs=out_specs, check_vma=False
    )
```

```python
import functools

import jax
import jax.numpy as jnp
from jax import lax
from jax.experimental import pallas as pl
from jax.experimental.pallas import tpu as pltpu
from jax.sharding import PartitionSpec as P

HEAD_DIM = 64
LANES = 128
F32 = jnp.float32
LOW = jnp.bfloat16
MASK = -1e30
CORE, CHIP = 1, 2
ROOM = 56 * 1024 * 1024
NT = (((1,), (1,)), ((), ()))


def params(steps=0):
    semantics = ("arbitrary",) * steps if steps else None
    return pltpu.CompilerParams(vmem_limit_bytes=ROOM, dimension_semantics=semantics)


def cost(flops, moved, exps=0):
    return pl.CostEstimate(flops=flops, bytes_accessed=moved, transcendentals=exps)


def whole(shape):
    return pl.BlockSpec(shape, lambda *_: (0,) * len(shape))


def swap(value, partner):
    size = lax.axis_size("tensor")
    return lax.ppermute(value, "tensor", [(i, i ^ partner) for i in range(size)])


def after(value, *others):
    return lax.optimization_barrier((value, *others))[0]


def gather(own):
    return [own, swap(own, CORE), swap(own, CHIP)]


def finish(parts, *others):
    across = after(parts[2], *others) if others else parts[2]
    return [*parts[:2], across, swap(across, CORE)]


def scatter_direct(parts):
    return [parts[0]] + [swap(parts[j], j) for j in range(1, len(parts))]


def thirds(value):
    high = value.astype(LOW)
    rest = value - high.astype(F32)
    mid = rest.astype(LOW)
    return high, mid, (rest - mid.astype(F32)).astype(LOW)


def place(base, lane, first, pieces):
    for offset, piece in enumerate(pieces):
        base = jnp.where(lane == first + offset, piece, base)
    return base


def norm(values):
    mean = jnp.mean(values, axis=-1, keepdims=True)
    centred = values - mean
    spread = jnp.mean(centred * centred, axis=-1, keepdims=True)
    scaler = lax.rsqrt(spread + 1e-05)
    return centred * scaler, scaler


def norm_back(grad, unit, scaler, gain):
    scaled = grad * gain
    return scaler * (
        scaled
        - jnp.mean(scaled, axis=-1, keepdims=True)
        - unit * jnp.mean(scaled * unit, axis=-1, keepdims=True)
    )


def present(value, count):
    if count == value.shape[0]:
        return value
    row = lax.broadcasted_iota(jnp.int32, value.shape, 0)
    return jnp.where(row < count, value.astype(F32), 0.0).astype(value.dtype)


def pick(step, refs, rows, count):
    size = refs[0].shape[0]
    slots = rows.shape[0] // size
    for turn in range(len(refs) // slots):

        @pl.when(step == turn)
        def _():
            for at in range(slots):
                block = present(refs[turn * slots + at][...], count)
                rows[at * size : (at + 1) * size] = block


def stack_kernel(*refs):
    vec_ref, bias_ref = refs[-2:]
    for index, ref in enumerate(refs[:7]):
        vec_ref[index : index + 1] = ref[...].astype(F32).reshape(1, -1)
    bias_ref[...] = jnp.zeros_like(bias_ref)
    for index, ref in ((0, refs[7]), (2, refs[8])):
        bias_ref[index : index + 1] = ref[...].astype(F32).reshape(1, -1)


def project_kernel(share, slots, aliased, *refs):
    x_refs = refs[:slots]
    vec_ref, bias_ref, wq_ref, wk_ref, wv_ref = refs[slots : slots + 5]
    n_ref, q_ref, k_ref, v_ref, rows, w_tiles, b_tiles = refs[slots + 5 + aliased :]
    half = pl.program_id(0)
    heads = q_ref.shape[0]
    size = x_refs[0].shape[0]

    @pl.when(half == 0)
    def _():
        w_tiles[...] = jnp.zeros_like(w_tiles)
        b_tiles[...] = jnp.zeros_like(b_tiles)
        spot = lax.broadcasted_iota(jnp.int32, (1, LANES), 1) - HEAD_DIM
        ones = (
            jnp.where(spot == 0, HEAD_DIM**0.5, 0.0),
            jnp.where((spot >= 1) & (spot <= 3), 1.0, 0.0),
            jnp.where((spot >= 0) & (spot <= 2), 1.0, 0.0),
        )
        for which, w_ref in enumerate((wq_ref, wk_ref, wv_ref)):
            for head in range(heads):
                at = (which * heads + head) * LANES
                own = slice(head * HEAD_DIM, (head + 1) * HEAD_DIM)
                w_tiles[at : at + HEAD_DIM] = w_ref[own]
                b_tiles[:, at : at + LANES] = ones[which]
                b_tiles[:, at : at + HEAD_DIM] = bias_ref[which : which + 1, own]

    row = lax.broadcasted_iota(jnp.int32, (size, rows.shape[1]), 0) + half * size
    for at in range(slots):
        block = jnp.where(row < share, x_refs[at][...].astype(F32), 0.0)
        rows[at * size : (at + 1) * size] = block
    unit, _ = norm(rows[...])
    normed = (unit * vec_ref[0:1] + vec_ref[1:2]).astype(LOW)
    n_ref[...] = normed
    out = lax.dot_general(normed, w_tiles[...], NT, preferred_element_type=F32) + b_tiles[...]
    row = lax.broadcasted_iota(jnp.int32, (out.shape[0], LANES), 0)
    lane = lax.broadcasted_iota(jnp.int32, (out.shape[0], LANES), 1)
    absent = (lax.rem(row, size) + half * size >= share) & (lane == HEAD_DIM)
    scale = HEAD_DIM ** (-0.5)
    for head in range(heads):
        part = lambda which: out[:, (which * heads + head) * LANES :][:, :LANES]
        q_ref[head] = (part(0).astype(LOW).astype(F32) * scale).astype(LOW)
        k_ref[head] = jnp.where(absent, MASK, part(1)).astype(LOW)
        v_ref[head] = part(2).astype(LOW)


def attend_kernel(aliased, slots, q_ref, k_ref, v_ref, *refs):
    o_ref, full_ref, q_out = refs[aliased:]
    heads, block, _ = q_ref.shape
    quarter = block // slots // 2
    lane = lax.broadcasted_iota(jnp.int32, (block, LANES), 1)
    for head in range(heads):
        query = q_ref[head]
        scores = lax.dot_general(query, k_ref[head], NT, preferred_element_type=F32)
        top = jnp.max(scores, axis=-1, keepdims=True)
        weights = jnp.exp(scores - top).astype(LOW)
        out = jnp.dot(weights, v_ref[head], preferred_element_type=F32)
        total = out[:, HEAD_DIM : HEAD_DIM + 1]
        out = out / total
        full_ref[:, head * LANES : (head + 1) * LANES] = out
        low = out[:, :HEAD_DIM].astype(LOW)
        for part in range(2 * slots):
            at = ((part % 2) * heads + head) * HEAD_DIM
            o_ref[part // 2 * quarter : (part // 2 + 1) * quarter, at : at + HEAD_DIM] = low[
                part * quarter : (part + 1) * quarter
            ]
        logsum = top + jnp.log(total)
        q_out[head] = place(query, lane, HEAD_DIM + 1, thirds(-logsum))


def feed_kernel(half, share, group, aliased, *refs):
    x_refs, m_refs, wo_refs = refs[:group], refs[group : 3 * group], refs[3 * group : 4 * group]
    g_refs = refs[4 * group : 5 * group]
    vec_ref, w1_ref, w2_ref = refs[5 * group : 5 * group + 3]
    old = refs[5 * group + 3 : 5 * group + 3 + half]
    outs = refs[5 * group + 3 + half + aliased :]
    h_ref, n_ref, a_ref, p_ref, c_ref, db_ref = outs[:6]
    d_refs = outs[6 : 6 + group]
    rows, mixed, wo_all = outs[6 + group :]
    step = pl.program_id(0)
    size = x_refs[0].shape[0]
    slots = rows.shape[0] // size
    quarter = size // 2
    count = min(size, share - half * size)
    pick(step, x_refs, rows, count)
    pick(step, g_refs, c_ref, count)
    local = wo_refs[0].shape[0]
    for source in range(group):
        for at in range(slots):
            packed = m_refs[source * slots + at][...]
            for part in range(2):
                first = at * size + part * quarter
                mixed[first : first + quarter, source * local : (source + 1) * local] = packed[
                    :, part * local : (part + 1) * local
                ]

    @pl.when(step == 0)
    def _():
        for source in range(group):
            wo_all[source * local : (source + 1) * local] = wo_refs[source][...]

    branch = jnp.dot(mixed[...], wo_all[...], preferred_element_type=F32)
    hidden = rows[...].astype(F32) + branch + vec_ref[2:3]

    @pl.when(step == 0)
    def _():
        h_ref[...] = hidden[:size]
        db_ref[...] = old[0][...] if old else jnp.zeros_like(db_ref)

    unit, _ = norm(hidden)
    normed = (unit * vec_ref[3:4] + vec_ref[4:5]).astype(LOW)
    n_ref[...] = normed
    pre = jnp.dot(normed, w1_ref[...], preferred_element_type=F32) + vec_ref[5:6]
    active_grad = lax.dot_general(c_ref[...], w2_ref[...], NT, preferred_element_type=F32)
    size_of = jnp.abs(pre)
    bell = jnp.exp(-0.5 * pre * pre)
    t = 1.0 / (1.0 + (0.3275911 * 0.5**0.5) * size_of)
    poly = t * (
        0.127414796 + t * (-0.142248368 + t * (0.7107068705 + t * (-0.7265760135 + t * 0.5307027145)))
    )
    tail = poly * bell
    gate = jnp.where(pre >= 0, 1.0 - tail, tail)
    a_ref[...] = (pre * gate).astype(LOW)
    pre_grad = active_grad * (gate + pre * bell * 0.3989422804014327)
    db_ref[...] += jnp.sum(pre_grad, axis=0, keepdims=True)
    pre_low = pre_grad.astype(LOW)
    p_ref[...] = pre_low
    back = lax.dot_general(pre_low, w1_ref[...], NT, preferred_element_type=F32).astype(LOW)
    for turn in range(group // slots):

        @pl.when(step == turn)
        def _():
            for at in range(slots):
                d_refs[turn * slots + at][...] = back[at * size : (at + 1) * size]


def middle_kernel(count, terms, h_ref, g_ref, vec_ref, *refs):
    out_ref, low_ref, sums_ref = refs[-3:]
    grad = sum(ref[...].astype(F32) for ref in refs[:terms])
    unit, scaler = norm(h_ref[...])
    cot = present(g_ref[...], count).astype(F32)
    hidden_grad = cot + norm_back(grad, unit, scaler, vec_ref[3:4])
    out_ref[...] = hidden_grad
    low_ref[...] = hidden_grad.astype(LOW)
    add = lambda value: jnp.sum(value, axis=0, keepdims=True)
    sums = jnp.concatenate([add(grad * unit), add(grad), add(hidden_grad), add(cot)], axis=0)
    sums_ref[...] = sum((ref[...] for ref in refs[terms:-3]), sums)


def attend_back_kernel(parts, head, heads, orders, *refs):
    h_refs = refs[:parts]
    full_ref, q_ref, k_ref, v_ref, wo_ref, n_ref, wq_ref, wk_ref, wv_ref = refs[parts : parts + 9]
    at = parts + 9
    last = head == heads - 1
    if head:
        old_ref = refs[at]
        at += 1
    if last:
        me_ref, vec_ref, sums_ref, db_ref = refs[at : at + 4]
        done_refs = refs[at + 4 : at + 3 + heads]
        at += 3 + heads
    grad_ref, small_ref = refs[at : at + 2]
    outs = refs[at + 2 : -7]
    rows, wo_tile, w_stack, kt_ref, dk_sum, dv_sum, dw_sum = refs[-7:]
    step = pl.program_id(0)
    _, block, _ = q_ref.shape
    own = [slice(which * HEAD_DIM, (which + 1) * HEAD_DIM) for which in range(4)]

    @pl.when(step == 0)
    def _():
        size = h_refs[0].shape[0]
        for part in range(parts):
            rows[part * size : (part + 1) * size] = h_refs[part][...]
        wo_tile[:HEAD_DIM] = wo_ref[...]
        wo_tile[HEAD_DIM:] = jnp.zeros_like(wo_tile[HEAD_DIM:])
        for which, w_ref in enumerate((wq_ref, wk_ref, wv_ref)):
            w_stack[own[which]] = w_ref[...]
        for total in (dk_sum, dv_sum, dw_sum):
            total[...] = jnp.zeros_like(total)
        kt_ref[...] = k_ref[0].astype(F32).T[:HEAD_DIM].astype(LOW)

    scale = HEAD_DIM ** (-0.5)
    lane = lax.broadcasted_iota(jnp.int32, (block, LANES), 1)
    here = pl.ds(pl.multiple_of(step * block, block), block)
    hidden_grad = rows[here]
    full = full_ref[...]
    out_grad = lax.dot_general(hidden_grad, wo_tile[...], NT, preferred_element_type=F32)
    out_grad = out_grad.astype(LOW)
    dw_sum[...] += lax.dot_general(
        full.astype(LOW), hidden_grad, (((0,), (0,)), ((), ())), preferred_element_type=F32
    )
    delta = jnp.sum(out_grad.astype(F32) * full, axis=-1, keepdims=True)
    out_grad = place(out_grad, lane, HEAD_DIM, thirds(-delta))
    query = q_ref[0]
    scores = lax.dot_general(k_ref[0], query, NT, preferred_element_type=F32)
    probs = jnp.exp(scores)
    prob_grad = lax.dot_general(v_ref[0], out_grad, NT, preferred_element_type=F32)
    score_grad = (probs * prob_grad).astype(LOW)
    dv_sum[...] += jnp.dot(probs.astype(LOW), out_grad, preferred_element_type=F32)
    dk_sum[...] += jnp.dot(score_grad, query, preferred_element_type=F32)
    turned = jnp.dot(kt_ref[...], score_grad, preferred_element_type=F32)
    grad_ref[here, own[0]] = (turned.T * scale).astype(LOW)

    @pl.when(step == pl.num_programs(0) - 1)
    def _():
        grad_ref[:, own[1]] = dk_sum[:, :HEAD_DIM].astype(LOW)
        grad_ref[:, own[2]] = dv_sum[:, :HEAD_DIM].astype(LOW)
        grads = grad_ref[...]
        weight_grad = lax.dot_general(
            grads, n_ref[...], (((0,), (0,)), ((), ())), preferred_element_type=F32
        )
        weights = w_stack[...].astype(F32)
        totals = jnp.sum(grads.astype(F32), axis=0, keepdims=True)
        gain = jnp.sum(weights * weight_grad, axis=0, keepdims=True)
        shift = jnp.dot(
            totals, weights, precision=lax.Precision.HIGHEST, preferred_element_type=F32
        )
        if head:
            gain += old_ref[0:1]
            shift += old_ref[1:2]
            small_ref[6:7] = old_ref[6:7]
        else:
            small_ref[...] = jnp.zeros_like(small_ref)
        local = heads * HEAD_DIM
        for which, first in ((0, 0), (2, local)):
            start = first + head * HEAD_DIM
            small_ref[6:7, start : start + HEAD_DIM] = totals[:, own[which]]
        small_ref[1:2] = shift
        if not last:
            small_ref[0:1] = gain
            outs[0][: 3 * HEAD_DIM] = weight_grad
            outs[0][3 * HEAD_DIM :] = dw_sum[:HEAD_DIM]
            return
        small_ref[0:1] = (gain - vec_ref[1:2] * shift) / vec_ref[0:1]
        small_ref[2:6] = sums_ref[...]
        small_ref[7:8] = db_ref[...]
        stacks = outs[-1]
        for which in range(4):
            for index, done in enumerate(done_refs):
                start = which * local + index * HEAD_DIM
                stacks[start : start + HEAD_DIM] = done[own[which]]
            start = which * local + head * HEAD_DIM
            value = weight_grad[own[which]] if which < 3 else dw_sum[:HEAD_DIM]
            stacks[start : start + HEAD_DIM] = value
        if orders is None:
            outs[0][...] = stacks[: 2 * local].astype(LOW)
            outs[1][...] = stacks[2 * local :].astype(LOW)
            return
        for stack, order in enumerate(orders):
            size = 2 * local // len(order)
            for spot, slot in enumerate(order):
                which, index = divmod(spot, len(order) // 2)
                start = stack * 2 * local + jnp.bitwise_xor(me_ref[0], slot) * size
                piece = stacks[pl.ds(pl.multiple_of(start, size), size)]
                outs[2 * stack + which][index * size : (index + 1) * size] = piece.astype(LOW)


def outer_kernel(order, me_ref, left_ref, right_ref, keep_ref, send_ref, total):
    step = pl.program_id(0)

    @pl.when(step == 0)
    def _():
        total[...] = jnp.zeros_like(total)

    total[...] += lax.dot_general(
        left_ref[...], right_ref[...], (((0,), (0,)), ((), ())), preferred_element_type=F32
    )

    @pl.when(step == pl.num_programs(0) - 1)
    def _():
        size = total.shape[0] // len(order)
        for spot, slot in enumerate(order):
            which, at = divmod(spot, len(order) // 2)
            start = jnp.bitwise_xor(me_ref[0], slot) * size
            piece = total[pl.ds(pl.multiple_of(start, size), size)].astype(LOW)
            (keep_ref, send_ref)[which][at * size : (at + 1) * size] = piece


def settle_kernel(orders, me_ref, *refs):
    outs = refs[2 * len(orders) :]
    sides = len(outs) // len(orders)
    for stack, order in enumerate(orders):
        halves = refs[2 * stack : 2 * stack + 2]
        size = 2 * halves[0].shape[0] // len(order)
        per = len(order) // sides
        for spot, slot in enumerate(order):
            which, at = divmod(spot, len(order) // 2)
            value = halves[which][at * size : (at + 1) * size].astype(F32)
            place_at = jnp.bitwise_xor(me_ref[0], slot)
            start = pl.multiple_of(lax.rem(place_at, per) * size, size)
            for side in range(sides):

                @pl.when(lax.div(place_at, per) == side)
                def _():
                    outs[sides * stack + side][pl.ds(start, size)] = value


def spread_kernel(heads, *refs):
    grads, weights, outs = refs[:heads], refs[heads : heads + 3], refs[heads + 3 : -1]
    w_stacks = refs[-1]
    step = pl.program_id(0)

    @pl.when(step == 0)
    def _():
        for head in range(heads):
            for which, w_ref in enumerate(weights):
                start = (head * 3 + which) * HEAD_DIM
                w_stacks[start : start + HEAD_DIM] = w_ref[
                    head * HEAD_DIM : (head + 1) * HEAD_DIM
                ]

    each = 3 * HEAD_DIM
    total = sum(
        jnp.dot(
            grads[head][...],
            w_stacks[head * each : (head + 1) * each],
            preferred_element_type=F32,
        )
        for head in range(heads)
    ).astype(LOW)
    size = outs[0].shape[0]
    slots = total.shape[0] // size
    for turn in range(len(outs) // slots):

        @pl.when(step == turn)
        def _():
            for at in range(slots):
                outs[turn * slots + at][...] = total[at * size : (at + 1) * size]


def last_kernel(aliased, x_ref, d0_ref, d1_ref, d2_ref, h_ref, vec_ref, *refs):
    out_ref = refs[aliased]
    grad = d0_ref[...].astype(F32) + d1_ref[...].astype(F32) + d2_ref[...].astype(F32)
    unit, scaler = norm(x_ref[...].astype(F32))
    out_ref[...] = (h_ref[...] + norm_back(grad, unit, scaler, vec_ref[0:1])).astype(LOW)


def output_kernel(ha_ref, hb_ref, vec_ref, *refs):
    out_ref = refs[-1]
    size = ha_ref.shape[0]
    share = out_ref.shape[0]
    for part, h_ref in enumerate((ha_ref, hb_ref)):
        mlp = sum(ref[part].astype(F32) for ref in refs[:-1])
        value = (h_ref[...] + mlp + vec_ref[6:7]).astype(LOW)
        count = min(size, share - part * size)
        out_ref[part * size : part * size + count] = value[:count]


def pair(value, axis, step):
    size = lax.axis_size(axis)
    return lax.ppermute(value, axis, [(i, i ^ step) for i in range(size)])


def sum_over(value, axis):
    size = lax.axis_size(axis)
    if size & (size - 1):
        return lax.psum(value, axis)
    step = 1
    while step < size:
        value = value + pair(value, axis, step)
        step *= 2
    return value


def exchange_order(bits):
    order = [0]
    for bit in reversed(bits):
        order = order + [slot | bit for slot in order]
    return order


def halve(parts, axis, bit):
    keep, send = parts
    return tuple(jnp.split(keep + pair(send, axis, bit), 2))


def on_device(
    features, cotangent, w_query, bias_query, w_key, w_value, bias_value, w_out, bias_out,
    norm1_gain, norm1_bias, norm2_gain, norm2_bias, w_fc1, bias_fc1, w_fc2, bias_fc2,
):
    _, share, width = features.shape
    local = w_query.shape[1]
    heads = local // HEAD_DIM
    hidden = w_fc1.shape[1]
    group = lax.axis_size("tensor")
    clips = lax.axis_size("dp")
    rows = -(-share // LANES) * LANES
    size = rows // 2
    frames = group * rows
    part_rows = group * size
    slots = 2
    block = slots * size
    steps = group // slots
    shape = jax.ShapeDtypeStruct
    halves = range(2)
    count = lambda half: min(size, share - half * size)

    x_own, g_own = features[0], cotangent[0]
    x_all = gather(x_own)
    wo_all = gather(after(w_out, x_all[2]))
    g_all = gather(after(g_own, wo_all[1]))
    vectors, biases = pl.pallas_call(
        stack_kernel,
        out_shape=[shape((7, width), F32), shape((3, local), F32)],
        compiler_params=params(),
        cost_estimate=cost(0, 12 * width * 8),
        name="stack",
    )(
        norm1_gain, norm1_bias, bias_out, norm2_gain, norm2_bias, bias_fc1, bias_fc2,
        bias_query, bias_value,
    )
    turned = [w_query.T, w_key.T, w_value.T]

    slot_spec = whole((size, width))
    turned_spec = whole((local, width))
    any_spec = pl.BlockSpec(memory_space=pl.ANY)
    at_half = lambda half, n: pl.BlockSpec((block, n), lambda i: (half * steps + i, 0))
    own_half = lambda half: pl.BlockSpec((size, width), lambda *_: (half, 0))
    head_half = lambda half: pl.BlockSpec((heads, block, LANES), lambda i: (0, half * steps + i, 0))
    head_shape = shape((heads, frames, LANES), LOW)

    made = []
    for turn in range(steps):
        if turn:
            x_all = finish(x_all, made[0])
        made = pl.pallas_call(
            functools.partial(project_kernel, share, slots, len(made)),
            grid=(2,),
            in_specs=[pl.BlockSpec((size, width), lambda i: (i, 0))] * slots
            + [whole(vectors.shape), whole(biases.shape)]
            + [turned_spec] * 3
            + [any_spec] * len(made),
            out_specs=[pl.BlockSpec((block, width), lambda i, turn=turn: (i * steps + turn, 0))]
            + [
                pl.BlockSpec((heads, block, LANES), lambda i, turn=turn: (0, i * steps + turn, 0))
            ]
            * 3,
            out_shape=[shape((frames, width), LOW)] + [head_shape] * 3,
            scratch_shapes=[
                pltpu.VMEM((block, width), F32),
                pltpu.VMEM((3 * heads * LANES, width), LOW),
                pltpu.VMEM((1, 3 * heads * LANES), F32),
            ],
            input_output_aliases={slots + 5 + i: i for i in range(len(made))},
            compiler_params=params(1),
            cost_estimate=cost(2 * part_rows * width * 9 * LANES, 6_000_000),
            name="project",
        )(*x_all[turn * slots : (turn + 1) * slots], vectors, biases, *turned, *made)
    normed1, query, key, value = made

    head_whole = whole((heads, frames, LANES))
    made, packed = [], []
    for half in halves:
        made = pl.pallas_call(
            functools.partial(attend_kernel, len(made), slots),
            grid=(steps,),
            in_specs=[head_half(half), head_whole, head_whole] + [any_spec] * len(made),
            out_specs=[
                pl.BlockSpec((block // 2, 2 * local), lambda i: (i, 0)),
                at_half(half, heads * LANES), head_half(half),
            ],
            out_shape=[
                shape((part_rows // 2, 2 * local), LOW), shape((frames, heads * LANES), F32),
                head_shape,
            ],
            input_output_aliases={3 + i: 1 + i for i in range(len(made))},
            compiler_params=params(1),
            cost_estimate=cost(
                2 * heads * frames * frames * 256, 5_000_000, heads * frames * frames // 2
            ),
            name="attend",
        )(query, key, value, *made)
        packed.append(gather(made[0]))
        made = made[1:]
        if half == 0:
            g_all = finish(g_all, made[0])
            wo_all = finish(wo_all, made[0])
    mixed_full, query_back = made
    packed[0] = finish(packed[0], mixed_full)

    low_rows = shape((frames, hidden), LOW)
    made, hidden1, fc1_bias_grad, normed2_parts = [], [], [], []
    for half in halves:
        if half:
            packed[half] = finish(packed[half], made[0])
        sources = packed[half]
        packed_specs, packed_args = [], []
        for source in range(group):
            for at in range(slots):
                packed_args.append(sources[source])
                packed_specs.append(
                    pl.BlockSpec(
                        (size // 2, 2 * local),
                        lambda i, source=source, at=at: ((i * slots + at) ^ source, 0),
                    )
                )
        made = pl.pallas_call(
            functools.partial(feed_kernel, half, share, group, len(made)),
            grid=(steps,),
            in_specs=[own_half(half)] * group
            + packed_specs
            + [whole((local, width))] * group
            + [own_half(half)] * group
            + [whole(vectors.shape), whole((width, hidden)), whole((hidden, width))]
            + [whole((1, hidden))] * half
            + [any_spec] * len(made),
            out_specs=[slot_spec]
            + [at_half(half, n) for n in (width, hidden, hidden, width)]
            + [whole((1, hidden))]
            + [slot_spec] * group,
            out_shape=[
                shape((size, width), F32), shape((frames, width), LOW), low_rows, low_rows,
                shape((frames, width), LOW), shape((1, hidden), F32),
            ]
            + [shape((size, width), LOW)] * group,
            scratch_shapes=[pltpu.VMEM((block, width), LOW)] * 2
            + [pltpu.VMEM((width, width), LOW)],
            input_output_aliases={5 * group + 3 + half + i: 1 + i for i in range(len(made))},
            compiler_params=params(1),
            cost_estimate=cost(4 * frames * width * hidden, 12_000_000, frames * hidden // 2),
            name="feed",
        )(
            *x_all, *packed_args, *wo_all, *g_all, vectors, w_fc1, w_fc2,
            *fc1_bias_grad, *made
        )
        hidden1.append(made[0])
        fc1_bias_grad = [made[5]]
        normed2_parts.append(made[6:])
        made = made[1:5]
    normed2, active, pre_low, cot_rows = made

    hidden1_grad, sums2, hidden1_rows = [], [], []
    far = normed2_parts[1][2] + swap(normed2_parts[1][3], CORE)
    all_terms = [
        scatter_direct(normed2_parts[0]),
        [normed2_parts[1][0], swap(normed2_parts[1][1], CORE), swap(far, CHIP)],
    ]
    for half in halves:
        terms = all_terms[half]
        grad, low, sums = pl.pallas_call(
            functools.partial(middle_kernel, count(half), len(terms)),
            grid=(1,),
            in_specs=[slot_spec, own_half(half), whole(vectors.shape)]
            + [slot_spec] * len(terms)
            + [whole((4, width))] * half,
            out_specs=[slot_spec, slot_spec, whole((4, width))],
            out_shape=[
                shape((size, width), F32), shape((size, width), LOW), shape((4, width), F32),
            ],
            compiler_params=params(1),
            cost_estimate=cost(20 * size * width, 16 * size * width),
            name="middle",
        )(hidden1[half], g_own, vectors, *terms, *sums2)
        hidden1_grad.append(grad)
        sums2 = [sums]
        hidden1_rows.append(gather(low if half else after(low, far)))

    tn = lambda left, right: lax.dot_general(
        left, right, (((0,), (0,)), ((), ())), preferred_element_type=F32
    )
    low_ready = hidden1_rows[0][0]
    active = after(active, low_ready)
    mlp_part = jnp.dot(active, w_fc2, preferred_element_type=F32).astype(LOW)
    mlp_part = mlp_part.reshape(2, group, size, width)
    me = lax.axis_index("dp").astype(jnp.int32).reshape(1)
    me_spec = pl.BlockSpec(memory_space=pltpu.SMEM)
    bits = ((1, 2, 4), (2, 1, 4)) if clips == 8 else None
    orders = [exchange_order(order) for order in bits] if bits else None
    hidden1_rows[0] = finish(hidden1_rows[0])
    hidden1_rows[1].append(swap(hidden1_rows[1][0], CORE | CHIP))
    if bits:
        fc = []
        normed2 = after(normed2, low_ready)
        for index, (left, right) in enumerate(((active, cot_rows), (normed2, pre_low))):
            if index:
                left = after(left, fc[0][1], mlp_part, all_terms[1][2])
            fc.append(
                pl.pallas_call(
                    functools.partial(outer_kernel, orders[index]),
                    grid=(2,),
                    in_specs=[me_spec]
                    + [
                        pl.BlockSpec((part_rows, part.shape[1]), lambda i: (i, 0))
                        for part in (left, right)
                    ],
                    out_specs=[whole((left.shape[1] // 2, right.shape[1]))] * 2,
                    out_shape=[shape((left.shape[1] // 2, right.shape[1]), LOW)] * 2,
                    scratch_shapes=[pltpu.VMEM((left.shape[1], right.shape[1]), F32)],
                    compiler_params=params(1),
                    cost_estimate=cost(2 * frames * width * hidden, 8_000_000),
                    name="outer",
                )(me, left, right)
            )
        fc = [halve(fc[index], "dp", bits[index][0]) for index in range(2)]
        hidden1_rows[0][0] = after(hidden1_rows[0][0], fc[0][1], fc[1][1])
    else:
        fc_own = (tn(active, cot_rows).astype(LOW), tn(normed2, pre_low).astype(LOW))
        fc2_grad, fc1_grad = [total.astype(F32) for total in lax.psum(fc_own, "dp")]
    mlp_far = mlp_part[:, 2] + swap(mlp_part[:, 3], CORE)
    mlp = [mlp_part[:, 0], mlp_part[:, 1], mlp_far]
    hidden1_rows[0][0] = after(hidden1_rows[0][0], *mlp)
    back = 512
    each = 3 * HEAD_DIM
    stack_rows = [local] * 4 if bits else [2 * local] * 2
    all_rows = hidden1_rows[0] + hidden1_rows[1]
    head_row = lambda head: pl.BlockSpec((HEAD_DIM, width), lambda i: (head, 0))
    head_tile = lambda head: pl.BlockSpec((1, frames, LANES), lambda i: (head, 0, 0))
    small_shape, done_shape = shape((8, width), F32), shape((4 * HEAD_DIM, width), F32)
    grads, dones, small = [], [], []
    for head in range(heads):
        last = head == heads - 1
        if head == 1:
            mlp = scatter_direct([after(part, grads[0]) for part in mlp])
            if bits:
                fc = [halve(fc[index], "dp", bits[index][1]) for index in range(2)]
                fc_keep, fc_send = [jnp.concatenate(pieces) for pieces in zip(*fc)]
                all_rows[0] = after(all_rows[0], fc_keep, fc_send)
        if last:
            all_rows[0] = after(all_rows[0], *mlp[1:])
            if bits:
                f = fc_keep + pair(fc_send, "dp", bits[0][2])
                all_rows[0] = after(all_rows[0], f)
        specs = [slot_spec] * len(all_rows) + [
            pl.BlockSpec((back, LANES), lambda i, head=head: (i, head)),
            pl.BlockSpec((1, back, LANES), lambda i, head=head: (head, i, 0)),
            head_tile(head), head_tile(head), head_row(head), whole((frames, width)),
            *[head_row(head)] * 3,
        ]
        args = [*all_rows, mixed_full, query_back, key, value, w_out, normed1, *turned]
        if head:
            specs += [whole((8, width))]
            args += small
        out_shape = [shape((frames, each), LOW), small_shape]
        scratch = [
            pltpu.VMEM((frames, width), LOW), pltpu.VMEM((LANES, width), LOW),
            pltpu.VMEM((each, width), LOW), pltpu.VMEM((HEAD_DIM, frames), LOW),
            pltpu.VMEM((frames, LANES), F32), pltpu.VMEM((frames, LANES), F32),
            pltpu.VMEM((LANES, width), F32),
        ]
        if last:
            specs += [me_spec, whole(vectors.shape), whole((4, width)), whole((1, hidden))]
            specs += [whole(done_shape.shape)] * len(dones)
            args += [me, vectors, *sums2, *fc1_bias_grad, *dones]
            out_shape += [shape((n, width), LOW) for n in stack_rows]
            scratch.insert(0, pltpu.VMEM((4 * local, width), F32))
        else:
            out_shape += [done_shape]
        grad, total, *rest = pl.pallas_call(
            functools.partial(attend_back_kernel, len(all_rows), head, heads, orders),
            grid=(frames // back,),
            in_specs=specs,
            out_specs=[whole(out.shape) for out in out_shape],
            out_shape=out_shape,
            scratch_shapes=scratch,
            compiler_params=params(1),
            cost_estimate=cost(10 * frames * frames * 256, 8_000_000, frames * frames),
            name="attend_back",
        )(*args)
        grads.append(grad)
        small = [total]
        if last:
            stacks = rest
        else:
            dones += rest
            all_rows[1] = after(all_rows[1], total)
    small = small[0]
    if bits:
        got = pair(f, "dp", bits[0][2])
        f0, f1 = [jnp.concatenate(pieces) for pieces in zip(jnp.split(f, 2), jnp.split(got, 2))]
        grads[0] = after(grads[0], f0, f1)

    block_rows = lambda n: pl.BlockSpec((block, n), lambda i: (i, 0))
    normed1_parts = pl.pallas_call(
        functools.partial(spread_kernel, heads),
        grid=(2 * steps,),
        in_specs=[block_rows(each)] * heads + [turned_spec] * 3,
        out_specs=[slot_spec] * (2 * group),
        out_shape=[shape((size, width), LOW)] * (2 * group),
        scratch_shapes=[pltpu.VMEM((heads * each, width), LOW)],
        compiler_params=params(1),
        cost_estimate=cost(2 * frames * width * 3 * local, 6_000_000),
        name="spread",
    )(*grads, *turned)
    parts = [normed1_parts[half * group : (half + 1) * group] for half in halves]

    def settle(ends, order, count, size):
        return pl.pallas_call(
            functools.partial(settle_kernel, order),
            in_specs=[me_spec] + [pl.BlockSpec(memory_space=pltpu.VMEM)] * len(ends),
            out_shape=[shape((size, width), F32)] * count,
            compiler_params=params(),
            cost_estimate=cost(0, 6 * count * size * width),
            name="settle",
        )(me, *ends)

    hop = lambda value, bit: pair(value, "dp", bit)
    side = lambda index, turn: bits[index][turn]
    join = lambda *values: jnp.concatenate(values)
    together = lambda *values: lax.optimization_barrier(values)
    if bits:
        q = [(stacks[0], stacks[1]), (stacks[2], stacks[3])]
        got = together(
            hop(q[0][1], side(0, 0)), hop(q[1][1], side(1, 0)),
            hop(f0, side(0, 1)), hop(f1, side(1, 1)), hop(small, 1), parts[0][0],
        )
        q = [tuple(jnp.split(q[i][0] + got[i], 2)) for i in range(2)]
        f0, f1 = join(f0, got[2]), join(f1, got[3])
        small = small + got[4]
        f_last = [hop(f0, side(0, 0)), hop(f1, side(1, 0))]
        got = together(hop(q[0][1], side(0, 1)), hop(q[1][1], side(1, 1)))
        small = after(small, *got)
        parts = [[after(part, *got) for part in own] for own in parts]
        q = [tuple(jnp.split(q[i][0] + got[i], 2)) for i in range(2)]
        keep, send = [join(*pieces) for pieces in zip(*q)]
        got = together(
            hop(send, side(0, 2)), hop(small, 2),
            *[swap(parts[half][j], CORE) for half in halves for j in (3, 1)],
        )
        keep, small = keep + got[0], small + got[1]
        beside = [got[3], got[5]]
        far = [swap(parts[half][2] + got[2 + 2 * half], CHIP) for half in halves]
        got = together(hop(keep, side(0, 2)), hop(small, 4), *f_last)
        q = [join(*pieces) for pieces in zip(jnp.split(keep, 2), jnp.split(got[0], 2))]
        small, f_last = small + got[1], got[2:]
        got = together(
            hop(q[0], side(0, 1)), hop(q[1], side(1, 1)), swap(small, CORE), *far
        )
        q = [join(q[i], got[i]) for i in range(2)]
        shared = small + got[2]
        far = got[3:]
        shared = shared + swap(shared, CHIP)
        ends = [q[0], hop(q[0], side(0, 0)), q[1], hop(q[1], side(1, 0))]
        (fc2_grad,) = settle([f0, f_last[0]], orders[:1], 1, hidden)
        (fc1_grad,) = settle([f1, f_last[1]], orders[1:], 1, hidden)
        grads = settle(ends, orders, 4, local)
    else:
        grads = jnp.concatenate(lax.psum(tuple(stacks), "dp")).astype(F32)
        grads = jnp.split(grads, 4)
        small = sum_over(small, "dp")
        shared = sum_over(small, "tensor")
        beside = [swap(part[1], CORE) for part in parts]
        far = [swap(part[2] + swap(part[3], CORE), CHIP) for part in parts]

    layer_out = pl.pallas_call(
        output_kernel,
        out_shape=shape((share, width), LOW),
        compiler_params=params(),
        cost_estimate=cost(8 * rows * width, 12 * rows * width),
        name="output",
    )(*hidden1, vectors, *mlp)

    features_grad = []
    for half in halves:
        features_grad = [
            pl.pallas_call(
                functools.partial(last_kernel, len(features_grad)),
                grid=(1,),
                in_specs=[own_half(half)]
                + [slot_spec] * 4
                + [whole(vectors.shape)]
                + [any_spec] * len(features_grad),
                out_specs=own_half(half),
                out_shape=shape((share, width), LOW),
                input_output_aliases={6: 0} if features_grad else {},
                compiler_params=params(1),
                cost_estimate=cost(20 * size * width, 14 * size * width),
                name="last",
            )(
                x_own,
                parts[half][0],
                beside[half],
                far[half],
                hidden1_grad[half],
                vectors,
                *features_grad,
            )
        ]
    return (
        layer_out[None],
        features_grad[0][None],
        grads[0].T,
        small[6, :local],
        grads[1].T,
        grads[2].T,
        small[6, local : 2 * local],
        grads[3],
        shared[4],
        shared[0],
        shared[1],
        shared[2],
        shared[3],
        fc1_grad,
        small[7],
        fc2_grad,
        shared[5],
    )


def solution(mesh):
    rows = P("dp", "tensor", None)
    columns, lines, vector, same = P(None, "tensor"), P("tensor", None), P("tensor"), P()
    in_specs = (
        rows, rows, columns, vector, columns, columns, vector, lines, same,
        same, same, same, same, columns, vector, lines, same,
    )
    out_specs = (
        rows, rows, columns, vector, columns, columns, vector, lines, same,
        same, same, same, same, columns, vector, lines, same,
    )
    return jax.shard_map(
        on_device, mesh=mesh, in_specs=in_specs, out_specs=out_specs, check_vma=False
    )
```

```python
import functools

import jax
import jax.numpy as jnp
from jax import lax
from jax.experimental import pallas as pl
from jax.experimental.pallas import tpu as pltpu
from jax.sharding import PartitionSpec as P

HEAD_DIM = 64
LANES = 128
F32 = jnp.float32
LOW = jnp.bfloat16
MASK = -1e30
CORE, CHIP = 1, 2
MIB = 1024 * 1024
NT = (((1,), (1,)), ((), ()))


def params(room, steps=0):
    semantics = ("arbitrary",) * steps if steps else None
    return pltpu.CompilerParams(vmem_limit_bytes=room * MIB, dimension_semantics=semantics)


def cost(flops, moved, exps=0):
    return pl.CostEstimate(flops=flops, bytes_accessed=moved, transcendentals=exps)


def whole(shape):
    return pl.BlockSpec(shape, lambda *_: (0,) * len(shape))


def swap(value, partner):
    size = lax.axis_size("tensor")
    return lax.ppermute(value, "tensor", [(i, i ^ partner) for i in range(size)])


def after(value, *others):
    return lax.optimization_barrier((value, *others))[0]


def gather(own):
    return [own, swap(own, CORE), swap(own, CHIP)]


def finish(parts, *others):
    across = after(parts[2], *others) if others else parts[2]
    return [*parts[:2], across, swap(across, CORE)]


def scatter_direct(parts):
    return [parts[0]] + [swap(parts[j], j) for j in range(1, len(parts))]


def thirds(value):
    high = value.astype(LOW)
    rest = value - high.astype(F32)
    mid = rest.astype(LOW)
    return high, mid, (rest - mid.astype(F32)).astype(LOW)


def place(base, lane, first, pieces):
    for offset, piece in enumerate(pieces):
        base = jnp.where(lane == first + offset, piece, base)
    return base


def norm(values):
    mean = jnp.mean(values, axis=-1, keepdims=True)
    centred = values - mean
    spread = jnp.mean(centred * centred, axis=-1, keepdims=True)
    scaler = lax.rsqrt(spread + 1e-05)
    return centred * scaler, scaler


def norm_back(grad, unit, scaler, gain):
    scaled = grad * gain
    return scaler * (
        scaled
        - jnp.mean(scaled, axis=-1, keepdims=True)
        - unit * jnp.mean(scaled * unit, axis=-1, keepdims=True)
    )


def present(value, count):
    if count == value.shape[0]:
        return value
    row = lax.broadcasted_iota(jnp.int32, value.shape, 0)
    return jnp.where(row < count, value.astype(F32), 0.0).astype(value.dtype)


def pick(step, refs, rows, count):
    size = refs[0].shape[0]
    slots = rows.shape[0] // size
    for turn in range(len(refs) // slots):

        @pl.when(step == turn)
        def _():
            for at in range(slots):
                block = present(refs[turn * slots + at][...], count)
                rows[at * size : (at + 1) * size] = block


def stack_kernel(*refs):
    vec_ref, bias_ref = refs[-2:]
    for index, ref in enumerate(refs[:7]):
        vec_ref[index : index + 1] = ref[...].astype(F32).reshape(1, -1)
    bias_ref[...] = jnp.zeros_like(bias_ref)
    for index, ref in ((0, refs[7]), (2, refs[8])):
        bias_ref[index : index + 1] = ref[...].astype(F32).reshape(1, -1)


def project_kernel(share, slots, aliased, *refs):
    x_refs = refs[:slots]
    vec_ref, bias_ref, wq_ref, wk_ref, wv_ref = refs[slots : slots + 5]
    n_ref, q_ref, k_ref, v_ref, rows, w_tiles, b_tiles = refs[slots + 5 + aliased :]
    half = pl.program_id(0)
    heads = q_ref.shape[0]
    size = x_refs[0].shape[0]

    @pl.when(half == 0)
    def _():
        w_tiles[...] = jnp.zeros_like(w_tiles)
        b_tiles[...] = jnp.zeros_like(b_tiles)
        spot = lax.broadcasted_iota(jnp.int32, (1, LANES), 1) - HEAD_DIM
        ones = (
            jnp.where(spot == 0, HEAD_DIM**0.5, 0.0),
            jnp.where((spot >= 1) & (spot <= 3), 1.0, 0.0),
            jnp.where((spot >= 0) & (spot <= 2), 1.0, 0.0),
        )
        for which, w_ref in enumerate((wq_ref, wk_ref, wv_ref)):
            for head in range(heads):
                at = (which * heads + head) * LANES
                own = slice(head * HEAD_DIM, (head + 1) * HEAD_DIM)
                w_tiles[at : at + HEAD_DIM] = w_ref[own]
                b_tiles[:, at : at + LANES] = ones[which]
                b_tiles[:, at : at + HEAD_DIM] = bias_ref[which : which + 1, own]

    row = lax.broadcasted_iota(jnp.int32, (size, rows.shape[1]), 0) + half * size
    for at in range(slots):
        block = jnp.where(row < share, x_refs[at][...].astype(F32), 0.0)
        rows[at * size : (at + 1) * size] = block
    unit, _ = norm(rows[...])
    normed = (unit * vec_ref[0:1] + vec_ref[1:2]).astype(LOW)
    n_ref[...] = normed
    out = lax.dot_general(normed, w_tiles[...], NT, preferred_element_type=F32) + b_tiles[...]
    row = lax.broadcasted_iota(jnp.int32, (out.shape[0], LANES), 0)
    lane = lax.broadcasted_iota(jnp.int32, (out.shape[0], LANES), 1)
    absent = (lax.rem(row, size) + half * size >= share) & (lane == HEAD_DIM)
    scale = HEAD_DIM ** (-0.5)
    for head in range(heads):
        part = lambda which: out[:, (which * heads + head) * LANES :][:, :LANES]
        q_ref[head] = (part(0).astype(LOW).astype(F32) * scale).astype(LOW)
        k_ref[head] = jnp.where(absent, MASK, part(1)).astype(LOW)
        v_ref[head] = part(2).astype(LOW)


def attend_kernel(aliased, slots, q_ref, k_ref, v_ref, *refs):
    o_ref, full_ref, q_out = refs[aliased:]
    heads, block, _ = q_ref.shape
    quarter = block // slots // 2
    lane = lax.broadcasted_iota(jnp.int32, (block, LANES), 1)
    for head in range(heads):
        query = q_ref[head]
        scores = lax.dot_general(query, k_ref[head], NT, preferred_element_type=F32)
        top = jnp.max(scores, axis=-1, keepdims=True)
        weights = jnp.exp(scores - top).astype(LOW)
        out = jnp.dot(weights, v_ref[head], preferred_element_type=F32)
        total = out[:, HEAD_DIM : HEAD_DIM + 1]
        out = out / total
        full_ref[:, head * LANES : (head + 1) * LANES] = out
        low = out[:, :HEAD_DIM].astype(LOW)
        for part in range(2 * slots):
            at = ((part % 2) * heads + head) * HEAD_DIM
            o_ref[part // 2 * quarter : (part // 2 + 1) * quarter, at : at + HEAD_DIM] = low[
                part * quarter : (part + 1) * quarter
            ]
        logsum = top + jnp.log(total)
        q_out[head] = place(query, lane, HEAD_DIM + 1, thirds(-logsum))


def feed_kernel(half, share, group, aliased, *refs):
    x_refs, m_refs, wo_refs = refs[:group], refs[group : 3 * group], refs[3 * group : 4 * group]
    g_refs = refs[4 * group : 5 * group]
    vec_ref, w1_ref, w2_ref = refs[5 * group : 5 * group + 3]
    old = refs[5 * group + 3 : 5 * group + 3 + half]
    outs = refs[5 * group + 3 + half + aliased :]
    h_ref, n_ref, a_ref, p_ref, c_ref, db_ref = outs[:6]
    d_refs = outs[6 : 6 + group]
    rows, mixed, wo_all = outs[6 + group :]
    step = pl.program_id(0)
    size = x_refs[0].shape[0]
    slots = rows.shape[0] // size
    quarter = size // 2
    count = min(size, share - half * size)
    pick(step, x_refs, rows, count)
    pick(step, g_refs, c_ref, count)
    local = wo_refs[0].shape[0]
    for source in range(group):
        for at in range(slots):
            packed = m_refs[source * slots + at][...]
            for part in range(2):
                first = at * size + part * quarter
                mixed[first : first + quarter, source * local : (source + 1) * local] = packed[
                    :, part * local : (part + 1) * local
                ]

    @pl.when(step == 0)
    def _():
        for source in range(group):
            wo_all[source * local : (source + 1) * local] = wo_refs[source][...]

    branch = jnp.dot(mixed[...], wo_all[...], preferred_element_type=F32)
    hidden = rows[...].astype(F32) + branch + vec_ref[2:3]

    @pl.when(step == 0)
    def _():
        h_ref[...] = hidden[:size]
        db_ref[...] = old[0][...] if old else jnp.zeros_like(db_ref)

    unit, _ = norm(hidden)
    normed = (unit * vec_ref[3:4] + vec_ref[4:5]).astype(LOW)
    n_ref[...] = normed
    pre = jnp.dot(normed, w1_ref[...], preferred_element_type=F32) + vec_ref[5:6]
    active_grad = lax.dot_general(c_ref[...], w2_ref[...], NT, preferred_element_type=F32)
    size_of = jnp.abs(pre)
    bell = jnp.exp(-0.5 * pre * pre)
    t = 1.0 / (1.0 + (0.3275911 * 0.5**0.5) * size_of)
    poly = t * (
        0.127414796 + t * (-0.142248368 + t * (0.7107068705 + t * (-0.7265760135 + t * 0.5307027145)))
    )
    tail = poly * bell
    gate = jnp.where(pre >= 0, 1.0 - tail, tail)
    a_ref[...] = (pre * gate).astype(LOW)
    pre_grad = active_grad * (gate + pre * bell * 0.3989422804014327)
    db_ref[...] += jnp.sum(pre_grad, axis=0, keepdims=True)
    pre_low = pre_grad.astype(LOW)
    p_ref[...] = pre_low
    back = lax.dot_general(pre_low, w1_ref[...], NT, preferred_element_type=F32).astype(LOW)
    for turn in range(group // slots):

        @pl.when(step == turn)
        def _():
            for at in range(slots):
                d_refs[turn * slots + at][...] = back[at * size : (at + 1) * size]


def middle_kernel(count, terms, h_ref, g_ref, vec_ref, *refs):
    out_ref, low_ref, sums_ref = refs[-3:]
    grad = sum(ref[...].astype(F32) for ref in refs[:terms])
    unit, scaler = norm(h_ref[...])
    cot = present(g_ref[...], count).astype(F32)
    hidden_grad = cot + norm_back(grad, unit, scaler, vec_ref[3:4])
    out_ref[...] = hidden_grad
    low_ref[...] = hidden_grad.astype(LOW)
    add = lambda value: jnp.sum(value, axis=0, keepdims=True)
    sums = jnp.concatenate([add(grad * unit), add(grad), add(hidden_grad), add(cot)], axis=0)
    sums_ref[...] = sum((ref[...] for ref in refs[terms:-3]), sums)


def attend_back_kernel(parts, head, heads, orders, *refs):
    h_refs = refs[:parts]
    full_ref, q_ref, k_ref, v_ref, wo_ref, n_ref, wq_ref, wk_ref, wv_ref = refs[parts : parts + 9]
    at = parts + 9
    last = head == heads - 1
    if head:
        old_ref = refs[at]
        at += 1
    if last:
        me_ref, vec_ref, sums_ref, db_ref = refs[at : at + 4]
        done_refs = refs[at + 4 : at + 3 + heads]
        at += 3 + heads
    grad_ref, small_ref = refs[at : at + 2]
    outs = refs[at + 2 : -7]
    rows, wo_tile, w_stack, kt_ref, dk_sum, dv_sum, dw_sum = refs[-7:]
    step = pl.program_id(0)
    _, block, _ = q_ref.shape
    own = [slice(which * HEAD_DIM, (which + 1) * HEAD_DIM) for which in range(4)]

    @pl.when(step == 0)
    def _():
        size = h_refs[0].shape[0]
        for part in range(parts):
            rows[part * size : (part + 1) * size] = h_refs[part][...]
        wo_tile[:HEAD_DIM] = wo_ref[...]
        wo_tile[HEAD_DIM:] = jnp.zeros_like(wo_tile[HEAD_DIM:])
        for which, w_ref in enumerate((wq_ref, wk_ref, wv_ref)):
            w_stack[own[which]] = w_ref[...]
        for total in (dk_sum, dv_sum, dw_sum):
            total[...] = jnp.zeros_like(total)
        kt_ref[...] = k_ref[0].astype(F32).T[:HEAD_DIM].astype(LOW)

    scale = HEAD_DIM ** (-0.5)
    lane = lax.broadcasted_iota(jnp.int32, (block, LANES), 1)
    here = pl.ds(pl.multiple_of(step * block, block), block)
    hidden_grad = rows[here]
    full = full_ref[...]
    out_grad = lax.dot_general(hidden_grad, wo_tile[...], NT, preferred_element_type=F32)
    out_grad = out_grad.astype(LOW)
    dw_sum[...] += lax.dot_general(
        full.astype(LOW), hidden_grad, (((0,), (0,)), ((), ())), preferred_element_type=F32
    )
    delta = jnp.sum(out_grad.astype(F32) * full, axis=-1, keepdims=True)
    out_grad = place(out_grad, lane, HEAD_DIM, thirds(-delta))
    query = q_ref[0]
    scores = lax.dot_general(k_ref[0], query, NT, preferred_element_type=F32)
    probs = jnp.exp(scores)
    prob_grad = lax.dot_general(v_ref[0], out_grad, NT, preferred_element_type=F32)
    score_grad = (probs * prob_grad).astype(LOW)
    dv_sum[...] += jnp.dot(probs.astype(LOW), out_grad, preferred_element_type=F32)
    dk_sum[...] += jnp.dot(score_grad, query, preferred_element_type=F32)
    turned = jnp.dot(kt_ref[...], score_grad, preferred_element_type=F32)
    grad_ref[here, own[0]] = (turned.T * scale).astype(LOW)

    @pl.when(step == pl.num_programs(0) - 1)
    def _():
        grad_ref[:, own[1]] = dk_sum[:, :HEAD_DIM].astype(LOW)
        grad_ref[:, own[2]] = dv_sum[:, :HEAD_DIM].astype(LOW)
        grads = grad_ref[...]
        weight_grad = lax.dot_general(
            grads, n_ref[...], (((0,), (0,)), ((), ())), preferred_element_type=F32
        )
        weights = w_stack[...].astype(F32)
        totals = jnp.sum(grads.astype(F32), axis=0, keepdims=True)
        gain = jnp.sum(weights * weight_grad, axis=0, keepdims=True)
        shift = jnp.dot(
            totals, weights, precision=lax.Precision.HIGHEST, preferred_element_type=F32
        )
        if head:
            gain += old_ref[0:1]
            shift += old_ref[1:2]
            small_ref[6:7] = old_ref[6:7]
        else:
            small_ref[...] = jnp.zeros_like(small_ref)
        local = heads * HEAD_DIM
        for which, first in ((0, 0), (2, local)):
            start = first + head * HEAD_DIM
            small_ref[6:7, start : start + HEAD_DIM] = totals[:, own[which]]
        small_ref[1:2] = shift
        if not last:
            small_ref[0:1] = gain
            outs[0][: 3 * HEAD_DIM] = weight_grad
            outs[0][3 * HEAD_DIM :] = dw_sum[:HEAD_DIM]
            return
        small_ref[0:1] = (gain - vec_ref[1:2] * shift) / vec_ref[0:1]
        small_ref[2:6] = sums_ref[...]
        small_ref[7:8] = db_ref[...]
        stacks = outs[-1]
        for which in range(4):
            for index, done in enumerate(done_refs):
                start = which * local + index * HEAD_DIM
                stacks[start : start + HEAD_DIM] = done[own[which]]
            start = which * local + head * HEAD_DIM
            value = weight_grad[own[which]] if which < 3 else dw_sum[:HEAD_DIM]
            stacks[start : start + HEAD_DIM] = value
        if orders is None:
            outs[0][...] = stacks[: 2 * local].astype(LOW)
            outs[1][...] = stacks[2 * local :].astype(LOW)
            return
        for stack, order in enumerate(orders):
            size = 2 * local // len(order)
            for spot, slot in enumerate(order):
                which, index = divmod(spot, len(order) // 2)
                start = stack * 2 * local + jnp.bitwise_xor(me_ref[0], slot) * size
                piece = stacks[pl.ds(pl.multiple_of(start, size), size)]
                outs[2 * stack + which][index * size : (index + 1) * size] = piece.astype(LOW)


def outer_kernel(order, me_ref, left_ref, right_ref, keep_ref, send_ref, total):
    step = pl.program_id(0)

    @pl.when(step == 0)
    def _():
        total[...] = jnp.zeros_like(total)

    total[...] += lax.dot_general(
        left_ref[...], right_ref[...], (((0,), (0,)), ((), ())), preferred_element_type=F32
    )

    @pl.when(step == pl.num_programs(0) - 1)
    def _():
        size = total.shape[0] // len(order)
        for spot, slot in enumerate(order):
            which, at = divmod(spot, len(order) // 2)
            start = jnp.bitwise_xor(me_ref[0], slot) * size
            piece = total[pl.ds(pl.multiple_of(start, size), size)].astype(LOW)
            (keep_ref, send_ref)[which][at * size : (at + 1) * size] = piece


def settle_kernel(orders, me_ref, *refs):
    outs = refs[2 * len(orders) :]
    sides = len(outs) // len(orders)
    for stack, order in enumerate(orders):
        halves = refs[2 * stack : 2 * stack + 2]
        size = 2 * halves[0].shape[0] // len(order)
        per = len(order) // sides
        for spot, slot in enumerate(order):
            which, at = divmod(spot, len(order) // 2)
            value = halves[which][at * size : (at + 1) * size].astype(F32)
            place_at = jnp.bitwise_xor(me_ref[0], slot)
            start = pl.multiple_of(lax.rem(place_at, per) * size, size)
            for side in range(sides):

                @pl.when(lax.div(place_at, per) == side)
                def _():
                    outs[sides * stack + side][pl.ds(start, size)] = value


def spread_kernel(heads, *refs):
    grads, weights, outs = refs[:heads], refs[heads : heads + 3], refs[heads + 3 : -1]
    w_stacks = refs[-1]
    step = pl.program_id(0)

    @pl.when(step == 0)
    def _():
        for head in range(heads):
            for which, w_ref in enumerate(weights):
                start = (head * 3 + which) * HEAD_DIM
                w_stacks[start : start + HEAD_DIM] = w_ref[
                    head * HEAD_DIM : (head + 1) * HEAD_DIM
                ]

    each = 3 * HEAD_DIM
    total = sum(
        jnp.dot(
            grads[head][...],
            w_stacks[head * each : (head + 1) * each],
            preferred_element_type=F32,
        )
        for head in range(heads)
    ).astype(LOW)
    size = outs[0].shape[0]
    slots = total.shape[0] // size
    for turn in range(len(outs) // slots):

        @pl.when(step == turn)
        def _():
            for at in range(slots):
                outs[turn * slots + at][...] = total[at * size : (at + 1) * size]


def last_kernel(aliased, x_ref, d0_ref, d1_ref, d2_ref, h_ref, vec_ref, *refs):
    out_ref = refs[aliased]
    grad = d0_ref[...].astype(F32) + d1_ref[...].astype(F32) + d2_ref[...].astype(F32)
    unit, scaler = norm(x_ref[...].astype(F32))
    out_ref[...] = (h_ref[...] + norm_back(grad, unit, scaler, vec_ref[0:1])).astype(LOW)


def output_kernel(ha_ref, hb_ref, vec_ref, *refs):
    out_ref = refs[-1]
    size = ha_ref.shape[0]
    share = out_ref.shape[0]
    for part, h_ref in enumerate((ha_ref, hb_ref)):
        mlp = sum(ref[part].astype(F32) for ref in refs[:-1])
        value = (h_ref[...] + mlp + vec_ref[6:7]).astype(LOW)
        count = min(size, share - part * size)
        out_ref[part * size : part * size + count] = value[:count]


def pair(value, axis, step):
    size = lax.axis_size(axis)
    return lax.ppermute(value, axis, [(i, i ^ step) for i in range(size)])


def sum_over(value, axis):
    size = lax.axis_size(axis)
    if size & (size - 1):
        return lax.psum(value, axis)
    step = 1
    while step < size:
        value = value + pair(value, axis, step)
        step *= 2
    return value


def exchange_order(bits):
    order = [0]
    for bit in reversed(bits):
        order = order + [slot | bit for slot in order]
    return order


def halve(parts, axis, bit):
    keep, send = parts
    return tuple(jnp.split(keep + pair(send, axis, bit), 2))


def on_device(
    features, cotangent, w_query, bias_query, w_key, w_value, bias_value, w_out, bias_out,
    norm1_gain, norm1_bias, norm2_gain, norm2_bias, w_fc1, bias_fc1, w_fc2, bias_fc2,
):
    _, share, width = features.shape
    local = w_query.shape[1]
    heads = local // HEAD_DIM
    hidden = w_fc1.shape[1]
    group = lax.axis_size("tensor")
    clips = lax.axis_size("dp")
    rows = -(-share // LANES) * LANES
    size = rows // 2
    frames = group * rows
    part_rows = group * size
    slots = 2
    block = slots * size
    steps = group // slots
    shape = jax.ShapeDtypeStruct
    halves = range(2)
    count = lambda half: min(size, share - half * size)

    x_own, g_own = features[0], cotangent[0]
    x_all = gather(x_own)
    wo_all = gather(after(w_out, x_all[2]))
    g_all = gather(after(g_own, x_all[2]))
    vectors, biases = pl.pallas_call(
        stack_kernel,
        out_shape=[shape((7, width), F32), shape((3, local), F32)],
        compiler_params=params(2),
        cost_estimate=cost(0, 12 * width * 8),
        name="stack",
    )(
        norm1_gain, norm1_bias, bias_out, norm2_gain, norm2_bias, bias_fc1, bias_fc2,
        bias_query, bias_value,
    )
    turned = [w_query.T, w_key.T, w_value.T]

    slot_spec = whole((size, width))
    turned_spec = whole((local, width))
    any_spec = pl.BlockSpec(memory_space=pl.ANY)
    at_half = lambda half, n: pl.BlockSpec((block, n), lambda i: (half * steps + i, 0))
    own_half = lambda half: pl.BlockSpec((size, width), lambda *_: (half, 0))
    head_half = lambda half: pl.BlockSpec((heads, block, LANES), lambda i: (0, half * steps + i, 0))
    head_shape = shape((heads, frames, LANES), LOW)

    made = []
    for turn in range(steps):
        if turn:
            x_all = finish(x_all, made[0])
        made = pl.pallas_call(
            functools.partial(project_kernel, share, slots, len(made)),
            grid=(2,),
            in_specs=[pl.BlockSpec((size, width), lambda i: (i, 0))] * slots
            + [whole(vectors.shape), whole(biases.shape)]
            + [turned_spec] * 3
            + [any_spec] * len(made),
            out_specs=[pl.BlockSpec((block, width), lambda i, turn=turn: (i * steps + turn, 0))]
            + [
                pl.BlockSpec((heads, block, LANES), lambda i, turn=turn: (0, i * steps + turn, 0))
            ]
            * 3,
            out_shape=[shape((frames, width), LOW)] + [head_shape] * 3,
            scratch_shapes=[
                pltpu.VMEM((block, width), F32),
                pltpu.VMEM((3 * heads * LANES, width), LOW),
                pltpu.VMEM((1, 3 * heads * LANES), F32),
            ],
            input_output_aliases={slots + 5 + i: i for i in range(len(made))},
            compiler_params=params(16, 1),
            cost_estimate=cost(2 * part_rows * width * 9 * LANES, 6_000_000),
            name="project",
        )(*x_all[turn * slots : (turn + 1) * slots], vectors, biases, *turned, *made)
    normed1, query, key, value = made

    head_whole = whole((heads, frames, LANES))
    made, packed = [], []
    for half in halves:
        made = pl.pallas_call(
            functools.partial(attend_kernel, len(made), slots),
            grid=(steps,),
            in_specs=[head_half(half), head_whole, head_whole] + [any_spec] * len(made),
            out_specs=[
                pl.BlockSpec((block // 2, 2 * local), lambda i: (i, 0)),
                at_half(half, heads * LANES), head_half(half),
            ],
            out_shape=[
                shape((part_rows // 2, 2 * local), LOW), shape((frames, heads * LANES), F32),
                head_shape,
            ],
            input_output_aliases={3 + i: 1 + i for i in range(len(made))},
            compiler_params=params(24, 1),
            cost_estimate=cost(
                2 * heads * frames * frames * 256, 5_000_000, heads * frames * frames // 2
            ),
            name="attend",
        )(query, key, value, *made)
        packed.append(gather(made[0]))
        made = made[1:]
        if half == 0:
            g_all = finish(g_all, made[0])
            wo_all = finish(wo_all, made[0])
    mixed_full, query_back = made
    packed[0] = finish(packed[0], mixed_full)

    low_rows = shape((frames, hidden), LOW)
    made, hidden1, fc1_bias_grad, normed2_parts = [], [], [], []
    for half in halves:
        if half:
            packed[half] = finish(packed[half], made[0])
        sources = packed[half]
        packed_specs, packed_args = [], []
        for source in range(group):
            for at in range(slots):
                packed_args.append(sources[source])
                packed_specs.append(
                    pl.BlockSpec(
                        (size // 2, 2 * local),
                        lambda i, source=source, at=at: ((i * slots + at) ^ source, 0),
                    )
                )
        made = pl.pallas_call(
            functools.partial(feed_kernel, half, share, group, len(made)),
            grid=(steps,),
            in_specs=[own_half(half)] * group
            + packed_specs
            + [whole((local, width))] * group
            + [own_half(half)] * group
            + [whole(vectors.shape), whole((width, hidden)), whole((hidden, width))]
            + [whole((1, hidden))] * half
            + [any_spec] * len(made),
            out_specs=[slot_spec]
            + [at_half(half, n) for n in (width, hidden, hidden, width)]
            + [whole((1, hidden))]
            + [slot_spec] * group,
            out_shape=[
                shape((size, width), F32), shape((frames, width), LOW), low_rows, low_rows,
                shape((frames, width), LOW), shape((1, hidden), F32),
            ]
            + [shape((size, width), LOW)] * group,
            scratch_shapes=[pltpu.VMEM((block, width), LOW)] * 2
            + [pltpu.VMEM((width, width), LOW)],
            input_output_aliases={5 * group + 3 + half + i: 1 + i for i in range(len(made))},
            compiler_params=params(28, 1),
            cost_estimate=cost(4 * frames * width * hidden, 12_000_000, frames * hidden // 2),
            name="feed",
        )(
            *x_all, *packed_args, *wo_all, *g_all, vectors, w_fc1, w_fc2,
            *fc1_bias_grad, *made
        )
        hidden1.append(made[0])
        fc1_bias_grad = [made[5]]
        normed2_parts.append(made[6:])
        made = made[1:5]
    normed2, active, pre_low, cot_rows = made

    hidden1_grad, sums2, hidden1_rows = [], [], []
    far = normed2_parts[1][2] + swap(normed2_parts[1][3], CORE)
    all_terms = [
        scatter_direct(normed2_parts[0]),
        [normed2_parts[1][0], swap(normed2_parts[1][1], CORE), swap(far, CHIP)],
    ]
    for half in halves:
        terms = all_terms[half]
        if half:
            terms[0] = after(terms[0], hidden1_rows[0][2])
        grad, low, sums = pl.pallas_call(
            functools.partial(middle_kernel, count(half), len(terms)),
            grid=(1,),
            in_specs=[slot_spec, own_half(half), whole(vectors.shape)]
            + [slot_spec] * len(terms)
            + [whole((4, width))] * half,
            out_specs=[slot_spec, slot_spec, whole((4, width))],
            out_shape=[
                shape((size, width), F32), shape((size, width), LOW), shape((4, width), F32),
            ],
            compiler_params=params(8, 1),
            cost_estimate=cost(20 * size * width, 16 * size * width),
            name="middle",
        )(hidden1[half], g_own, vectors, *terms, *sums2)
        hidden1_grad.append(grad)
        sums2 = [sums]
        hidden1_rows.append(gather(low if half else after(low, far)))

    tn = lambda left, right: lax.dot_general(
        left, right, (((0,), (0,)), ((), ())), preferred_element_type=F32
    )
    low_ready = hidden1_rows[0][0]
    active = after(active, low_ready)
    mlp_part = jnp.dot(active, w_fc2, preferred_element_type=F32).astype(LOW)
    mlp_part = mlp_part.reshape(2, group, size, width)
    me = lax.axis_index("dp").astype(jnp.int32).reshape(1)
    me_spec = pl.BlockSpec(memory_space=pltpu.SMEM)
    bits = ((1, 2, 4), (2, 1, 4)) if clips == 8 else None
    orders = [exchange_order(order) for order in bits] if bits else None
    hidden1_rows[0] = finish(hidden1_rows[0])
    hidden1_rows[1].append(swap(hidden1_rows[1][0], CORE | CHIP))
    if bits:
        fc = []
        normed2 = after(normed2, low_ready)
        for index, (left, right) in enumerate(((active, cot_rows), (normed2, pre_low))):
            if index:
                left = after(left, fc[0][1], mlp_part, all_terms[1][2])
            fc.append(
                pl.pallas_call(
                    functools.partial(outer_kernel, orders[index]),
                    grid=(2,),
                    in_specs=[me_spec]
                    + [
                        pl.BlockSpec((part_rows, part.shape[1]), lambda i: (i, 0))
                        for part in (left, right)
                    ],
                    out_specs=[whole((left.shape[1] // 2, right.shape[1]))] * 2,
                    out_shape=[shape((left.shape[1] // 2, right.shape[1]), LOW)] * 2,
                    scratch_shapes=[pltpu.VMEM((left.shape[1], right.shape[1]), F32)],
                    compiler_params=params(24, 1),
                    cost_estimate=cost(2 * frames * width * hidden, 8_000_000),
                    name="outer",
                )(me, left, right)
            )
        fc = [halve(fc[index], "dp", bits[index][0]) for index in range(2)]
        fc = [halve(fc[index], "dp", bits[index][1]) for index in range(2)]
        fc_keep, fc_send = [jnp.concatenate(pieces) for pieces in zip(*fc)]
        hidden1_rows[0][0] = after(hidden1_rows[0][0], fc_keep, fc_send)
    else:
        fc_own = (tn(active, cot_rows).astype(LOW), tn(normed2, pre_low).astype(LOW))
        fc2_grad, fc1_grad = [total.astype(F32) for total in lax.psum(fc_own, "dp")]
    mlp_far = mlp_part[:, 2] + swap(mlp_part[:, 3], CORE)
    mlp = [mlp_part[:, 0], mlp_part[:, 1], mlp_far]
    hidden1_rows[0][0] = after(hidden1_rows[0][0], *mlp)
    back = 512
    each = 3 * HEAD_DIM
    stack_rows = [local] * 4 if bits else [2 * local] * 2
    all_rows = hidden1_rows[0] + hidden1_rows[1]
    head_row = lambda head: pl.BlockSpec((HEAD_DIM, width), lambda i: (head, 0))
    head_tile = lambda head: pl.BlockSpec((1, frames, LANES), lambda i: (head, 0, 0))
    small_shape, done_shape = shape((8, width), F32), shape((4 * HEAD_DIM, width), F32)
    grads, dones, small = [], [], []
    for head in range(heads):
        last = head == heads - 1
        if head == 1:
            mlp = scatter_direct([after(part, grads[0]) for part in mlp])
            if bits:
                f = fc_keep + pair(fc_send, "dp", bits[0][2])
                all_rows[0] = after(all_rows[0], f)
        if last:
            all_rows[0] = after(all_rows[0], *mlp[1:])
            if bits:
                got = pair(f, "dp", bits[0][2])
                f = [jnp.concatenate(both) for both in zip(jnp.split(f, 2), jnp.split(got, 2))]
                all_rows[0] = after(all_rows[0], *f)
        specs = [slot_spec] * len(all_rows) + [
            pl.BlockSpec((back, LANES), lambda i, head=head: (i, head)),
            pl.BlockSpec((1, back, LANES), lambda i, head=head: (head, i, 0)),
            head_tile(head), head_tile(head), head_row(head), whole((frames, width)),
            *[head_row(head)] * 3,
        ]
        args = [*all_rows, mixed_full, query_back, key, value, w_out, normed1, *turned]
        if head:
            specs += [whole((8, width))]
            args += small
        out_shape = [shape((frames, each), LOW), small_shape]
        scratch = [
            pltpu.VMEM((frames, width), LOW), pltpu.VMEM((LANES, width), LOW),
            pltpu.VMEM((each, width), LOW), pltpu.VMEM((HEAD_DIM, frames), LOW),
            pltpu.VMEM((frames, LANES), F32), pltpu.VMEM((frames, LANES), F32),
            pltpu.VMEM((LANES, width), F32),
        ]
        if last:
            specs += [me_spec, whole(vectors.shape), whole((4, width)), whole((1, hidden))]
            specs += [whole(done_shape.shape)] * len(dones)
            args += [me, vectors, *sums2, *fc1_bias_grad, *dones]
            out_shape += [shape((n, width), LOW) for n in stack_rows]
            scratch.insert(0, pltpu.VMEM((4 * local, width), F32))
        else:
            out_shape += [done_shape]
        grad, total, *rest = pl.pallas_call(
            functools.partial(attend_back_kernel, len(all_rows), head, heads, orders),
            grid=(frames // back,),
            in_specs=specs,
            out_specs=[whole(out.shape) for out in out_shape],
            out_shape=out_shape,
            scratch_shapes=scratch,
            compiler_params=params(36, 1),
            cost_estimate=cost(10 * frames * frames * 256, 8_000_000, frames * frames),
            name="attend_back",
        )(*args)
        grads.append(grad)
        small = [total]
        if last:
            stacks = rest
        else:
            dones += rest
            all_rows[1] = after(all_rows[1], total)
    small = small[0]
    if bits:
        f = [
            jnp.concatenate([part, pair(part, "dp", bits[index][1])])
            for index, part in enumerate(f)
        ]
        grads[0] = after(grads[0], *f)

    block_rows = lambda n: pl.BlockSpec((block, n), lambda i: (i, 0))
    normed1_parts = pl.pallas_call(
        functools.partial(spread_kernel, heads),
        grid=(2 * steps,),
        in_specs=[block_rows(each)] * heads + [turned_spec] * 3,
        out_specs=[slot_spec] * (2 * group),
        out_shape=[shape((size, width), LOW)] * (2 * group),
        scratch_shapes=[pltpu.VMEM((heads * each, width), LOW)],
        compiler_params=params(16, 1),
        cost_estimate=cost(2 * frames * width * 3 * local, 6_000_000),
        name="spread",
    )(*grads, *turned)
    parts = [normed1_parts[half * group : (half + 1) * group] for half in halves]

    def settle(ends, order, count, size):
        return pl.pallas_call(
            functools.partial(settle_kernel, order),
            in_specs=[me_spec] + [pl.BlockSpec(memory_space=pltpu.VMEM)] * len(ends),
            out_shape=[shape((size, width), F32)] * count,
            compiler_params=params(12),
            cost_estimate=cost(0, 6 * count * size * width),
            name="settle",
        )(me, *ends)

    hop = lambda value, bit: pair(value, "dp", bit)
    side = lambda index, turn: bits[index][turn]
    join = lambda *values: jnp.concatenate(values)
    together = lambda *values: lax.optimization_barrier(values)
    if bits:
        q = [(stacks[0], stacks[1]), (stacks[2], stacks[3])]
        got = together(
            hop(q[0][1], side(0, 0)), hop(q[1][1], side(1, 0)), hop(small, 1), parts[0][0]
        )
        f_last = [hop(f[0], side(0, 0)), hop(f[1], side(1, 0))]
        q = [tuple(jnp.split(q[i][0] + got[i], 2)) for i in range(2)]
        small = small + got[2]
        got = together(hop(q[0][1], side(0, 1)), hop(q[1][1], side(1, 1)))
        rest = join(*[q[i][0] + got[i] for i in range(2)])
        small = after(small, rest)
        parts = [[after(part, rest) for part in own] for own in parts]
        got = together(
            hop(rest, side(0, 2)), hop(small, 2), *f_last,
            *[swap(parts[half][j], CORE) for half in halves for j in (3, 1)],
        )
        quarters = jnp.split(got[0], 4)
        rest = rest + join(quarters[1], quarters[0], quarters[3], quarters[2])
        q, small, f_last = jnp.split(rest, 2), small + got[1], got[2:4]
        beside = [got[5], got[7]]
        far = [swap(parts[half][2] + got[4 + 2 * half], CHIP) for half in halves]
        got = together(hop(q[0], side(0, 1)), hop(q[1], side(1, 1)), hop(small, 4))
        q = [join(q[i], got[i]) for i in range(2)]
        small = small + got[2]
        ends = [q[0], hop(q[0], side(0, 0)), q[1], hop(q[1], side(1, 0))]
        shared = small + swap(small, CORE)
        shared = shared + swap(shared, CHIP)
        (fc2_grad,) = settle([f[0], f_last[0]], orders[:1], 1, hidden)
        (fc1_grad,) = settle([f[1], f_last[1]], orders[1:], 1, hidden)
        grads = settle(ends, orders, 4, local)
    else:
        grads = jnp.concatenate(lax.psum(tuple(stacks), "dp")).astype(F32)
        grads = jnp.split(grads, 4)
        small = sum_over(small, "dp")
        shared = sum_over(small, "tensor")
        beside = [swap(part[1], CORE) for part in parts]
        far = [swap(part[2] + swap(part[3], CORE), CHIP) for part in parts]

    layer_out = pl.pallas_call(
        output_kernel,
        out_shape=shape((share, width), LOW),
        compiler_params=params(12),
        cost_estimate=cost(8 * rows * width, 12 * rows * width),
        name="output",
    )(*hidden1, vectors, *mlp)

    features_grad = []
    for half in halves:
        features_grad = [
            pl.pallas_call(
                functools.partial(last_kernel, len(features_grad)),
                grid=(1,),
                in_specs=[own_half(half)]
                + [slot_spec] * 4
                + [whole(vectors.shape)]
                + [any_spec] * len(features_grad),
                out_specs=own_half(half),
                out_shape=shape((share, width), LOW),
                input_output_aliases={6: 0} if features_grad else {},
                compiler_params=params(8, 1),
                cost_estimate=cost(20 * size * width, 14 * size * width),
                name="last",
            )(
                x_own,
                parts[half][0],
                beside[half],
                far[half],
                hidden1_grad[half],
                vectors,
                *features_grad,
            )
        ]
    return (
        layer_out[None],
        features_grad[0][None],
        grads[0].T,
        small[6, :local],
        grads[1].T,
        grads[2].T,
        small[6, local : 2 * local],
        grads[3],
        shared[4],
        shared[0],
        shared[1],
        shared[2],
        shared[3],
        fc1_grad,
        small[7],
        fc2_grad,
        shared[5],
    )


def solution(mesh):
    rows = P("dp", "tensor", None)
    columns, lines, vector, same = P(None, "tensor"), P("tensor", None), P("tensor"), P()
    in_specs = (
        rows, rows, columns, vector, columns, columns, vector, lines, same,
        same, same, same, same, columns, vector, lines, same,
    )
    out_specs = (
        rows, rows, columns, vector, columns, columns, vector, lines, same,
        same, same, same, same, columns, vector, lines, same,
    )
    return jax.shard_map(
        on_device, mesh=mesh, in_specs=in_specs, out_specs=out_specs, check_vma=False
    )
```

```python
import functools

import jax
import jax.numpy as jnp
from jax import lax
from jax.experimental import pallas as pl
from jax.experimental.pallas import tpu as pltpu
from jax.sharding import PartitionSpec as P

HEAD_DIM = 64
LANES = 128
F32 = jnp.float32
LOW = jnp.bfloat16
MASK = -1e30
CORE, CHIP = 1, 2
MIB = 1024 * 1024
NT = (((1,), (1,)), ((), ()))


def params(room, steps=0):
    semantics = ("arbitrary",) * steps if steps else None
    return pltpu.CompilerParams(vmem_limit_bytes=room * MIB, dimension_semantics=semantics)


def cost(flops, moved, exps=0):
    return pl.CostEstimate(
        flops=flops // 4, bytes_accessed=moved // 4, transcendentals=exps // 4
    )


def whole(shape):
    return pl.BlockSpec(shape, lambda *_: (0,) * len(shape))


def swap(value, partner):
    size = lax.axis_size("tensor")
    return lax.ppermute(value, "tensor", [(i, i ^ partner) for i in range(size)])


def after(value, *others):
    return lax.optimization_barrier((value, *others))[0]


def gather(own):
    return [own, swap(own, CORE), swap(own, CHIP)]


def finish(parts, *others):
    across = after(parts[2], *others) if others else parts[2]
    return [*parts[:2], across, swap(across, CORE)]


def scatter_direct(parts):
    return [parts[0]] + [swap(parts[j], j) for j in range(1, len(parts))]


def thirds(value):
    high = value.astype(LOW)
    rest = value - high.astype(F32)
    mid = rest.astype(LOW)
    return high, mid, (rest - mid.astype(F32)).astype(LOW)


def place(base, lane, first, pieces):
    for offset, piece in enumerate(pieces):
        base = jnp.where(lane == first + offset, piece, base)
    return base


def norm(values):
    mean = jnp.mean(values, axis=-1, keepdims=True)
    centred = values - mean
    spread = jnp.mean(centred * centred, axis=-1, keepdims=True)
    scaler = lax.rsqrt(spread + 1e-05)
    return centred * scaler, scaler


def norm_back(grad, unit, scaler, gain):
    scaled = grad * gain
    return scaler * (
        scaled
        - jnp.mean(scaled, axis=-1, keepdims=True)
        - unit * jnp.mean(scaled * unit, axis=-1, keepdims=True)
    )


def present(value, count):
    if count == value.shape[0]:
        return value
    row = lax.broadcasted_iota(jnp.int32, value.shape, 0)
    return jnp.where(row < count, value.astype(F32), 0.0).astype(value.dtype)


def pick(step, refs, rows, count):
    size = refs[0].shape[0]
    slots = rows.shape[0] // size
    for turn in range(len(refs) // slots):

        @pl.when(step == turn)
        def _():
            for at in range(slots):
                block = present(refs[turn * slots + at][...], count)
                rows[at * size : (at + 1) * size] = block


def stack_kernel(*refs):
    vec_ref, bias_ref = refs[-2:]
    for index, ref in enumerate(refs[:7]):
        vec_ref[index : index + 1] = ref[...].astype(F32).reshape(1, -1)
    bias_ref[...] = jnp.zeros_like(bias_ref)
    for index, ref in ((0, refs[7]), (2, refs[8])):
        bias_ref[index : index + 1] = ref[...].astype(F32).reshape(1, -1)


def project_kernel(share, slots, aliased, *refs):
    x_refs = refs[:slots]
    vec_ref, bias_ref, wq_ref, wk_ref, wv_ref = refs[slots : slots + 5]
    n_ref, q_ref, k_ref, v_ref, rows, w_tiles, b_tiles = refs[slots + 5 + aliased :]
    half = pl.program_id(0)
    heads = q_ref.shape[0]
    size = x_refs[0].shape[0]

    @pl.when(half == 0)
    def _():
        w_tiles[...] = jnp.zeros_like(w_tiles)
        b_tiles[...] = jnp.zeros_like(b_tiles)
        spot = lax.broadcasted_iota(jnp.int32, (1, LANES), 1) - HEAD_DIM
        ones = (
            jnp.where(spot == 0, HEAD_DIM**0.5, 0.0),
            jnp.where((spot >= 1) & (spot <= 3), 1.0, 0.0),
            jnp.where((spot >= 0) & (spot <= 2), 1.0, 0.0),
        )
        for which, w_ref in enumerate((wq_ref, wk_ref, wv_ref)):
            for head in range(heads):
                at = (which * heads + head) * LANES
                own = slice(head * HEAD_DIM, (head + 1) * HEAD_DIM)
                w_tiles[at : at + HEAD_DIM] = w_ref[own]
                b_tiles[:, at : at + LANES] = ones[which]
                b_tiles[:, at : at + HEAD_DIM] = bias_ref[which : which + 1, own]

    row = lax.broadcasted_iota(jnp.int32, (size, rows.shape[1]), 0) + half * size
    for at in range(slots):
        block = jnp.where(row < share, x_refs[at][...].astype(F32), 0.0)
        rows[at * size : (at + 1) * size] = block
    unit, _ = norm(rows[...])
    normed = (unit * vec_ref[0:1] + vec_ref[1:2]).astype(LOW)
    n_ref[...] = normed
    out = lax.dot_general(normed, w_tiles[...], NT, preferred_element_type=F32) + b_tiles[...]
    row = lax.broadcasted_iota(jnp.int32, (out.shape[0], LANES), 0)
    lane = lax.broadcasted_iota(jnp.int32, (out.shape[0], LANES), 1)
    absent = (lax.rem(row, size) + half * size >= share) & (lane == HEAD_DIM)
    scale = HEAD_DIM ** (-0.5)
    for head in range(heads):
        part = lambda which: out[:, (which * heads + head) * LANES :][:, :LANES]
        q_ref[head] = (part(0).astype(LOW).astype(F32) * scale).astype(LOW)
        k_ref[head] = jnp.where(absent, MASK, part(1)).astype(LOW)
        v_ref[head] = part(2).astype(LOW)


def attend_kernel(aliased, slots, q_ref, k_ref, v_ref, *refs):
    o_ref, full_ref, q_out = refs[aliased:]
    heads, block, _ = q_ref.shape
    quarter = block // slots // 2
    lane = lax.broadcasted_iota(jnp.int32, (block, LANES), 1)
    for head in range(heads):
        query = q_ref[head]
        scores = lax.dot_general(query, k_ref[head], NT, preferred_element_type=F32)
        top = jnp.max(scores, axis=-1, keepdims=True)
        weights = jnp.exp(scores - top).astype(LOW)
        out = jnp.dot(weights, v_ref[head], preferred_element_type=F32)
        total = out[:, HEAD_DIM : HEAD_DIM + 1]
        out = out / total
        full_ref[:, head * LANES : (head + 1) * LANES] = out
        low = out[:, :HEAD_DIM].astype(LOW)
        for part in range(2 * slots):
            at = ((part % 2) * heads + head) * HEAD_DIM
            o_ref[part // 2 * quarter : (part // 2 + 1) * quarter, at : at + HEAD_DIM] = low[
                part * quarter : (part + 1) * quarter
            ]
        logsum = top + jnp.log(total)
        q_out[head] = place(query, lane, HEAD_DIM + 1, thirds(-logsum))


def feed_kernel(half, share, group, order_pair, *refs):
    x_refs, m_refs, wo_refs = refs[:group], refs[group : 3 * group], refs[3 * group : 4 * group]
    g_refs = refs[4 * group : 5 * group]
    vec_ref, w1_ref, w2_ref = refs[5 * group : 5 * group + 3]
    at = 5 * group + 3
    old = refs[at : at + 3 * half]
    if half:
        me_ref = refs[at + 3]
        at += 4 + group
    h_ref, db_ref = refs[at : at + 2]
    d_refs = refs[at + 2 : at + 2 + group]
    mlp_refs = refs[at + 2 + group : at + 2 + 2 * group]
    outs = refs[at + 2 + 2 * group : -6]
    rows, mixed, c_ref, wo_all, fc2_sum, fc1_sum = refs[-6:]
    step = pl.program_id(0)
    size = x_refs[0].shape[0]
    slots = rows.shape[0] // size
    quarter = size // 2
    local = wo_refs[0].shape[0]
    count = min(size, share - half * size)
    pick(step, x_refs, rows, count)
    pick(step, g_refs, c_ref, size)
    local = wo_refs[0].shape[0]
    for source in range(group):
        for at in range(slots):
            packed = m_refs[source * slots + at][...]
            for part in range(2):
                first = at * size + part * quarter
                mixed[first : first + quarter, source * local : (source + 1) * local] = packed[
                    :, part * local : (part + 1) * local
                ]

    @pl.when(step == 0)
    def _():
        for source in range(group):
            wo_all[source * local : (source + 1) * local] = wo_refs[source][...]

    branch = jnp.dot(mixed[...], wo_all[...], preferred_element_type=F32)
    hidden = rows[...].astype(F32) + branch + vec_ref[2:3]

    @pl.when(step == 0)
    def _():
        h_ref[...] = hidden[:size]
        for total, value in zip((db_ref, fc2_sum, fc1_sum), old or [None] * 3):
            total[...] = jnp.zeros_like(total) if value is None else value[...]

    unit, _ = norm(hidden)
    normed = (unit * vec_ref[3:4] + vec_ref[4:5]).astype(LOW)
    pre = jnp.dot(normed, w1_ref[...], preferred_element_type=F32) + vec_ref[5:6]
    active_grad = lax.dot_general(c_ref[...], w2_ref[...], NT, preferred_element_type=F32)
    size_of = jnp.abs(pre)
    bell = jnp.exp(-0.5 * pre * pre)
    t = 1.0 / (1.0 + (0.3275911 * 0.5**0.5) * size_of)
    poly = t * (
        0.127414796 + t * (-0.142248368 + t * (0.7107068705 + t * (-0.7265760135 + t * 0.5307027145)))
    )
    tail = poly * bell
    gate = jnp.where(pre >= 0, 1.0 - tail, tail)
    active = (pre * gate).astype(LOW)
    pre_grad = active_grad * (gate + pre * bell * 0.3989422804014327)
    db_ref[...] += jnp.sum(pre_grad, axis=0, keepdims=True)
    pre_low = pre_grad.astype(LOW)
    back = lax.dot_general(pre_low, w1_ref[...], NT, preferred_element_type=F32).astype(LOW)
    mlp = jnp.dot(active, w2_ref[...], preferred_element_type=F32).astype(LOW)
    for turn in range(group // slots):

        @pl.when(step == turn)
        def _():
            for at in range(slots):
                part = slice(at * size, (at + 1) * size)
                d_refs[turn * slots + at][...] = back[part]
                mlp_refs[turn * slots + at][0] = mlp[part]

    for total, left, right in ((fc2_sum, active, c_ref[...]), (fc1_sum, normed, pre_low)):
        total[...] += lax.dot_general(
            left, right, (((0,), (0,)), ((), ())), preferred_element_type=F32
        )

    @pl.when(step == pl.num_programs(0) - 1)
    def _():
        if not (half and order_pair):
            outs[0][...] = fc2_sum[...]
            outs[1][...] = fc1_sum[...]
            return
        for index, (total, order) in enumerate(zip((fc2_sum, fc1_sum), order_pair)):
            each = total.shape[0] // len(order)
            for spot, slot in enumerate(order):
                which, at = divmod(spot, len(order) // 2)
                start = jnp.bitwise_xor(me_ref[0], slot) * each
                piece = total[pl.ds(pl.multiple_of(start, each), each)].astype(LOW)
                outs[2 * index + which][at * each : (at + 1) * each] = piece


def middle_kernel(terms, h_ref, g_ref, vec_ref, *refs):
    out_ref, low_ref, sums_ref = refs[-3:]
    grad = sum(ref[...].astype(F32) for ref in refs[:terms])
    unit, scaler = norm(h_ref[...])
    cot = g_ref[...].astype(F32)
    hidden_grad = cot + norm_back(grad, unit, scaler, vec_ref[3:4])
    out_ref[...] = hidden_grad
    low_ref[...] = hidden_grad.astype(LOW)
    add = lambda value: jnp.sum(value, axis=0, keepdims=True)
    sums = jnp.concatenate([add(grad * unit), add(grad), add(hidden_grad), add(cot)], axis=0)
    sums_ref[...] = sum((ref[...] for ref in refs[terms:-3]), sums)


def attend_back_kernel(parts, head, heads, orders, *refs):
    h_refs = refs[:parts]
    full_ref, q_ref, k_ref, v_ref, wo_ref, n_ref, wq_ref, wk_ref, wv_ref = refs[parts : parts + 9]
    at = parts + 9
    last = head == heads - 1
    if head:
        old_ref = refs[at]
        at += 1
    if last:
        me_ref, vec_ref, sums_ref, db_ref = refs[at : at + 4]
        done_refs = refs[at + 4 : at + 3 + heads]
        at += 3 + heads
    grad_ref, small_ref = refs[at : at + 2]
    outs = refs[at + 2 : -7]
    rows, wo_tile, w_stack, kt_ref, dk_sum, dv_sum, dw_sum = refs[-7:]
    step = pl.program_id(0)
    _, block, _ = q_ref.shape
    own = [slice(which * HEAD_DIM, (which + 1) * HEAD_DIM) for which in range(4)]

    @pl.when(step == 0)
    def _():
        size = h_refs[0].shape[0]
        for part in range(parts):
            rows[part * size : (part + 1) * size] = h_refs[part][...]
        wo_tile[:HEAD_DIM] = wo_ref[...]
        wo_tile[HEAD_DIM:] = jnp.zeros_like(wo_tile[HEAD_DIM:])
        for which, w_ref in enumerate((wq_ref, wk_ref, wv_ref)):
            w_stack[own[which]] = w_ref[...]
        for total in (dk_sum, dv_sum, dw_sum):
            total[...] = jnp.zeros_like(total)
        kt_ref[...] = k_ref[0].astype(F32).T[:HEAD_DIM].astype(LOW)

    scale = HEAD_DIM ** (-0.5)
    lane = lax.broadcasted_iota(jnp.int32, (block, LANES), 1)
    here = pl.ds(pl.multiple_of(step * block, block), block)
    hidden_grad = rows[here]
    full = full_ref[...]
    out_grad = lax.dot_general(hidden_grad, wo_tile[...], NT, preferred_element_type=F32)
    out_grad = out_grad.astype(LOW)
    dw_sum[...] += lax.dot_general(
        full.astype(LOW), hidden_grad, (((0,), (0,)), ((), ())), preferred_element_type=F32
    )
    delta = jnp.sum(out_grad.astype(F32) * full, axis=-1, keepdims=True)
    out_grad = place(out_grad, lane, HEAD_DIM, thirds(-delta))
    query = q_ref[0]
    scores = lax.dot_general(k_ref[0], query, NT, preferred_element_type=F32)
    probs = jnp.exp(scores)
    prob_grad = lax.dot_general(v_ref[0], out_grad, NT, preferred_element_type=F32)
    score_grad = (probs * prob_grad).astype(LOW)
    dv_sum[...] += jnp.dot(probs.astype(LOW), out_grad, preferred_element_type=F32)
    dk_sum[...] += jnp.dot(score_grad, query, preferred_element_type=F32)
    turned = jnp.dot(kt_ref[...], score_grad, preferred_element_type=F32)
    grad_ref[here, own[0]] = (turned.T * scale).astype(LOW)

    @pl.when(step == pl.num_programs(0) - 1)
    def _():
        grad_ref[:, own[1]] = dk_sum[:, :HEAD_DIM].astype(LOW)
        grad_ref[:, own[2]] = dv_sum[:, :HEAD_DIM].astype(LOW)
        grads = grad_ref[...]
        weight_grad = lax.dot_general(
            grads, n_ref[...], (((0,), (0,)), ((), ())), preferred_element_type=F32
        )
        weights = w_stack[...].astype(F32)
        totals = jnp.sum(grads.astype(F32), axis=0, keepdims=True)
        gain = jnp.sum(weights * weight_grad, axis=0, keepdims=True)
        shift = jnp.dot(
            totals, weights, precision=lax.Precision.HIGHEST, preferred_element_type=F32
        )
        if head:
            gain += old_ref[0:1]
            shift += old_ref[1:2]
            small_ref[6:7] = old_ref[6:7]
        else:
            small_ref[...] = jnp.zeros_like(small_ref)
        local = heads * HEAD_DIM
        for which, first in ((0, 0), (2, local)):
            start = first + head * HEAD_DIM
            small_ref[6:7, start : start + HEAD_DIM] = totals[:, own[which]]
        small_ref[1:2] = shift
        if not last:
            small_ref[0:1] = gain
            outs[0][: 3 * HEAD_DIM] = weight_grad
            outs[0][3 * HEAD_DIM :] = dw_sum[:HEAD_DIM]
            return
        small_ref[0:1] = (gain - vec_ref[1:2] * shift) / vec_ref[0:1]
        small_ref[2:6] = sums_ref[...]
        small_ref[7:8] = db_ref[...]
        stacks = outs[-1]
        for which in range(4):
            for index, done in enumerate(done_refs):
                start = which * local + index * HEAD_DIM
                stacks[start : start + HEAD_DIM] = done[own[which]]
            start = which * local + head * HEAD_DIM
            value = weight_grad[own[which]] if which < 3 else dw_sum[:HEAD_DIM]
            stacks[start : start + HEAD_DIM] = value
        if orders is None:
            outs[0][...] = stacks[: 2 * local].astype(LOW)
            outs[1][...] = stacks[2 * local :].astype(LOW)
            return
        for stack, order in enumerate(orders):
            size = 2 * local // len(order)
            for spot, slot in enumerate(order):
                which, index = divmod(spot, len(order) // 2)
                start = stack * 2 * local + jnp.bitwise_xor(me_ref[0], slot) * size
                piece = stacks[pl.ds(pl.multiple_of(start, size), size)]
                outs[2 * stack + which][index * size : (index + 1) * size] = piece.astype(LOW)


def settle_kernel(orders, me_ref, *refs):
    outs = refs[2 * len(orders) :]
    sides = len(outs) // len(orders)
    for stack, order in enumerate(orders):
        halves = refs[2 * stack : 2 * stack + 2]
        size = 2 * halves[0].shape[0] // len(order)
        per = len(order) // sides
        for spot, slot in enumerate(order):
            which, at = divmod(spot, len(order) // 2)
            value = halves[which][at * size : (at + 1) * size].astype(F32)
            place_at = jnp.bitwise_xor(me_ref[0], slot)
            start = pl.multiple_of(lax.rem(place_at, per) * size, size)
            for side in range(sides):

                @pl.when(lax.div(place_at, per) == side)
                def _():
                    outs[sides * stack + side][pl.ds(start, size)] = value


def spread_kernel(heads, *refs):
    grads, weights, outs = refs[:heads], refs[heads : heads + 3], refs[heads + 3 : -1]
    w_stacks = refs[-1]
    step = pl.program_id(0)

    @pl.when(step == 0)
    def _():
        for head in range(heads):
            for which, w_ref in enumerate(weights):
                start = (head * 3 + which) * HEAD_DIM
                w_stacks[start : start + HEAD_DIM] = w_ref[
                    head * HEAD_DIM : (head + 1) * HEAD_DIM
                ]

    each = 3 * HEAD_DIM
    total = sum(
        jnp.dot(
            grads[head][...],
            w_stacks[head * each : (head + 1) * each],
            preferred_element_type=F32,
        )
        for head in range(heads)
    ).astype(LOW)
    size = outs[0].shape[0]
    slots = total.shape[0] // size
    for turn in range(len(outs) // slots):

        @pl.when(step == turn)
        def _():
            for at in range(slots):
                outs[turn * slots + at][...] = total[at * size : (at + 1) * size]


def last_kernel(aliased, x_ref, d0_ref, d1_ref, d2_ref, h_ref, vec_ref, *refs):
    out_ref = refs[aliased]
    grad = d0_ref[...].astype(F32) + d1_ref[...].astype(F32) + d2_ref[...].astype(F32)
    unit, scaler = norm(x_ref[...].astype(F32))
    out_ref[...] = (h_ref[...] + norm_back(grad, unit, scaler, vec_ref[0:1])).astype(LOW)


def output_kernel(ha_ref, hb_ref, vec_ref, *refs):
    out_ref = refs[-1]
    size = ha_ref.shape[0]
    share = out_ref.shape[0]
    for part, h_ref in enumerate((ha_ref, hb_ref)):
        mlp = sum(ref[part].astype(F32) for ref in refs[:-1])
        value = (h_ref[...] + mlp + vec_ref[6:7]).astype(LOW)
        count = min(size, share - part * size)
        out_ref[part * size : part * size + count] = value[:count]


def pair(value, axis, step):
    size = lax.axis_size(axis)
    return lax.ppermute(value, axis, [(i, i ^ step) for i in range(size)])


def sum_over(value, axis):
    size = lax.axis_size(axis)
    if size & (size - 1):
        return lax.psum(value, axis)
    step = 1
    while step < size:
        value = value + pair(value, axis, step)
        step *= 2
    return value


def exchange_order(bits):
    order = [0]
    for bit in reversed(bits):
        order = order + [slot | bit for slot in order]
    return order


def halve(parts, axis, bit):
    keep, send = parts
    return tuple(jnp.split(keep + pair(send, axis, bit), 2))


def on_device(
    features, cotangent, w_query, bias_query, w_key, w_value, bias_value, w_out, bias_out,
    norm1_gain, norm1_bias, norm2_gain, norm2_bias, w_fc1, bias_fc1, w_fc2, bias_fc2,
):
    _, share, width = features.shape
    local = w_query.shape[1]
    heads = local // HEAD_DIM
    hidden = w_fc1.shape[1]
    group = lax.axis_size("tensor")
    clips = lax.axis_size("dp")
    rows = -(-share // LANES) * LANES
    size = rows // 2
    frames = group * rows
    part_rows = group * size
    slots = 2
    block = slots * size
    steps = group // slots
    shape = jax.ShapeDtypeStruct
    halves = range(2)

    x_own, g_own = features[0], cotangent[0]
    x_all = gather(x_own)
    wo_all = gather(after(w_out, x_all[2]))
    g_own = [g_own[:size], jnp.pad(g_own[size:], ((0, rows - share), (0, 0)))]
    g_all = [gather(after(g_own[0], x_all[2]))]
    vectors, biases = pl.pallas_call(
        stack_kernel,
        out_shape=[shape((7, width), F32), shape((3, local), F32)],
        compiler_params=params(2),
        cost_estimate=cost(0, 12 * width * 8),
        name="stack",
    )(
        norm1_gain, norm1_bias, bias_out, norm2_gain, norm2_bias, bias_fc1, bias_fc2,
        bias_query, bias_value,
    )
    turned = [w_query.T, w_key.T, w_value.T]

    slot_spec = whole((size, width))
    turned_spec = whole((local, width))
    any_spec = pl.BlockSpec(memory_space=pl.ANY)
    at_half = lambda half, n: pl.BlockSpec((block, n), lambda i: (half * steps + i, 0))
    own_half = lambda half: pl.BlockSpec((size, width), lambda *_: (half, 0))
    head_half = lambda half: pl.BlockSpec((heads, block, LANES), lambda i: (0, half * steps + i, 0))
    head_shape = shape((heads, frames, LANES), LOW)

    made = []
    for turn in range(steps):
        if turn:
            x_all = finish(x_all, made[0])
        made = pl.pallas_call(
            functools.partial(project_kernel, share, slots, len(made)),
            grid=(2,),
            in_specs=[pl.BlockSpec((size, width), lambda i: (i, 0))] * slots
            + [whole(vectors.shape), whole(biases.shape)]
            + [turned_spec] * 3
            + [any_spec] * len(made),
            out_specs=[pl.BlockSpec((block, width), lambda i, turn=turn: (i * steps + turn, 0))]
            + [
                pl.BlockSpec((heads, block, LANES), lambda i, turn=turn: (0, i * steps + turn, 0))
            ]
            * 3,
            out_shape=[pltpu.HBM((frames, width), LOW)] + [head_shape] * 3,
            scratch_shapes=[
                pltpu.VMEM((block, width), F32),
                pltpu.VMEM((3 * heads * LANES, width), LOW),
                pltpu.VMEM((1, 3 * heads * LANES), F32),
            ],
            input_output_aliases={slots + 5 + i: i for i in range(len(made))},
            compiler_params=params(16, 1),
            cost_estimate=cost(2 * part_rows * width * 9 * LANES, 6_000_000),
            name="project",
        )(*x_all[turn * slots : (turn + 1) * slots], vectors, biases, *turned, *made)
    normed1, query, key, value = made

    head_whole = whole((heads, frames, LANES))
    made, packed = [], []
    for half in halves:
        made = pl.pallas_call(
            functools.partial(attend_kernel, len(made), slots),
            grid=(steps,),
            in_specs=[head_half(half), head_whole, head_whole] + [any_spec] * len(made),
            out_specs=[
                pl.BlockSpec((block // 2, 2 * local), lambda i: (i, 0)),
                at_half(half, heads * LANES), head_half(half),
            ],
            out_shape=[
                shape((part_rows // 2, 2 * local), LOW), pltpu.HBM((frames, heads * LANES), F32),
                head_shape,
            ],
            input_output_aliases={3 + i: 1 + i for i in range(len(made))},
            compiler_params=params(24, 1),
            cost_estimate=cost(
                2 * heads * frames * frames * 256, 5_000_000, heads * frames * frames // 2
            ),
            name="attend",
        )(query, key, value, *made)
        packed.append(gather(made[0]))
        made = made[1:]
        if half == 0:
            query = after(query, wo_all[2], g_all[0][2])
    mixed_full, query_back = made
    wo_all = finish(wo_all, mixed_full)
    g_all[0] = finish(g_all[0], mixed_full)
    packed[0] = finish(packed[0], mixed_full)
    g_all.append(gather(after(g_own[1], mixed_full)))

    me = lax.axis_index("dp").astype(jnp.int32).reshape(1)
    me_spec = pl.BlockSpec(memory_space=pltpu.SMEM)
    bits = ((1, 2, 4), (2, 1, 4)) if clips == 8 else None
    orders = [exchange_order(order) for order in bits] if bits else None
    sum_shapes = [shape((hidden, width), F32), shape((width, hidden), F32)]
    hidden1, normed2_parts, carried, mlp = [], [], [], []
    for half in halves:
        if half:
            packed[half] = finish(packed[half], hidden1[0])
            g_all[half] = finish(g_all[half], hidden1[0])
        sources = packed[half]
        packed_specs, packed_args = [], []
        for source in range(group):
            for at in range(slots):
                packed_args.append(sources[source])
                packed_specs.append(
                    pl.BlockSpec(
                        (size // 2, 2 * local),
                        lambda i, source=source, at=at: ((i * slots + at) ^ source, 0),
                    )
                )
        if half and bits:
            ends = [shape((total.shape[0] // 2, total.shape[1]), LOW) for total in sum_shapes]
            ends = [ends[0], ends[0], ends[1], ends[1]]
        else:
            ends = sum_shapes
        first_mlp = 5 * group + 7
        made = pl.pallas_call(
            functools.partial(feed_kernel, half, share, group, orders),
            grid=(steps,),
            in_specs=[own_half(half)] * group
            + packed_specs
            + [whole((local, width))] * group
            + [slot_spec] * group
            + [whole(vectors.shape), whole((width, hidden)), whole((hidden, width))]
            + [whole(part.shape) for part in carried]
            + ([me_spec] + [any_spec] * group if half else []),
            out_specs=[slot_spec, whole((1, hidden))]
            + [slot_spec] * group
            + [pl.BlockSpec((1, size, width), lambda i, half=half: (half, 0, 0))] * group
            + [whole(part.shape) for part in ends],
            out_shape=[shape((size, width), F32), shape((1, hidden), F32)]
            + [shape((size, width), LOW)] * group
            + [shape((2, size, width), LOW)] * group
            + ends,
            scratch_shapes=[pltpu.VMEM((block, width), LOW)] * 3
            + [pltpu.VMEM((width, width), LOW)]
            + [pltpu.VMEM(total.shape, F32) for total in sum_shapes],
            input_output_aliases={first_mlp + i: 2 + group + i for i in range(len(mlp))},
            compiler_params=params(46, 1),
            cost_estimate=cost(7 * frames * width * hidden, 12_000_000, frames * hidden // 2),
            name="feed",
        )(
            *x_all, *packed_args, *wo_all, *g_all[half], vectors, w_fc1, w_fc2, *carried,
            *([me, *mlp] if half else []),
        )
        hidden1.append(made[0])
        normed2_parts.append(made[2 : 2 + group])
        mlp = made[2 + group : 2 + 2 * group]
        fc = made[2 + 2 * group :]
        carried = [made[1], *fc]
    fc1_bias_grad = [made[1]]

    hidden1_grad, sums2, hidden1_rows = [], [], []
    all_terms = [scatter_direct(normed2_parts[0])]
    all_terms[0][0] = after(all_terms[0][0], normed2_parts[1][0])
    for half in halves:
        if half:
            own, beside, far, corner = normed2_parts[1]
            far = far + swap(after(corner, low), CORE)
            all_terms.append([own, swap(beside, CORE), swap(far, CHIP)])
            hidden1_rows = [gather(after(low, far))]
            all_terms[1][0] = after(own, hidden1_rows[0][2])
        terms = all_terms[half]
        grad, low, sums = pl.pallas_call(
            functools.partial(middle_kernel, len(terms)),
            grid=(1,),
            in_specs=[slot_spec, slot_spec, whole(vectors.shape)]
            + [slot_spec] * len(terms)
            + [whole((4, width))] * half,
            out_specs=[slot_spec, slot_spec, whole((4, width))],
            out_shape=[
                shape((size, width), F32), shape((size, width), LOW), shape((4, width), F32),
            ],
            compiler_params=params(8, 1),
            cost_estimate=cost(20 * size * width, 16 * size * width),
            name="middle",
        )(hidden1[half], g_own[half], vectors, *terms, *sums2)
        hidden1_grad.append(grad)
        sums2 = [sums]
    hidden1_rows.append(gather(low))

    if bits:
        fc = [halve(fc[2 * index : 2 * index + 2], "dp", bits[index][0]) for index in range(2)]
        fc = [halve(fc[index], "dp", bits[index][1]) for index in range(2)]
        fc = jnp.concatenate([piece for both in fc for piece in both])
        fc_across = pair(fc, "dp", bits[0][2])
        hidden1_rows[0][0] = after(hidden1_rows[0][0], fc)
    else:
        fc2_grad, fc1_grad = [
            total.astype(F32) for total in lax.psum(tuple(part.astype(LOW) for part in fc), "dp")
        ]
    mlp_far = mlp[2] + swap(mlp[3], CORE)
    mlp = [mlp[0], mlp[1], mlp_far]
    hidden1_rows[0] = finish(hidden1_rows[0])
    hidden1_rows[1] = finish(hidden1_rows[1])
    hidden1_rows[0][0] = after(hidden1_rows[0][0], *mlp)

    back = 512
    each = 3 * HEAD_DIM
    stack_rows = [local] * 4 if bits else [2 * local] * 2
    all_rows = hidden1_rows[0] + hidden1_rows[1]
    head_row = lambda head: pl.BlockSpec((HEAD_DIM, width), lambda i: (head, 0))
    head_tile = lambda head: pl.BlockSpec((1, frames, LANES), lambda i: (head, 0, 0))
    small_shape, done_shape = shape((8, width), F32), shape((4 * HEAD_DIM, width), F32)
    grads, dones, small = [], [], []
    for head in range(heads):
        last = head == heads - 1
        if head == 1:
            mlp = scatter_direct([after(part, grads[0]) for part in mlp])
        if last:
            all_rows[0] = after(all_rows[0], *mlp[1:])
        specs = [slot_spec] * len(all_rows) + [
            pl.BlockSpec((back, LANES), lambda i, head=head: (i, head)),
            pl.BlockSpec((1, back, LANES), lambda i, head=head: (head, i, 0)),
            head_tile(head), head_tile(head), head_row(head), whole((frames, width)),
            *[head_row(head)] * 3,
        ]
        args = [*all_rows, mixed_full, query_back, key, value, w_out, normed1, *turned]
        if head:
            specs += [whole((8, width))]
            args += small
        out_shape = [shape((frames, each), LOW), small_shape]
        scratch = [
            pltpu.VMEM((frames, width), LOW), pltpu.VMEM((LANES, width), LOW),
            pltpu.VMEM((each, width), LOW), pltpu.VMEM((HEAD_DIM, frames), LOW),
            pltpu.VMEM((frames, LANES), F32), pltpu.VMEM((frames, LANES), F32),
            pltpu.VMEM((LANES, width), F32),
        ]
        if last:
            specs += [me_spec, whole(vectors.shape), whole((4, width)), whole((1, hidden))]
            specs += [whole(done_shape.shape)] * len(dones)
            args += [me, vectors, *sums2, *fc1_bias_grad, *dones]
            out_shape += [shape((n, width), LOW) for n in stack_rows]
            scratch.insert(0, pltpu.VMEM((4 * local, width), F32))
        else:
            out_shape += [done_shape]
        grad, total, *rest = pl.pallas_call(
            functools.partial(attend_back_kernel, len(all_rows), head, heads, orders),
            grid=(frames // back,),
            in_specs=specs,
            out_specs=[whole(out.shape) for out in out_shape],
            out_shape=out_shape,
            scratch_shapes=scratch,
            compiler_params=params(36, 1),
            cost_estimate=cost(10 * frames * frames * 256, 8_000_000, frames * frames),
            name="attend_back",
        )(*args)
        grads.append(grad)
        small = [total]
        if last:
            stacks = rest
        else:
            dones += rest
            all_rows[1] = after(all_rows[1], total)
    small = small[0]
    if bits:
        fc_across = after(fc_across, grads[-1])
        grads[0] = after(grads[0], fc_across)
    block_rows = lambda n: pl.BlockSpec((block, n), lambda i: (i, 0))
    normed1_parts = pl.pallas_call(
        functools.partial(spread_kernel, heads),
        grid=(2 * steps,),
        in_specs=[block_rows(each)] * heads + [turned_spec] * 3,
        out_specs=[slot_spec] * (2 * group),
        out_shape=[shape((size, width), LOW)] * (2 * group),
        scratch_shapes=[pltpu.VMEM((heads * each, width), LOW)],
        compiler_params=params(16, 1),
        cost_estimate=cost(2 * frames * width * 3 * local, 6_000_000),
        name="spread",
    )(*grads, *turned)
    parts = [normed1_parts[half * group : (half + 1) * group] for half in halves]

    def settle(ends, order, count, size):
        return pl.pallas_call(
            functools.partial(settle_kernel, order),
            in_specs=[me_spec] + [pl.BlockSpec(memory_space=pltpu.VMEM)] * len(ends),
            out_shape=[shape((size, width), F32)] * count,
            compiler_params=params(12),
            cost_estimate=cost(0, 6 * count * size * width),
            name="settle",
        )(me, *ends)

    hop = lambda value, bit: pair(value, "dp", bit)
    side = lambda index, turn: bits[index][turn]
    join = lambda *values: jnp.concatenate(values)
    together = lambda *values: lax.optimization_barrier(values)
    if bits:
        def add_across(own, other):
            quarters = jnp.split(other, 4)
            return own + join(quarters[1], quarters[0], quarters[3], quarters[2])

        q = [(stacks[0], stacks[1]), (stacks[2], stacks[3])]
        fc = jnp.split(add_across(fc, fc_across), 2)
        f_next = [hop(fc[0], side(0, 1)), hop(fc[1], side(1, 1))]
        got = together(
            hop(q[0][1], side(0, 0)), hop(q[1][1], side(1, 0)), hop(small, 1), parts[0][0]
        )
        q = [tuple(jnp.split(q[i][0] + got[i], 2)) for i in range(2)]
        small = small + got[2]
        parts = [[after(part, got[0]) for part in own] for own in parts]
        beside = [swap(part[1], CORE) for part in parts]
        far = [swap(part[2] + swap(part[3], CORE), CHIP) for part in parts]
        got = together(hop(q[0][1], side(0, 1)), hop(q[1][1], side(1, 1)), *f_next)
        fc = [join(fc[i], got[2 + i]) for i in range(2)]
        f_last = [hop(fc[0], side(0, 0)), hop(fc[1], side(1, 0))]
        rest = join(*[q[i][0] + got[i] for i in range(2)])
        small = after(small, rest)
        q = jnp.split(add_across(rest, hop(rest, side(0, 2))), 2)
        got = together(hop(q[0], side(0, 1)), hop(q[1], side(1, 1)))
        q = [join(q[i], got[i]) for i in range(2)]
        got = together(hop(q[0], side(0, 0)), hop(q[1], side(1, 0)), *f_last)
        ends, f_last = [q[0], got[0], q[1], got[1]], got[2:]
        small = small + hop(small, 2)
        small = small + hop(small, 4)
        shared = small + swap(small, CORE)
        shared = shared + swap(shared, CHIP)
        (fc2_grad,) = settle([fc[0], f_last[0]], orders[:1], 1, hidden)
        (fc1_grad,) = settle([fc[1], f_last[1]], orders[1:], 1, hidden)
        ends[1] = after(ends[1], fc2_grad, fc1_grad)
        grads = settle(ends, orders, 4, local)
    else:
        grads = jnp.concatenate(lax.psum(tuple(stacks), "dp")).astype(F32)
        grads = jnp.split(grads, 4)
        small = sum_over(small, "dp")
        shared = sum_over(small, "tensor")
        beside = [swap(part[1], CORE) for part in parts]
        far = [swap(part[2] + swap(part[3], CORE), CHIP) for part in parts]

    layer_out = pl.pallas_call(
        output_kernel,
        out_shape=shape((share, width), LOW),
        compiler_params=params(12),
        cost_estimate=cost(8 * rows * width, 12 * rows * width),
        name="output",
    )(*hidden1, vectors, *mlp)

    features_grad = []
    for half in halves:
        features_grad = [
            pl.pallas_call(
                functools.partial(last_kernel, len(features_grad)),
                grid=(1,),
                in_specs=[own_half(half)]
                + [slot_spec] * 4
                + [whole(vectors.shape)]
                + [any_spec] * len(features_grad),
                out_specs=own_half(half),
                out_shape=shape((share, width), LOW),
                input_output_aliases={6: 0} if features_grad else {},
                compiler_params=params(8, 1),
                cost_estimate=cost(20 * size * width, 14 * size * width),
                name="last",
            )(
                x_own,
                parts[half][0],
                beside[half],
                far[half],
                hidden1_grad[half],
                vectors,
                *features_grad,
            )
        ]
    return (
        layer_out[None],
        features_grad[0][None],
        grads[0].T,
        small[6, :local],
        grads[1].T,
        grads[2].T,
        small[6, local : 2 * local],
        grads[3],
        shared[4],
        shared[0],
        shared[1],
        shared[2],
        shared[3],
        fc1_grad,
        small[7],
        fc2_grad,
        shared[5],
    )


def solution(mesh):
    rows = P("dp", "tensor", None)
    columns, lines, vector, same = P(None, "tensor"), P("tensor", None), P("tensor"), P()
    in_specs = (
        rows, rows, columns, vector, columns, columns, vector, lines, same,
        same, same, same, same, columns, vector, lines, same,
    )
    out_specs = (
        rows, rows, columns, vector, columns, columns, vector, lines, same,
        same, same, same, same, columns, vector, lines, same,
    )
    return jax.shard_map(
        on_device, mesh=mesh, in_specs=in_specs, out_specs=out_specs, check_vma=False
    )
```
